32 devices in a mesh: head: 4 (over x, core), blk: 8 (over z, y).
Axes of the slice: x: 2, y: 2, z: 4, core: 2. Of those that a mesh axis runs over, the one named last changes fastest.
Arguments:
- tokens: bfloat16 [4, 8, 256, 1024], P(None, 'blk', 'head'), may hold values from -6 to 6
- cotangent: bfloat16 [4, 8, 256, 1024], P(None, 'blk', 'head'), may hold values from -6 to 6
- block_table: int32 [8, 2], replicated, may hold values from 0 to 15, as said below
- norm1_gain: bfloat16 [1024], P(('head', 'blk')), may hold values from 0.5 to 1.5
- norm1_bias: bfloat16 [1024], P(('head', 'blk')), may hold values from -1.5 to 1.5
- w_query: bfloat16 [1024, 1024], P(('head', 'blk')), may hold values from -0.1875 to 0.1875
- w_key: bfloat16 [1024, 1024], P(('head', 'blk')), may hold values from -0.1875 to 0.1875
- w_value: bfloat16 [1024, 1024], P(('head', 'blk')), may hold values from -0.1875 to 0.1875
- w_output: bfloat16 [1024, 1024], P(('head', 'blk')), may hold values from -0.5 to 0.5
- norm2_gain: bfloat16 [1024], P(('head', 'blk')), may hold values from 0.5 to 1.5
- norm2_bias: bfloat16 [1024], P(('head', 'blk')), may hold values from -1.5 to 1.5
- w_up: bfloat16 [1024, 4096], P(('head', 'blk')), may hold values from -0.1875 to 0.1875
- b_up: bfloat16 [4096], P(('head', 'blk')), may hold values from -2.5 to 2.5
- w_down: bfloat16 [4096, 1024], P(('head', 'blk')), may hold values from -0.09375 to 0.09375
- b_down: bfloat16 [1024], P(('head', 'blk')), may hold values from -1.5 to 1.5
Outputs:
- activations: bfloat16 [4, 8, 256, 1024], P(None, 'blk', 'head')
- input_grad: bfloat16 [4, 8, 256, 1024], P(None, 'blk', 'head')
- grad_norm1_gain: float32 [1024], P(('head', 'blk'))
- grad_norm1_bias: float32 [1024], P(('head', 'blk'))
- grad_w_query: float32 [1024, 1024], P(('head', 'blk'))
- grad_w_key: float32 [1024, 1024], P(('head', 'blk'))
- grad_w_value: float32 [1024, 1024], P(('head', 'blk'))
- grad_w_output: float32 [1024, 1024], P(('head', 'blk'))
- grad_norm2_gain: float32 [1024], P(('head', 'blk'))
- grad_norm2_bias: float32 [1024], P(('head', 'blk'))
- grad_w_up: float32 [1024, 4096], P(('head', 'blk'))
- grad_b_up: float32 [4096], P(('head', 'blk'))
- grad_w_down: float32 [4096, 1024], P(('head', 'blk'))
- grad_b_down: float32 [1024], P(('head', 'blk'))
The draws below stay inside these ranges and needn't reach their ends.
Inputs may be any that keep to these rules, and one draw needn't show every extreme that they name: `block_table`: row b names two blocks of 128 positions, j and 15 - j for some j, in either order; every block of the sequence stands once in the table.
All inputs are finite; a program needn't handle non-finite values.
Results may differ from the reference program's by a relative error of at most 0.015.
Values may be sent and summed in bfloat16 or wider, within the bound.
No kernel may reach another device: no remote copies, remote signals or barrier semaphores. Data moves between devices by JAX's collectives and lax.ppermute only.
A program may use at most 320 MiB of HBM per device.

```python
import math
import jax
import jax.numpy as jnp
from jax import lax

D = 1024
HEADS = 8
HEAD_DIM = 128
FF = 4096
SEQS = 4
BIAS_SPAN = 1024
RT = 256
NR = 8
HALF = 128


def draw_block_table(key, part):
    order = jax.random.permutation(jax.random.fold_in(key, 11), NR).astype(jnp.int32)
    flipped = jax.random.randint(jax.random.fold_in(key, 12), (NR,), 0, 2)
    mirror = 2 * NR - 1 - order
    first_block = jnp.where(flipped == 1, mirror, order)
    second_block = jnp.where(flipped == 1, order, mirror)
    return jnp.stack([first_block, second_block], axis=1).astype(jnp.int32)


def block_scale(key, shape, pieces, least, top_value):
    level, own = 1.0, jax.random.fold_in(key, 6)
    for axis_at, blocks in pieces:
        steps = jnp.exp(jax.random.uniform(jax.random.fold_in(own, axis_at), (blocks,), jnp.float32, least / len(pieces), top_value / len(pieces)))
        level = level * jnp.repeat(steps, shape[axis_at] // blocks).reshape([-1 if axis == axis_at else 1 for axis in range(len(shape))])
    return level


def scatter_about(stream_key, shape, deviation, most, split=(), kind=jnp.bfloat16):
    factor_of = block_scale(stream_key, shape, split, -0.22, 0.18) if split else 1.0
    entries = jax.random.normal(stream_key, shape, jnp.float32) * deviation * factor_of
    return jnp.minimum(jnp.maximum(entries, -most), most).astype(kind)


def setup_inputs(seed: int = 0) -> dict:
    arg_keys = jax.random.split(jax.random.key(seed), 16)
    return {
        "tokens": scatter_about(arg_keys[0], (SEQS, NR, RT, D), 1.0, 6.0, ((1, 8), (2, 4))),
        "cotangent": scatter_about(arg_keys[1], (SEQS, NR, RT, D), 1.0, 6.0, ((1, 8), (2, 4))),
        "block_table": draw_block_table(jax.random.fold_in(arg_keys[15], 71), 0),
        "norm1_gain": jnp.clip(1.0 + 0.1 * jax.random.normal(arg_keys[3], (D,), jnp.float32), 0.5, 1.5).astype(jnp.bfloat16),
        "norm1_bias": scatter_about(arg_keys[4], (D,), 0.3, 1.5, ((0, 32),)),
        "w_query": scatter_about(arg_keys[5], (D, D), D ** -0.5, 0.1875, ((0, 32),)),
        "w_key": scatter_about(arg_keys[6], (D, D), D ** -0.5, 0.1875, ((0, 32),)),
        "w_value": scatter_about(arg_keys[7], (D, D), D ** -0.5, 0.1875, ((0, 32),)),
        "w_output": scatter_about(arg_keys[8], (D, D), (D // 8) ** -0.5, 0.5, ((0, 32),)),
        "norm2_gain": jnp.clip(1.0 + 0.1 * jax.random.normal(arg_keys[9], (D,), jnp.float32), 0.5, 1.5).astype(jnp.bfloat16),
        "norm2_bias": scatter_about(arg_keys[10], (D,), 0.3, 1.5, ((0, 32),)),
        "w_up": scatter_about(arg_keys[11], (D, FF), D ** -0.5, 0.1875, ((0, 32),)),
        "b_up": scatter_about(arg_keys[12], (FF,), 0.5, 2.5, ((0, 32),)),
        "w_down": scatter_about(arg_keys[13], (FF, D), FF ** -0.5, 0.09375, ((0, 32),)),
        "b_down": scatter_about(arg_keys[14], (D,), 0.3, 1.5, ((0, 32),)),
    }


@jax.custom_vjp
def low(v):
    return lax.optimization_barrier(v.astype(jnp.bfloat16)).astype(jnp.float32)

@jax.custom_vjp
def low_back(v):
    return v

def low_keep(v):
    return (low(v), None)

def low_pass(kept, grad):
    return (grad,)

def back_keep(v):
    return (v, None)

def back_low(kept, grad):
    return (low(grad),)
low.defvjp(low_keep, low_pass)
low_back.defvjp(back_keep, back_low)

def layer_norm(values, gain, shift):
    center = values - lax.optimization_barrier(jnp.mean(values, axis=-1, keepdims=True))
    spread = lax.rsqrt(lax.optimization_barrier(jnp.mean(center * center, axis=-1, keepdims=True)) + 1e-05)
    return center * spread * gain + shift

def reference(tokens, cotangent, block_table, norm1_gain, norm1_bias, w_query, w_key, w_value, w_output, norm2_gain, norm2_bias, w_up, b_up, w_down, b_down):
    highest = lax.Precision.HIGHEST
    seq_len = NR * RT
    params = tuple((weight.astype(jnp.float32) for weight in (norm1_gain, norm1_bias, w_query, w_key, w_value, w_output, norm2_gain, norm2_bias, w_up, b_up, w_down, b_down)))
    inputs = tokens.astype(jnp.float32).reshape(SEQS, seq_len, D)
    upstream = cotangent.astype(jnp.float32).reshape(SEQS, seq_len, D)
    layout_rows = jnp.arange(seq_len, dtype=jnp.int32)
    flat_table = block_table.reshape(-1).astype(jnp.int32)
    positions = flat_table[layout_rows // HALF] * HALF + layout_rows % HALF
    slopes = jnp.exp2(-8.0 * (jnp.arange(HEADS, dtype=jnp.float32) + 1.0) / HEADS) * (BIAS_SPAN / seq_len)
    query_block = math.gcd(seq_len, 512)
    score_scale = 1.0 / math.sqrt(HEAD_DIM)

    def attend_block(queries, key_heads, values, offset):
        block_queries = lax.dynamic_slice_in_dim(queries, offset, query_block, 0)
        block_pos = lax.dynamic_slice_in_dim(positions, offset, query_block, 0)
        distance = (block_pos[:, None] - positions[None, :]).astype(jnp.float32)
        scores = jnp.einsum('qhd,khd->hqk', block_queries, key_heads, precision=highest) * score_scale
        scores = scores - slopes[:, None, None] * distance[None]
        scores = low_back(scores)
        allowed = (positions[None, :] <= block_pos[:, None])[None]
        scores = jnp.where(allowed, scores, -1e+30)
        shifted = jnp.where(allowed, jnp.exp(scores - lax.optimization_barrier(jnp.max(scores, axis=-1, keepdims=True))), 0.0)
        attention = shifted / lax.optimization_barrier(jnp.sum(shifted, axis=-1, keepdims=True))
        return jnp.einsum('hqk,khd->qhd', low(attention), values, precision=highest)

    def one_sequence(sequence_rows, weights):
        first_gain, first_shift, query_weight, key_weight, value_weight, output_weight, second_gain, second_shift, up_weight, up_bias, down_weight, down_bias = weights
        normed = low(layer_norm(sequence_rows, first_gain, first_shift))

        def project(weight):
            return low_back(low(jnp.dot(normed, weight, precision=highest))).reshape(seq_len, HEADS, HEAD_DIM)
        queries = project(query_weight)
        key_heads = project(key_weight)
        values = project(value_weight)
        offsets = jnp.arange(seq_len // query_block, dtype=jnp.int32) * query_block
        blocks = lax.map(jax.checkpoint(lambda offset: attend_block(queries, key_heads, values, offset)), offsets)
        attended = low_back(low(blocks.reshape(seq_len, D)))
        middle = sequence_rows + low_back(jnp.dot(attended, output_weight, precision=highest))
        normed_two = low(layer_norm(middle, second_gain, second_shift))
        hidden = low_back(jnp.dot(normed_two, up_weight, precision=highest) + up_bias)
        activated = low(jax.nn.gelu(hidden, approximate=True))
        return middle + low_back(jnp.dot(activated, down_weight, precision=highest) + down_bias)

    def forward(sequences, weights):
        return lax.map(lambda sequence_rows: jax.checkpoint(one_sequence)(sequence_rows, weights), sequences)
    result, pullback = jax.vjp(forward, inputs, params)
    grad_inputs, grad_params = pullback(upstream)
    grad_first_gain, grad_first_shift, grad_query, grad_key, grad_value, grad_output, grad_second_gain, grad_second_shift, grad_up, grad_up_bias, grad_down, grad_down_bias = grad_params
    return (result.astype(jnp.bfloat16).reshape(tokens.shape), grad_inputs.astype(jnp.bfloat16).reshape(tokens.shape), grad_first_gain, grad_first_shift, grad_query, grad_key, grad_value, grad_output, grad_second_gain, grad_second_shift, grad_up, grad_up_bias, grad_down, grad_down_bias)
```

```python
import functools
import math

import jax
import jax.numpy as jnp
from jax import lax
from jax.experimental import pallas as pl
from jax.experimental.pallas import tpu as pltpu
from jax.sharding import PartitionSpec as P

HEADS = 8
HEAD_DIM = 128
BIAS_SPAN = 1024
EPSILON = 1e-05
NEG_LARGE = -1e30
LOG2E = 1.4426950408889634
F32 = jnp.float32
BF16 = jnp.bfloat16


def shift(x, axis, inner, outer_step, inner_step):
    count = lax.axis_size(axis)
    outer = count // inner
    if outer_step % outer == 0 and inner_step % inner == 0:
        return x
    pairs = [
        (o * inner + i, ((o + outer_step) % outer) * inner + (i + inner_step) % inner)
        for o in range(outer)
        for i in range(inner)
    ]
    return lax.ppermute(x, axis, pairs)


def place_of(axis, inner):
    me = lax.axis_index(axis)
    return me // inner, me % inner


def gather_pieces(x, axis, inner):
    outer = lax.axis_size(axis) // inner
    pieces = []
    for a in range(outer):
        far = shift(x, axis, inner, a, 0)
        for c in range(inner):
            pieces.append((a, c, shift(far, axis, inner, 0, c)))
    return pieces


def gather_relative(x, axis, inner):
    return jnp.concatenate([p for _, _, p in gather_pieces(x, axis, inner)], axis=0)


def gather_absolute(x, axis, inner, slot_dim):
    outer = lax.axis_size(axis) // inner
    o, i = place_of(axis, inner)
    shape = x.shape[:slot_dim] + (outer * inner,) + x.shape[slot_dim:]
    whole = jnp.zeros(shape, x.dtype)
    for a, c, piece in gather_pieces(x, axis, inner):
        slot = ((o - a) % outer) * inner + (i - c) % inner
        at = [0] * len(shape)
        at[slot_dim] = slot
        whole = lax.dynamic_update_slice(whole, jnp.expand_dims(piece, slot_dim), tuple(at))
    return whole


def scatter_sum_relative(x, axis, inner):
    outer = lax.axis_size(axis) // inner
    x = x.reshape((outer, inner) + x.shape[1:])
    total = x[:, 0].astype(F32)
    for c in range(1, inner):
        total = total + shift(x[:, c], axis, inner, 0, -c).astype(F32)
    near = total.astype(BF16)
    result = total[0]
    for a in range(1, outer):
        result = result + shift(near[a], axis, inner, -a, 0).astype(F32)
    return result


def scatter_sum_absolute(x, axis, inner, slot_dim):
    outer = lax.axis_size(axis) // inner
    o, i = place_of(axis, inner)
    lead, rest = x.shape[:slot_dim], x.shape[slot_dim + 1 :]
    x = x.reshape(lead + (outer, inner) + rest)

    def column(c):
        return lax.dynamic_index_in_dim(x, (i - c) % inner, slot_dim + 1, keepdims=False)

    total = column(0).astype(F32)
    for c in range(1, inner):
        total = total + shift(column(c), axis, inner, 0, -c).astype(F32)
    near = total.astype(BF16)
    result = lax.dynamic_index_in_dim(total, o, slot_dim, keepdims=False)
    for a in range(1, outer):
        piece = lax.dynamic_index_in_dim(near, (o - a) % outer, slot_dim, keepdims=False)
        result = result + shift(piece, axis, inner, -a, 0).astype(F32)
    return result


def norm_parts(values):
    center = values - jnp.mean(values, axis=-1, keepdims=True)
    spread = lax.rsqrt(jnp.mean(center * center, axis=-1, keepdims=True) + EPSILON)
    return (center * spread, spread)


def norm_back(grad_normed, normed, spread, gain):
    scaled = grad_normed * gain
    inner = (
        scaled
        - jnp.mean(scaled, axis=-1, keepdims=True)
        - normed * jnp.mean(scaled * normed, axis=-1, keepdims=True)
    )
    return (spread * inner, jnp.sum(grad_normed * normed, axis=0), jnp.sum(grad_normed, axis=0))


def plain_dot(left, right):
    return jnp.dot(left, right, preferred_element_type=F32)


def rows_dot(left, right):
    return lax.dot_general(left, right, (((0,), (0,)), ((), ())), preferred_element_type=F32)


def dot_trans(left, right):
    return lax.dot_general(left, right, (((1,), (1,)), ((), ())), preferred_element_type=F32)


def gelu_and_slope(u):
    k = math.sqrt(2.0 / math.pi)
    t = jnp.tanh(k * (u + 0.044715 * (u * u * u)))
    half = 0.5 * (1.0 + t)
    slope = half + 0.5 * u * (1.0 - t * t) * (k * (1.0 + 3 * 0.044715 * (u * u)))
    return u * half, slope


def attend_forward_kernel(tile, piece, src_ref, slope_ref, recv_ref, out_ref, q_ref, k_ref, v_ref, o_ref, l_ref, vt_ref):
    pieces = q_ref.shape[0] // piece
    rel = recv_ref.shape[0] // piece // 3 // src_ref.shape[1]
    for t in range(pieces):
        for c, ref in enumerate((q_ref, k_ref, v_ref)):
            at = pl.multiple_of((src_ref[0, t] + c * src_ref[1, 0]) * piece, piece)
            ref[t * piece : (t + 1) * piece, :] = recv_ref[pl.ds(at, piece), :]
    tiles = q_ref.shape[0] // tile
    for j in range(tiles):
        rows = slice(j * tile, (j + 1) * tile)
        vt_ref[:, rows] = v_ref[rows, :].T
    slope = slope_ref[0]
    scale = LOG2E / math.sqrt(HEAD_DIM)
    for i in range(tiles):
        span = (i + 1) * tile
        scores = dot_trans(k_ref[0:span, :], q_ref[i * tile : span, :]) * scale
        key_at = lax.broadcasted_iota(jnp.int32, (span, tile), 0)
        scores = scores + slope * key_at.astype(F32)
        low = key_at[i * tile : span] - i * tile <= lax.broadcasted_iota(jnp.int32, (tile, tile), 1)
        last = jnp.where(low, scores[i * tile : span], NEG_LARGE)
        if i:
            scores = jnp.concatenate([scores[: i * tile], last], axis=0)
        else:
            scores = last
        top = jnp.max(scores, axis=0, keepdims=True)
        shifted = jnp.exp2(scores - top)
        total = jnp.sum(shifted, axis=0, keepdims=True)
        l_ref[i : i + 1, :] = top + jnp.log2(total)
        prob = (shifted * (1.0 / total)).astype(BF16)
        o_ref[i * tile : span, :] = plain_dot(vt_ref[:, 0:span], prob).T.astype(BF16)
    for t in range(pieces):
        at = pl.multiple_of(src_ref[2, t] * piece, piece)
        out_ref[pl.ds(at, piece), :] = o_ref[t * piece : (t + 1) * piece, :]


def attend_backward_kernel(tile, piece, src_ref, slope_ref, recv_ref, q_ref, k_ref, v_ref, o_ref, l_ref, out_ref, d_ref, kt_ref, dq_ref, dk_ref, dv_ref):
    pieces = q_ref.shape[0] // piece
    for t in range(pieces):
        at = pl.multiple_of(src_ref[2, t] * piece, piece)
        d_ref[t * piece : (t + 1) * piece, :] = recv_ref[pl.ds(at, piece), :]
    tiles = q_ref.shape[0] // tile
    for j in range(tiles):
        rows = slice(j * tile, (j + 1) * tile)
        kt_ref[:, rows] = k_ref[rows, :].T
    slope = slope_ref[0]
    scale = LOG2E / math.sqrt(HEAD_DIM)
    for i in reversed(range(tiles)):
        span = (i + 1) * tile
        mine = slice(i * tile, span)
        queries, grads = q_ref[mine, :], d_ref[mine, :]
        row_dot = lax.dot_general(
            jnp.ones((8, HEAD_DIM), F32),
            grads.astype(F32) * o_ref[mine, :].astype(F32),
            (((1,), (1,)), ((), ())),
            precision=lax.Precision.HIGHEST,
            preferred_element_type=F32,
        )[0:1]
        scores = dot_trans(k_ref[0:span, :], queries) * scale
        key_at = lax.broadcasted_iota(jnp.int32, (span, tile), 0)
        scores = scores + slope * key_at.astype(F32)
        low = key_at[mine] - i * tile <= lax.broadcasted_iota(jnp.int32, (tile, tile), 1)
        last = jnp.where(low, scores[mine], NEG_LARGE)
        if i:
            scores = jnp.concatenate([scores[: i * tile], last], axis=0)
        else:
            scores = last
        prob = jnp.exp2(scores - l_ref[i : i + 1, :])
        grad_prob = dot_trans(v_ref[0:span, :], grads)
        grad_scores = (prob * (grad_prob - row_dot)).astype(BF16)
        dv = plain_dot(prob.astype(BF16), grads)
        dk = plain_dot(grad_scores, queries)
        if i == tiles - 1:
            dv_ref[...] = dv
            dk_ref[...] = dk
        else:
            dv_ref[0:span, :] += dv
            dk_ref[0:span, :] += dk
        dq_ref[mine, :] = plain_dot(kt_ref[:, 0:span], grad_scores).T
    for t in range(pieces):
        rows = slice(t * piece, (t + 1) * piece)
        for c, (ref, factor) in enumerate(
            ((dq_ref, 1.0 / math.sqrt(HEAD_DIM)), (dk_ref, 1.0 / math.sqrt(HEAD_DIM)), (dv_ref, 1.0))
        ):
            at = pl.multiple_of((src_ref[0, t] + c * src_ref[1, 0]) * piece, piece)
            out_ref[pl.ds(at, piece), :] = (ref[rows, :] * factor).astype(BF16)


SMEM = pl.BlockSpec(memory_space=pltpu.SMEM)
VMEM = pl.BlockSpec(memory_space=pltpu.VMEM)


def unit_forward(recv, sources, slope2, tile, piece):
    rows = recv.shape[0] // 3
    half = jax.ShapeDtypeStruct((rows, HEAD_DIM), BF16)
    area = rows * rows // 2 * HEAD_DIM
    return pl.pallas_call(
        functools.partial(attend_forward_kernel, tile, piece),
        out_shape=(half,) * 5 + (jax.ShapeDtypeStruct((rows // tile, tile), F32),),
        in_specs=[SMEM, SMEM, VMEM],
        out_specs=(VMEM,) * 6,
        scratch_shapes=[pltpu.VMEM((HEAD_DIM, rows), BF16)],
        compiler_params=pltpu.CompilerParams(vmem_limit_bytes=48 << 20),
        cost_estimate=pl.CostEstimate(flops=4 * area, bytes_accessed=rows * 2048, transcendentals=rows * rows // 2),
        name="attend_forward",
    )(sources, slope2, recv)


def unit_backward(recv, kept, sources, slope2, tile, piece):
    rows = recv.shape[0]
    area = rows * rows // 2 * HEAD_DIM
    return pl.pallas_call(
        functools.partial(attend_backward_kernel, tile, piece),
        out_shape=jax.ShapeDtypeStruct((rows * 3, HEAD_DIM), BF16),
        in_specs=[SMEM, SMEM] + [VMEM] * 6,
        out_specs=VMEM,
        scratch_shapes=[
            pltpu.VMEM((rows, HEAD_DIM), BF16),
            pltpu.VMEM((HEAD_DIM, rows), BF16),
            pltpu.VMEM((rows, HEAD_DIM), F32),
            pltpu.VMEM((rows, HEAD_DIM), F32),
            pltpu.VMEM((rows, HEAD_DIM), F32),
        ],
        compiler_params=pltpu.CompilerParams(vmem_limit_bytes=48 << 20),
        cost_estimate=pl.CostEstimate(flops=10 * area, bytes_accessed=rows * 2560, transcendentals=rows * rows // 2),
        name="attend_backward",
    )(sources, slope2, recv, *kept)


def general_scores(queries, keys, query_pos, key_pos, slope):
    scores = dot_trans(queries, keys) / math.sqrt(HEAD_DIM)
    distance = (query_pos[:, None] - key_pos[None, :]).astype(F32)
    allowed = key_pos[None, :] <= query_pos[:, None]
    return jnp.where(allowed, scores - slope * distance, NEG_LARGE), allowed


def general_forward(queries, keys, values, query_pos, key_pos, slope):
    count = queries.shape[0]
    span = math.gcd(keys.shape[0], 1024)

    def visit(n, state):
        top, total, weighted = state
        key_rows = lax.dynamic_slice_in_dim(keys, n * span, span, 0)
        value_rows = lax.dynamic_slice_in_dim(values, n * span, span, 0)
        place = lax.dynamic_slice_in_dim(key_pos, n * span, span, 0)
        scores, allowed = general_scores(queries, key_rows, query_pos, place, slope)
        new_top = jnp.maximum(top, jnp.max(scores, axis=-1, keepdims=True))
        fade = jnp.exp(top - new_top)
        shifted = jnp.where(allowed, jnp.exp(scores - new_top), 0.0)
        total = total * fade + jnp.sum(shifted, axis=-1, keepdims=True)
        return new_top, total, weighted * fade + plain_dot(shifted.astype(BF16), value_rows)

    start = (jnp.full((count, 1), NEG_LARGE, F32), jnp.zeros((count, 1), F32), jnp.zeros((count, HEAD_DIM), F32))
    top, total, weighted = lax.fori_loop(0, keys.shape[0] // span, visit, start)
    return (weighted / total).astype(BF16), top + jnp.log(total)


def general_backward(queries, keys, values, attended, log_norm, grads, query_pos, key_pos, slope):
    span = math.gcd(keys.shape[0], 1024)
    row_dot = jnp.sum(grads.astype(F32) * attended.astype(F32), axis=-1, keepdims=True)

    def visit(n, state):
        key_rows = lax.dynamic_slice_in_dim(keys, n * span, span, 0)
        value_rows = lax.dynamic_slice_in_dim(values, n * span, span, 0)
        place = lax.dynamic_slice_in_dim(key_pos, n * span, span, 0)
        scores, allowed = general_scores(queries, key_rows, query_pos, place, slope)
        prob = jnp.where(allowed, jnp.exp(scores - log_norm), 0.0)
        grad_scores = (prob * (dot_trans(grads, value_rows) - row_dot)).astype(BF16)
        dq = state[0] + plain_dot(grad_scores, key_rows)
        dk = lax.dynamic_update_slice_in_dim(state[1], rows_dot(grad_scores, queries), n * span, 0)
        dv = lax.dynamic_update_slice_in_dim(state[2], rows_dot(prob.astype(BF16), grads), n * span, 0)
        return dq, dk, dv

    start = (jnp.zeros(queries.shape, F32), jnp.zeros(keys.shape, F32), jnp.zeros(keys.shape, F32))
    dq, dk, dv = lax.fori_loop(0, keys.shape[0] // span, visit, start)
    scale = 1.0 / math.sqrt(HEAD_DIM)
    return (dq * scale).astype(BF16), (dk * scale).astype(BF16), dv.astype(BF16)


def body(
    tokens,
    cotangent,
    block_table,
    norm1_gain,
    norm1_bias,
    w_query,
    w_key,
    w_value,
    w_output,
    norm2_gain,
    norm2_bias,
    w_up,
    b_up,
    w_down,
    b_down,
):
    head_count, blk_count = lax.axis_size("head"), lax.axis_size("blk")
    devices = head_count * blk_count
    sequences, _, tok_rows, width = tokens.shape
    head_in, blk_in = 2, (2 if blk_count <= 8 else 4)
    heads_here = HEADS // head_count
    cycle_rows = tok_rows * head_count
    half_rows = cycle_rows // 2
    seq_len = cycle_rows * blk_count
    own_rows = sequences * tok_rows
    d_part, f_part = width // devices, b_up.shape[0]
    hidden = f_part * devices
    f_here = hidden // head_count
    units = sequences * heads_here
    parts = blk_count // units
    rel_part = head_count // parts
    head_at, blk_at = lax.axis_index("head"), lax.axis_index("blk")
    head_o, head_i = place_of("head", head_in)
    everyone = ("head", "blk")

    x_own = tokens[:, 0].reshape(own_rows, width)
    g_own = cotangent[:, 0].reshape(own_rows, width)
    x_all = gather_relative(x_own, "head", head_in)

    def columns(*weights):
        cut = [w.reshape(d_part, head_count, -1).transpose(1, 0, 2) for w in weights]
        return lax.all_to_all(jnp.concatenate(cut, axis=2), "head", 0, 0, tiled=True)

    qkv_cols = columns(w_query, w_key, w_value)
    up_cols = columns(w_up)
    qkv_weight = gather_absolute(qkv_cols, "blk", blk_in, 1).reshape(width, -1)
    small = jnp.concatenate([norm1_gain, norm1_bias, norm2_gain, norm2_bias, b_down, b_up])
    small = lax.all_to_all(
        jnp.broadcast_to(small, (devices, 1, small.shape[0])), everyone, 0, 0, tiled=True
    )[:, 0].astype(F32)
    first_gain, first_shift, second_gain, second_shift, down_bias = (
        small[:, n * d_part : (n + 1) * d_part].reshape(width) for n in range(5)
    )
    up_bias = lax.dynamic_index_in_dim(
        small[:, 5 * d_part :].reshape(head_count, f_here), head_at, 0, keepdims=False
    )
    g_all = gather_relative(g_own, "head", head_in)
    output_weight = gather_absolute(w_output, "blk", blk_in, 0).reshape(-1, width)
    up_weight = gather_absolute(up_cols, "blk", blk_in, 1).reshape(width, f_here)
    down_weight = gather_absolute(w_down, "blk", blk_in, 0).reshape(f_here, width)

    flat_table = block_table.reshape(-1)
    head_of_rel = jnp.arange(head_count, dtype=jnp.int32)
    head_outer = head_count // head_in
    rel_head = ((head_o - head_of_rel // head_in) % head_outer) * head_in + (
        head_i - head_of_rel % head_in
    ) % head_in
    head_ids = head_at * heads_here + jnp.arange(heads_here, dtype=jnp.int32)
    unit, part = blk_at // parts, blk_at % parts
    my_head = head_ids[0] + unit % heads_here
    slope = jnp.exp2(-8.0 * (my_head + 1).astype(F32) / HEADS) * (BIAS_SPAN / seq_len)

    normed_all, spread_all = norm_parts(x_all.astype(F32))
    hidden_one = (normed_all * first_gain + first_shift).astype(BF16)
    normed_one, spread_one = normed_all[:own_rows], spread_all[:own_rows]
    qkv = plain_dot(hidden_one, qkv_weight).astype(BF16)

    def to_units(rows, kinds):
        rows = rows.reshape(parts, rel_part, sequences, tok_rows, kinds, heads_here, HEAD_DIM)
        rows = rows.transpose(2, 5, 0, 4, 1, 3, 6)
        rows = rows.reshape(blk_count, kinds, rel_part, tok_rows, HEAD_DIM)
        return lax.all_to_all(rows, "blk", 0, 0, tiled=True)

    def from_units(rows, kinds):
        rows = rows.reshape(blk_count, kinds, rel_part, tok_rows, HEAD_DIM)
        rows = lax.all_to_all(rows, "blk", 0, 0, tiled=True)
        rows = rows.reshape(sequences, heads_here, parts, kinds, rel_part, tok_rows, HEAD_DIM)
        rows = rows.transpose(2, 4, 0, 5, 3, 1, 6)
        return rows.reshape(head_count * own_rows, kinds * heads_here * HEAD_DIM)

    received = to_units(qkv, 3)
    if parts == 1:
        tile = 2 * half_rows
        count = seq_len // tok_rows
        pieces = jnp.arange(count, dtype=jnp.int32)
        per_half = half_rows // tok_rows
        blocks = pieces // per_half
        slots = jnp.arange(flat_table.shape[0], dtype=jnp.int32)
        slot = jnp.sum(jnp.where(flat_table[None, :] == blocks[:, None], slots[None, :], 0), axis=1)
        head_src = (slot % 2) * per_half + pieces % per_half
        rel = ((head_o - head_src // head_in) % head_outer) * head_in + (head_i - head_src % head_in) % head_in
        sources = jnp.stack(
            [
                (slot // 2) * (3 * head_count) + rel,
                jnp.full((count,), head_count, jnp.int32),
                (slot // 2) * head_count + rel,
            ]
        )
        slope2 = (slope * LOG2E).reshape(1)
        attended_unit, *kept = unit_forward(received.reshape(-1, HEAD_DIM), sources, slope2, tile, tok_rows)
    else:
        rel_rows = rel_head.reshape(parts, 1, rel_part, 1) * tok_rows + jnp.arange(tok_rows, dtype=jnp.int32)
        rows_at = rel_rows + jnp.arange(blk_count, dtype=jnp.int32)[None, :, None, None] * cycle_rows
        block_ids = rows_at // half_rows
        slots = jnp.arange(flat_table.shape[0], dtype=jnp.int32)
        picked = jnp.sum(jnp.where(block_ids[..., None] == slots, flat_table, 0), axis=-1)
        places = (picked * half_rows + rows_at % half_rows).reshape(parts, -1)

        def whole_unit(own):
            whole = jnp.zeros((parts,) + own.shape, own.dtype)
            for n in range(parts):
                piece = shift(own, "blk", parts, 0, n)
                whole = lax.dynamic_update_index_in_dim(whole, piece, (part - n) % parts, 0)
            return whole.reshape(-1, HEAD_DIM)

        queries, own_keys, own_values = (received[:, n].reshape(-1, HEAD_DIM) for n in range(3))
        keys, values = whole_unit(own_keys), whole_unit(own_values)
        query_pos = lax.dynamic_index_in_dim(places, part, 0, keepdims=False)
        key_pos = places.reshape(-1)
        attended_unit, log_norm = general_forward(queries, keys, values, query_pos, key_pos, slope)
    attended = from_units(attended_unit, 1)

    middle = x_own.astype(F32) + scatter_sum_relative(
        plain_dot(attended, output_weight).astype(BF16).reshape(head_count, own_rows, width), "head", head_in
    )
    normed_two, spread_two = norm_parts(middle)
    hidden_two = gather_relative((normed_two * second_gain + second_shift).astype(BF16), "head", head_in)

    up_values = plain_dot(hidden_two, up_weight) + up_bias
    activated, gelu_slope = gelu_and_slope(up_values)
    activated = activated.astype(BF16)
    grad_up_values = (dot_trans(g_all, down_weight) * gelu_slope).astype(BF16)
    grad_hidden_two = scatter_sum_relative(
        dot_trans(grad_up_values, up_weight).astype(BF16).reshape(head_count, own_rows, width), "head", head_in
    )
    result = scatter_sum_relative(
        plain_dot(activated, down_weight).astype(BF16).reshape(head_count, own_rows, width), "head", head_in
    )
    activations = (middle + result + down_bias).astype(BF16).reshape(tokens.shape)
    grad_down = rows_dot(activated, g_all).astype(BF16).reshape(blk_count, f_part, width)
    grad_up = rows_dot(hidden_two, grad_up_values).astype(BF16)
    grad_up_bias = jnp.sum(grad_up_values.astype(F32), axis=0)
    grad_float = g_own.astype(F32)
    grad_down_bias = jnp.sum(grad_float, axis=0)

    def grad_columns(grad):
        grad = grad.reshape(head_count, blk_count, d_part, -1)
        grad = scatter_sum_absolute(grad, "blk", blk_in, 1).astype(BF16)
        return lax.all_to_all(grad, "head", 0, 0, tiled=True).astype(F32)

    back_two, grad_second_gain, grad_second_shift = norm_back(grad_hidden_two, normed_two, spread_two, second_gain)
    grad_middle = grad_float + back_two
    grad_branch = gather_relative(grad_middle.astype(BF16), "head", head_in)
    grad_attended = dot_trans(grad_branch, output_weight).astype(BF16)
    grad_output = rows_dot(attended, grad_branch).astype(BF16).reshape(blk_count, d_part, width)
    grad_unit = to_units(grad_attended, 1)
    if parts == 1:
        grad_qkv_unit = unit_backward(grad_unit.reshape(-1, HEAD_DIM), kept, sources, slope2, tile, tok_rows)
    else:
        dq, dk, dv = general_backward(
            queries, keys, values, attended_unit, log_norm, grad_unit.reshape(-1, HEAD_DIM), query_pos, key_pos, slope
        )

        def own_part(grad):
            grad = grad.reshape(parts, -1, HEAD_DIM)
            total = 0.0
            for n in range(parts):
                piece = lax.dynamic_index_in_dim(grad, (part - n) % parts, 0, keepdims=False)
                total = total + shift(piece, "blk", parts, 0, -n).astype(F32)
            return total.astype(BF16)

        cut = (blk_count, rel_part, tok_rows, HEAD_DIM)
        grad_qkv_unit = jnp.stack([dq.reshape(cut), own_part(dk).reshape(cut), own_part(dv).reshape(cut)], axis=1)
    grad_qkv = from_units(grad_qkv_unit, 3)

    grad_hidden_one = scatter_sum_relative(
        dot_trans(grad_qkv, qkv_weight).astype(BF16).reshape(head_count, own_rows, width), "head", head_in
    )
    grad_down_own = scatter_sum_absolute(grad_down, "blk", blk_in, 0)
    grad_up_own = grad_columns(grad_up).transpose(1, 0, 2).reshape(d_part, hidden)
    grad_output_own = scatter_sum_absolute(grad_output, "blk", blk_in, 0)
    grad_qkv_own = grad_columns(rows_dot(hidden_one, grad_qkv).astype(BF16))
    grad_query, grad_key, grad_value = (
        grad_qkv_own[..., n * heads_here * HEAD_DIM : (n + 1) * heads_here * HEAD_DIM]
        .transpose(1, 0, 2)
        .reshape(d_part, width)
        for n in range(3)
    )
    back_one, grad_first_gain, grad_first_shift = norm_back(grad_hidden_one, normed_one, spread_one, first_gain)
    input_grad = (grad_middle + back_one).astype(BF16).reshape(tokens.shape)

    mine = (jnp.arange(head_count) == head_at)[:, None]
    bias_terms = jnp.where(mine, grad_up_bias[None, :], 0.0).reshape(devices, f_part)
    terms = jnp.concatenate(
        [
            t.reshape(devices, d_part)
            for t in (grad_first_gain, grad_first_shift, grad_second_gain, grad_second_shift, grad_down_bias)
        ]
        + [bias_terms],
        axis=1,
    )
    terms = jnp.sum(lax.all_to_all(terms[:, None, :], everyone, 0, 0, tiled=True), axis=(0, 1))
    g1, s1, g2, s2, bd = (terms[n * d_part : (n + 1) * d_part] for n in range(5))
    return (
        activations,
        input_grad,
        g1,
        s1,
        grad_query,
        grad_key,
        grad_value,
        grad_output_own,
        g2,
        s2,
        grad_up_own,
        terms[5 * d_part :],
        grad_down_own,
        bd,
    )


def solution(mesh):
    rows = P(None, "blk", "head", None)
    vector = P(("head", "blk"))
    matrix = P(("head", "blk"), None)
    params = (vector, vector, matrix, matrix, matrix, matrix, vector, vector, matrix, vector, matrix, vector)
    return jax.shard_map(
        body,
        mesh=mesh,
        in_specs=(rows, rows, P()) + params,
        out_specs=(rows, rows) + params,
        check_vma=False,
    )
```

```python
import functools
import math

import jax
import jax.numpy as jnp
from jax import lax
from jax.experimental import pallas as pl
from jax.experimental.pallas import tpu as pltpu
from jax.sharding import PartitionSpec as P

HEADS = 8
HEAD_DIM = 128
BIAS_SPAN = 1024
EPSILON = 1e-05
NEG_LARGE = -1e30
LOG2E = 1.4426950408889634
F32 = jnp.float32
BF16 = jnp.bfloat16
SMEM = pl.BlockSpec(memory_space=pltpu.SMEM)
VMEM = pl.BlockSpec(memory_space=pltpu.VMEM)
ANY = pl.BlockSpec(memory_space=pl.ANY)


def fixed(*shape):
    return pl.BlockSpec(shape, lambda n: (0,) * len(shape))


def shift(x, axis, inner, outer_step, inner_step):
    count = lax.axis_size(axis)
    outer = count // inner
    if outer_step % outer == 0 and inner_step % inner == 0:
        return x
    pairs = [
        (o * inner + i, ((o + outer_step) % outer) * inner + (i + inner_step) % inner)
        for o in range(outer)
        for i in range(inner)
    ]
    return lax.ppermute(x, axis, pairs)


def place_of(axis, inner):
    me = lax.axis_index(axis)
    return me // inner, me % inner


def gather_far(x, axis, inner):
    return [shift(x, axis, inner, a, 0) for a in range(lax.axis_size(axis) // inner)]


def gather_near(far, axis, inner):
    return [shift(x, axis, inner, 0, c) for x in far for c in range(inner)]


def gather_pieces(x, axis, inner):
    return gather_near(gather_far(x, axis, inner), axis, inner)


def gather_relative(x, axis, inner):
    return jnp.concatenate(gather_pieces(x, axis, inner), axis=0)


def copies_kernel(moves, count, numbers_ref, *refs):
    sems = refs[-1]
    started = []
    for n, (source, source_at, target, target_at) in enumerate(moves(numbers_ref)):
        from_ref, to_ref = refs[source], refs[count + target]
        move = pltpu.make_async_copy(from_ref.at[source_at], to_ref.at[target_at], sems.at[n])
        move.start()
        started.append(move)
    for move in started:
        move.wait()


def copy_blocks(arrays, numbers, shapes, moves, how_many, name):
    size = sum(math.prod(a.shape) for a in arrays) * 4
    return pl.pallas_call(
        functools.partial(copies_kernel, moves, len(arrays)),
        out_shape=tuple(jax.ShapeDtypeStruct(shape, arrays[0].dtype) for shape in shapes),
        in_specs=[SMEM] + [ANY] * len(arrays),
        out_specs=(VMEM,) * len(shapes),
        scratch_shapes=[pltpu.SemaphoreType.DMA((how_many,))],
        compiler_params=pltpu.CompilerParams(vmem_limit_bytes=24 << 20),
        cost_estimate=pl.CostEstimate(flops=0, bytes_accessed=size, transcendentals=0),
        name=name,
    )(numbers, *arrays)


def slots_of(axis, inner):
    count = lax.axis_size(axis)
    outer = count // inner
    o, i = place_of(axis, inner)
    rel = jnp.arange(count, dtype=jnp.int32)
    return ((o - rel // inner) % outer) * inner + (i - rel % inner) % inner


def laid_by_devices(pieces, axes, name):
    (outer_axis, outer_in), (inner_axis, inner_in) = axes
    count, stacked = len(pieces), pieces[0].shape[0]
    numbers = jnp.concatenate([slots_of(outer_axis, outer_in), slots_of(inner_axis, inner_in)])

    def moves(slots):
        return [
            (n, (r,), 0, (slots[r], slots[stacked + n])) for n in range(count) for r in range(stacked)
        ]

    shape = (stacked, count) + pieces[0].shape[1:]
    return copy_blocks(pieces, numbers, [shape], moves, count * stacked, name)[0]


def partners_of(axis, inner):
    count = lax.axis_size(axis)
    outer = count // inner
    o, i = place_of(axis, inner)
    rel = jnp.arange(count, dtype=jnp.int32)
    return ((o + rel // inner) % outer) * inner + (i + rel % inner) % inner


def small_call(kernel, numbers, arrays, shapes, name):
    return pl.pallas_call(
        kernel,
        grid=(1,),
        out_shape=tuple(shapes),
        in_specs=[SMEM] + [fixed(*a.shape) for a in arrays],
        out_specs=tuple(fixed(*o.shape) for o in shapes),
        compiler_params=pltpu.CompilerParams(vmem_limit_bytes=24 << 20),
        cost_estimate=pl.CostEstimate(flops=0, bytes_accessed=1 << 20, transcendentals=0),
        name=name,
    )(numbers, *arrays)


def exchange(pieces, axis, inner):
    return [shift(p, axis, inner, n // inner, n % inner) for n, p in enumerate(pieces)]


def cut_columns(weights, axis, inner, name):
    count, rows = lax.axis_size(axis), weights[0].shape[0]
    widths = [w.shape[1] // count for w in weights]

    def kernel(numbers_ref, *refs):
        for n in range(count):
            at = 0
            for ref, wide in zip(refs[: len(weights)], widths, strict=True):
                start = pl.multiple_of(numbers_ref[n] * wide, wide)
                refs[len(weights) + n][:, at : at + wide] = ref[:, pl.ds(start, wide)]
                at += wide

    shapes = [jax.ShapeDtypeStruct((rows, sum(widths)), BF16)] * count
    return small_call(kernel, partners_of(axis, inner), weights, shapes, name)


def sum_slabs(parts, axis, inner, name):
    count, rows, wide = parts[0].shape

    def kernel(numbers_ref, *refs):
        for n in range(count):
            total = refs[0][numbers_ref[n]].astype(F32)
            for ref in refs[1 : len(parts)]:
                total = total + ref[numbers_ref[n]].astype(F32)
            refs[len(parts) + n][...] = total.astype(BF16)

    shapes = [jax.ShapeDtypeStruct((rows, wide), BF16)] * count
    return small_call(kernel, partners_of(axis, inner), parts, shapes, name)


def join_columns(pieces, axis, inner, kinds, name):
    count = len(pieces)
    rows, wide = pieces[0].shape
    wide //= kinds

    def kernel(numbers_ref, *refs):
        for n in range(count):
            start = pl.multiple_of(numbers_ref[n] * wide, wide)
            for k in range(kinds):
                refs[count + k][:, pl.ds(start, wide)] = refs[n][:, k * wide : (k + 1) * wide].astype(F32)

    shapes = [jax.ShapeDtypeStruct((rows, wide * count), F32)] * kinds
    return small_call(kernel, slots_of(axis, inner), pieces, shapes, name)


def after(value, *others):
    return lax.optimization_barrier((value, others))[0]


def halves_near(keep, came):
    return [(keep[a].astype(F32) + came[a].astype(F32)).astype(BF16) for a in range(1, keep.shape[0])]


def halves_far(near, axis):
    return [shift(n, axis, 2, -1 - a, 0) for a, n in enumerate(near)]


def scatter_near(x, axis, inner, slot_dim):
    outer = lax.axis_size(axis) // inner
    _, i = place_of(axis, inner)
    lead, rest = x.shape[:slot_dim], x.shape[slot_dim + 1 :]
    x = x.reshape(lead + (outer, inner) + rest)

    def column(c):
        return lax.dynamic_index_in_dim(x, (i - c) % inner, slot_dim + 1, keepdims=False)

    total = column(0).astype(F32)
    for c in range(1, inner):
        total = total + shift(column(c), axis, inner, 0, -c).astype(F32)
    return total.astype(BF16)


def scatter_far_first(x, axis, inner):
    outer = lax.axis_size(axis) // inner
    x = x.reshape((outer, inner) + x.shape[1:])
    return sum(part.astype(F32) for part in far_parts(x, axis, inner, 0)).astype(BF16)


def scatter_near_last(far, axis, inner):
    _, i = place_of(axis, inner)
    pieces = [lax.dynamic_index_in_dim(far, (i - c) % inner, 0, keepdims=False) for c in range(inner)]
    return sum(shift(piece, axis, inner, 0, -c).astype(F32) for c, piece in enumerate(pieces))


def far_parts(near, axis, inner, slot_dim):
    outer = lax.axis_size(axis) // inner
    o, _ = place_of(axis, inner)
    pieces = [lax.dynamic_index_in_dim(near, (o - a) % outer, slot_dim, keepdims=False) for a in range(outer)]
    return [shift(piece, axis, inner, -a, 0) for a, piece in enumerate(pieces)]


def scatter_far(near, axis, inner, slot_dim):
    return sum(part.astype(F32) for part in far_parts(near, axis, inner, slot_dim))


def norm_parts(values):
    center = values - jnp.mean(values, axis=-1, keepdims=True)
    spread = lax.rsqrt(jnp.mean(center * center, axis=-1, keepdims=True) + EPSILON)
    return (center * spread, spread)


def norm_back(grad_normed, normed, spread, gain):
    scaled = grad_normed * gain
    inner = (
        scaled
        - jnp.mean(scaled, axis=-1, keepdims=True)
        - normed * jnp.mean(scaled * normed, axis=-1, keepdims=True)
    )
    return (spread * inner, jnp.sum(grad_normed * normed, axis=0), jnp.sum(grad_normed, axis=0))


def plain_dot(left, right):
    return jnp.dot(left, right, preferred_element_type=F32)


def rows_dot(left, right):
    return lax.dot_general(left, right, (((0,), (0,)), ((), ())), preferred_element_type=F32)


def dot_stacked(left, right, rows):
    return plain_dot(left, right[:, :rows].reshape(-1, right.shape[2]))


def dot_trans(left, right):
    return lax.dot_general(left, right, (((1,), (1,)), ((), ())), preferred_element_type=F32)


def gelu_and_slope(u):
    k = math.sqrt(2.0 / math.pi)
    t = jnp.tanh(k * (u + 0.044715 * (u * u * u)))
    half = 0.5 * (1.0 + t)
    slope = half + 0.5 * u * (1.0 - t * t) * (k * (1.0 + 3 * 0.044715 * (u * u)))
    return u * half, slope


class Plan:
    def __init__(self, head_count, blk_count, sequences, tok_rows, heads_here):
        self.blocks, self.sequences, self.tok, self.heads = head_count, sequences, tok_rows, heads_here
        self.own = sequences * tok_rows
        self.units = sequences * heads_here
        self.parts = blk_count // self.units
        self.rel = head_count // self.parts

    def packed(self, kinds):
        return (self.units, self.parts, kinds, self.rel, self.tok, HEAD_DIM)

    def packed_spec(self, kinds):
        return pl.BlockSpec(
            (self.units, 1, kinds, 1, self.tok, HEAD_DIM), lambda n: (0, n // self.rel, 0, n % self.rel, 0, 0)
        )

    def rows_spec(self, width):
        return pl.BlockSpec((self.own, width), lambda n: (n, 0))

    def pick(self, refs):
        value = refs[0][...]
        for n in range(1, self.blocks):
            value = jnp.where(pl.program_id(0) == n, refs[n][...], value)
        return value

    def half_spec(self, width):
        return pl.BlockSpec((1, self.own, width), lambda n: (n // 2, 0, 0))

    def half(self, width):
        return jax.ShapeDtypeStruct((self.blocks // 2, self.own, width), BF16)

    def pack(self, out_ref, rows, kinds):
        for c in range(kinds):
            for e in range(self.heads):
                col = (c * self.heads + e) * HEAD_DIM
                for s in range(self.sequences):
                    cut = rows[s * self.tok : (s + 1) * self.tok, col : col + HEAD_DIM]
                    out_ref[s * self.heads + e, 0, c, 0] = cut

    def unpack(self, in_ref, rows_ref, kinds):
        for c in range(kinds):
            for e in range(self.heads):
                col = (c * self.heads + e) * HEAD_DIM
                for s in range(self.sequences):
                    cut = in_ref[s * self.heads + e, 0, c, 0]
                    rows_ref[s * self.tok : (s + 1) * self.tok, col : col + HEAD_DIM] = cut


def split_store(keep_ref, send_ref, value):
    odd = pl.program_id(0) % 2 == 1
    value = value.astype(BF16)

    @pl.when(jnp.logical_not(odd))
    def _():
        keep_ref[0] = value

    @pl.when(odd)
    def _():
        send_ref[0] = value


def stacked_part(joint, start, rows):
    count, _, width = joint.shape
    if start % rows or rows % 16:
        joint, start = joint[:, start : start + rows], 0
    at = start // rows
    return joint, pl.BlockSpec((count, rows, width), lambda n: (0, at, 0))


def big_call(kernel, plan, name, flops, out_shape, in_specs, out_specs, scratch=()):
    return pl.pallas_call(
        kernel,
        grid=(plan.blocks,),
        out_shape=out_shape,
        in_specs=in_specs,
        out_specs=out_specs,
        scratch_shapes=scratch,
        compiler_params=pltpu.CompilerParams(vmem_limit_bytes=48 << 20),
        cost_estimate=pl.CostEstimate(flops=flops, bytes_accessed=8 << 20, transcendentals=0),
        name=name,
    )


def project(plan, x, gain, shift_row, weight):
    width, kinds_width = weight.shape
    rows = plan.blocks * plan.own

    def kernel(*refs):
        x_refs, (gain_ref, shift_ref, w_ref, h_ref, out_ref) = refs[: plan.blocks], refs[plan.blocks :]
        normed, _ = norm_parts(plan.pick(x_refs).astype(F32))
        h = (normed * gain_ref[...] + shift_ref[...]).astype(BF16)
        h_ref[...] = h
        plan.pack(out_ref, plain_dot(h, w_ref[...]).astype(BF16), 3)

    return big_call(
        kernel,
        plan,
        "project",
        2 * rows * width * kinds_width,
        (jax.ShapeDtypeStruct((rows, width), BF16), jax.ShapeDtypeStruct(plan.packed(3), BF16)),
        [fixed(plan.own, width)] * plan.blocks + [fixed(1, width), fixed(1, width), fixed(width, kinds_width)],
        (plan.rows_spec(width), plan.packed_spec(3)),
    )(*x, gain, shift_row, weight)


def project_out(plan, received, weight):
    weight, w_spec = weight
    here, width = plan.heads * HEAD_DIM, weight.shape[2]

    def kernel(in_ref, w_ref, rows_ref, keep_ref, send_ref):
        plan.unpack(in_ref, rows_ref, 1)
        split_store(keep_ref, send_ref, plain_dot(rows_ref[...], w_ref[...].reshape(here, width)))

    rows = plan.blocks * plan.own
    return big_call(
        kernel,
        plan,
        "project_out",
        2 * rows * width * here,
        (jax.ShapeDtypeStruct((rows, here), BF16), plan.half(width), plan.half(width)),
        [plan.packed_spec(1), w_spec],
        (plan.rows_spec(here), plan.half_spec(width), plan.half_spec(width)),
    )(received, weight)


def project_out_back(plan, grad, weight, behind):
    weight, w_spec = weight
    here, width = plan.heads * HEAD_DIM, weight.shape[2]
    rows = plan.blocks * plan.own

    def kernel(*refs):
        in_refs, w_ref, (rows_ref, out_ref) = refs[: plan.blocks], refs[plan.blocks], refs[-2:]
        value = plan.pick(in_refs)
        rows_ref[...] = value
        plan.pack(out_ref, dot_trans(value, w_ref[...].reshape(here, width)).astype(BF16), 1)

    return big_call(
        kernel,
        plan,
        "project_out_back",
        2 * rows * width * here,
        (jax.ShapeDtypeStruct((rows, width), BF16), jax.ShapeDtypeStruct(plan.packed(1), BF16)),
        [fixed(plan.own, width)] * plan.blocks + [w_spec] + [ANY] * len(behind),
        (plan.rows_spec(width), plan.packed_spec(1)),
    )(*grad, weight, *behind)


def project_back(plan, received, weight, behind):
    width, here = weight.shape

    def kernel(in_ref, w_ref, *refs):
        rows_ref, keep_ref, send_ref = refs[-3:]
        plan.unpack(in_ref, rows_ref, 3)
        split_store(keep_ref, send_ref, dot_trans(rows_ref[...], w_ref[...]))

    rows = plan.blocks * plan.own
    return big_call(
        kernel,
        plan,
        "project_back",
        2 * rows * width * here,
        (jax.ShapeDtypeStruct((rows, here), BF16), plan.half(width), plan.half(width)),
        [plan.packed_spec(3), fixed(width, here)] + [ANY] * len(behind),
        (plan.rows_spec(here), plan.half_spec(width), plan.half_spec(width)),
    )(received, weight, *behind)


def feed_forward(plan, hidden, grad, up_weight, up_bias, down_weight):
    up_weight, up_spec = up_weight
    down_weight, down_spec = down_weight
    width, here = down_weight.shape[2], up_weight.shape[2]
    count, stacked = up_weight.shape[0], plan.blocks
    cut = width // (count * stacked)
    rows = plan.blocks * plan.own

    def kernel(*refs):
        h_refs, refs = refs[: plan.blocks], refs[plan.blocks :]
        g_ref, up_ref, bias_ref, down_ref, h_ref, act_ref, grad_ref, bias_grad_ref, keep_ref, send_ref, in_order = refs

        @pl.when(pl.program_id(0) == 0)
        def _():
            for b in range(count):
                for h in range(stacked):
                    in_order[h, b] = up_ref[b, h * cut : (h + 1) * cut, :]

        up_rows = in_order[...].reshape(width, here)
        value = plan.pick(h_refs)
        h_ref[...] = value
        act, slope = gelu_and_slope(plain_dot(value, up_rows) + bias_ref[...])
        act_ref[...] = act.astype(BF16)
        grad_up = (dot_trans(g_ref[...], down_ref[...].reshape(here, width)) * slope).astype(BF16)
        grad_ref[...] = grad_up
        sums = jnp.sum(grad_up.astype(F32), axis=0, keepdims=True)

        @pl.when(pl.program_id(0) == 0)
        def _():
            bias_grad_ref[...] = sums

        @pl.when(pl.program_id(0) > 0)
        def _():
            bias_grad_ref[...] += sums

        split_store(keep_ref, send_ref, dot_trans(grad_up, up_rows))

    return big_call(
        kernel,
        plan,
        "feed_forward",
        6 * rows * width * here,
        (
            jax.ShapeDtypeStruct((rows, width), BF16),
            jax.ShapeDtypeStruct((rows, here), BF16),
            jax.ShapeDtypeStruct((rows, here), BF16),
            jax.ShapeDtypeStruct((1, here), F32),
            plan.half(width),
            plan.half(width),
        ),
        [fixed(plan.own, width)] * plan.blocks
        + [plan.rows_spec(width), up_spec, fixed(1, here), down_spec],
        (
            plan.rows_spec(width),
            plan.rows_spec(here),
            plan.rows_spec(here),
            fixed(1, here),
            plan.half_spec(width),
            plan.half_spec(width),
        ),
        [pltpu.VMEM((stacked, count, cut, here), BF16)],
    )(*hidden, grad, up_weight, up_bias, down_weight)


def norm_call(kernel, arrays, behind, shapes, name):
    def body(*refs):
        kernel(refs[: len(arrays)], refs[len(arrays) + len(behind) :])

    return pl.pallas_call(
        body,
        grid=(1,),
        out_shape=tuple(shapes),
        in_specs=[fixed(*a.shape) for a in arrays] + [ANY] * len(behind),
        out_specs=tuple(fixed(*o.shape) for o in shapes),
        compiler_params=pltpu.CompilerParams(vmem_limit_bytes=40 << 20),
        cost_estimate=pl.CostEstimate(flops=10 << 20, bytes_accessed=4 << 20, transcendentals=0),
        name=name,
    )(*arrays, *behind)


def summed(refs):
    keep_ref, came_ref = refs[:2]
    total = keep_ref[0].astype(F32) + came_ref[0].astype(F32)
    for ref in refs[2:]:
        total = total + ref[...].astype(F32)
    return total


def second_norm(x, terms, gain, shift_row, behind):
    def kernel(ins, outs):
        middle = ins[0][...].astype(F32) + summed(ins[3:])
        normed, _ = norm_parts(middle)
        outs[0][...] = middle
        outs[1][...] = (normed * ins[1][...] + ins[2][...]).astype(BF16)

    shapes = [jax.ShapeDtypeStruct(x.shape, F32), jax.ShapeDtypeStruct(x.shape, BF16)]
    return norm_call(kernel, [x, gain, shift_row, *terms], behind, shapes, "second_norm")


def second_norm_back(middle, grad, terms, gain, behind):
    def kernel(ins, outs):
        normed, spread = norm_parts(ins[0][...])
        grad_out = ins[1][...].astype(F32)
        back, gain_sum, shift_sum = norm_back(summed(ins[3:]), normed, spread, ins[2][...])
        total = grad_out + back
        outs[0][...] = total
        outs[1][...] = total.astype(BF16)
        outs[2][...] = gain_sum[None]
        outs[3][...] = shift_sum[None]
        outs[4][...] = jnp.sum(grad_out, axis=0, keepdims=True)

    row = jax.ShapeDtypeStruct((1, grad.shape[1]), F32)
    shapes = [jax.ShapeDtypeStruct(grad.shape, F32), jax.ShapeDtypeStruct(grad.shape, BF16), row, row, row]
    return norm_call(kernel, [middle, grad, gain, *terms], behind, shapes, "second_norm_back")


def first_norm_back(x, grad, terms, gain, behind):
    def kernel(ins, outs):
        normed, spread = norm_parts(ins[0][...].astype(F32))
        back, gain_sum, shift_sum = norm_back(summed(ins[3:]), normed, spread, ins[2][...])
        outs[0][...] = (ins[1][...] + back).astype(BF16)
        outs[1][...] = gain_sum[None]
        outs[2][...] = shift_sum[None]

    row = jax.ShapeDtypeStruct((1, x.shape[1]), F32)
    return norm_call(kernel, [x, grad, gain, *terms], behind, [jax.ShapeDtypeStruct(x.shape, BF16), row, row], "first_norm_back")


def attend_forward_kernel(tile, piece, src_ref, slope_ref, recv_ref, out_ref, q_ref, k_ref, v_ref, o_ref, l_ref, vt_ref):
    pieces = q_ref.shape[0] // piece
    rel = recv_ref.shape[0] // piece // 3 // src_ref.shape[1]
    for t in range(pieces):
        for c, ref in enumerate((q_ref, k_ref, v_ref)):
            at = pl.multiple_of((src_ref[0, t] + c * src_ref[1, 0]) * piece, piece)
            ref[t * piece : (t + 1) * piece, :] = recv_ref[pl.ds(at, piece), :]
    tiles = q_ref.shape[0] // tile
    for j in range(tiles):
        rows = slice(j * tile, (j + 1) * tile)
        vt_ref[:, rows] = v_ref[rows, :].T
    slope = slope_ref[0]
    scale = LOG2E / math.sqrt(HEAD_DIM)
    for i in range(tiles):
        span = (i + 1) * tile
        scores = dot_trans(k_ref[0:span, :], q_ref[i * tile : span, :]) * scale
        key_at = lax.broadcasted_iota(jnp.int32, (span, tile), 0)
        scores = scores + slope * key_at.astype(F32)
        low = key_at[i * tile : span] - i * tile <= lax.broadcasted_iota(jnp.int32, (tile, tile), 1)
        last = jnp.where(low, scores[i * tile : span], NEG_LARGE)
        if i:
            scores = jnp.concatenate([scores[: i * tile], last], axis=0)
        else:
            scores = last
        top = jnp.max(scores, axis=0, keepdims=True)
        shifted = jnp.exp2(scores - top)
        total = jnp.sum(shifted, axis=0, keepdims=True)
        l_ref[i : i + 1, :] = top + jnp.log2(total)
        prob = (shifted * (1.0 / total)).astype(BF16)
        o_ref[i * tile : span, :] = plain_dot(vt_ref[:, 0:span], prob).T.astype(BF16)
    for t in range(pieces):
        at = pl.multiple_of(src_ref[2, t] * piece, piece)
        out_ref[pl.ds(at, piece), :] = o_ref[t * piece : (t + 1) * piece, :]


def attend_backward_kernel(tile, piece, src_ref, slope_ref, recv_ref, q_ref, k_ref, v_ref, o_ref, l_ref, *refs):
    out_ref, d_ref, kt_ref, dq_ref, dk_ref, dv_ref = refs[-6:]
    pieces = q_ref.shape[0] // piece
    for t in range(pieces):
        at = pl.multiple_of(src_ref[2, t] * piece, piece)
        d_ref[t * piece : (t + 1) * piece, :] = recv_ref[pl.ds(at, piece), :]
    tiles = q_ref.shape[0] // tile
    for j in range(tiles):
        rows = slice(j * tile, (j + 1) * tile)
        kt_ref[:, rows] = k_ref[rows, :].T
    slope = slope_ref[0]
    scale = LOG2E / math.sqrt(HEAD_DIM)
    for i in reversed(range(tiles)):
        span = (i + 1) * tile
        mine = slice(i * tile, span)
        queries, grads = q_ref[mine, :], d_ref[mine, :]
        row_dot = lax.dot_general(
            jnp.ones((8, HEAD_DIM), F32),
            grads.astype(F32) * o_ref[mine, :].astype(F32),
            (((1,), (1,)), ((), ())),
            precision=lax.Precision.HIGHEST,
            preferred_element_type=F32,
        )[0:1]
        scores = dot_trans(k_ref[0:span, :], queries) * scale
        key_at = lax.broadcasted_iota(jnp.int32, (span, tile), 0)
        scores = scores + slope * key_at.astype(F32)
        low = key_at[mine] - i * tile <= lax.broadcasted_iota(jnp.int32, (tile, tile), 1)
        last = jnp.where(low, scores[mine], NEG_LARGE)
        if i:
            scores = jnp.concatenate([scores[: i * tile], last], axis=0)
        else:
            scores = last
        prob = jnp.exp2(scores - l_ref[i : i + 1, :])
        grad_prob = dot_trans(v_ref[0:span, :], grads)
        grad_scores = (prob * (grad_prob - row_dot)).astype(BF16)
        dv = plain_dot(prob.astype(BF16), grads)
        dk = plain_dot(grad_scores, queries)
        if i == tiles - 1:
            dv_ref[...] = dv
            dk_ref[...] = dk
        else:
            dv_ref[0:span, :] += dv
            dk_ref[0:span, :] += dk
        dq_ref[mine, :] = plain_dot(kt_ref[:, 0:span], grad_scores).T
    for t in range(pieces):
        rows = slice(t * piece, (t + 1) * piece)
        for c, (ref, factor) in enumerate(
            ((dq_ref, 1.0 / math.sqrt(HEAD_DIM)), (dk_ref, 1.0 / math.sqrt(HEAD_DIM)), (dv_ref, 1.0))
        ):
            at = pl.multiple_of((src_ref[0, t] + c * src_ref[1, 0]) * piece, piece)
            out_ref[pl.ds(at, piece), :] = (ref[rows, :] * factor).astype(BF16)


def unit_forward(recv, sources, slope2, tile, piece):
    rows = recv.shape[0] // 3
    half = jax.ShapeDtypeStruct((rows, HEAD_DIM), BF16)
    area = rows * rows // 2 * HEAD_DIM
    return pl.pallas_call(
        functools.partial(attend_forward_kernel, tile, piece),
        grid=(1,),
        out_shape=(half,) * 5 + (jax.ShapeDtypeStruct((rows // tile, tile), F32),),
        in_specs=[SMEM, SMEM, fixed(*recv.shape)],
        out_specs=(fixed(rows, HEAD_DIM),) * 5 + (fixed(rows // tile, tile),),
        scratch_shapes=[pltpu.VMEM((HEAD_DIM, rows), BF16)],
        compiler_params=pltpu.CompilerParams(vmem_limit_bytes=48 << 20),
        cost_estimate=pl.CostEstimate(flops=4 * area, bytes_accessed=rows * 2048, transcendentals=rows * rows // 2),
        name="attend_forward",
    )(sources, slope2, recv)


def unit_backward(recv, kept, sources, slope2, tile, piece, behind):
    rows = recv.shape[0]
    area = rows * rows // 2 * HEAD_DIM
    return pl.pallas_call(
        functools.partial(attend_backward_kernel, tile, piece),
        grid=(1,),
        out_shape=jax.ShapeDtypeStruct((rows * 3, HEAD_DIM), BF16),
        in_specs=[SMEM, SMEM] + [fixed(*a.shape) for a in (recv, *kept)] + [ANY] * len(behind),
        out_specs=fixed(rows * 3, HEAD_DIM),
        scratch_shapes=[
            pltpu.VMEM((rows, HEAD_DIM), BF16),
            pltpu.VMEM((HEAD_DIM, rows), BF16),
            pltpu.VMEM((rows, HEAD_DIM), F32),
            pltpu.VMEM((rows, HEAD_DIM), F32),
            pltpu.VMEM((rows, HEAD_DIM), F32),
        ],
        compiler_params=pltpu.CompilerParams(vmem_limit_bytes=48 << 20),
        cost_estimate=pl.CostEstimate(flops=10 * area, bytes_accessed=rows * 2560, transcendentals=rows * rows // 2),
        name="attend_backward",
    )(sources, slope2, recv, *kept, *behind)


def general_scores(queries, keys, query_pos, key_pos, slope):
    scores = dot_trans(queries, keys) / math.sqrt(HEAD_DIM)
    distance = (query_pos[:, None] - key_pos[None, :]).astype(F32)
    allowed = key_pos[None, :] <= query_pos[:, None]
    return jnp.where(allowed, scores - slope * distance, NEG_LARGE), allowed


def general_forward(queries, keys, values, query_pos, key_pos, slope):
    count = queries.shape[0]
    span = math.gcd(keys.shape[0], 1024)

    def visit(n, state):
        top, total, weighted = state
        key_rows = lax.dynamic_slice_in_dim(keys, n * span, span, 0)
        value_rows = lax.dynamic_slice_in_dim(values, n * span, span, 0)
        place = lax.dynamic_slice_in_dim(key_pos, n * span, span, 0)
        scores, allowed = general_scores(queries, key_rows, query_pos, place, slope)
        new_top = jnp.maximum(top, jnp.max(scores, axis=-1, keepdims=True))
        fade = jnp.exp(top - new_top)
        shifted = jnp.where(allowed, jnp.exp(scores - new_top), 0.0)
        total = total * fade + jnp.sum(shifted, axis=-1, keepdims=True)
        return new_top, total, weighted * fade + plain_dot(shifted.astype(BF16), value_rows)

    start = (jnp.full((count, 1), NEG_LARGE, F32), jnp.zeros((count, 1), F32), jnp.zeros((count, HEAD_DIM), F32))
    top, total, weighted = lax.fori_loop(0, keys.shape[0] // span, visit, start)
    return (weighted / total).astype(BF16), top + jnp.log(total)


def general_backward(queries, keys, values, attended, log_norm, grads, query_pos, key_pos, slope):
    span = math.gcd(keys.shape[0], 1024)
    row_dot = jnp.sum(grads.astype(F32) * attended.astype(F32), axis=-1, keepdims=True)

    def visit(n, state):
        key_rows = lax.dynamic_slice_in_dim(keys, n * span, span, 0)
        value_rows = lax.dynamic_slice_in_dim(values, n * span, span, 0)
        place = lax.dynamic_slice_in_dim(key_pos, n * span, span, 0)
        scores, allowed = general_scores(queries, key_rows, query_pos, place, slope)
        prob = jnp.where(allowed, jnp.exp(scores - log_norm), 0.0)
        grad_scores = (prob * (dot_trans(grads, value_rows) - row_dot)).astype(BF16)
        dq = state[0] + plain_dot(grad_scores, key_rows)
        dk = lax.dynamic_update_slice_in_dim(state[1], rows_dot(grad_scores, queries), n * span, 0)
        dv = lax.dynamic_update_slice_in_dim(state[2], rows_dot(prob.astype(BF16), grads), n * span, 0)
        return dq, dk, dv

    start = (jnp.zeros(queries.shape, F32), jnp.zeros(keys.shape, F32), jnp.zeros(keys.shape, F32))
    dq, dk, dv = lax.fori_loop(0, keys.shape[0] // span, visit, start)
    scale = 1.0 / math.sqrt(HEAD_DIM)
    return (dq * scale).astype(BF16), (dk * scale).astype(BF16), dv.astype(BF16)


def body(
    tokens,
    cotangent,
    block_table,
    norm1_gain,
    norm1_bias,
    w_query,
    w_key,
    w_value,
    w_output,
    norm2_gain,
    norm2_bias,
    w_up,
    b_up,
    w_down,
    b_down,
):
    head_count, blk_count = lax.axis_size("head"), lax.axis_size("blk")
    devices = head_count * blk_count
    sequences, _, tok_rows, width = tokens.shape
    head_in, blk_in = 2, (2 if blk_count <= 8 else 4)
    heads_here = HEADS // head_count
    cycle_rows = tok_rows * head_count
    half_rows = cycle_rows // 2
    seq_len = cycle_rows * blk_count
    own_rows = sequences * tok_rows
    d_part, f_part = width // devices, b_up.shape[0]
    hidden = f_part * devices
    f_here = hidden // head_count
    units = sequences * heads_here
    parts = blk_count // units
    rel_part = head_count // parts
    head_at, blk_at = lax.axis_index("head"), lax.axis_index("blk")
    head_o, head_i = place_of("head", head_in)
    everyone = ("head", "blk")

    x_own = tokens[:, 0].reshape(own_rows, width)
    g_own = cotangent[:, 0].reshape(own_rows, width)

    def columns(*weights):
        cut = [w.reshape(d_part, head_count, -1).transpose(1, 0, 2) for w in weights]
        return lax.all_to_all(jnp.concatenate(cut, axis=2), "head", 0, 0, tiled=True)

    qkv_cols = cut_columns([w_query, w_key, w_value], "head", head_in, "cut_qkv")
    qkv_cols = jnp.stack(exchange(qkv_cols, "head", head_in))
    x_pieces = gather_pieces(after(x_own, qkv_cols), "head", head_in)
    qkv_far = gather_far(qkv_cols, "blk", blk_in)
    qkv_pieces = gather_near(qkv_far, "blk", blk_in)
    small = jnp.concatenate(
        [v.reshape(-1, d_part) for v in (norm1_gain, norm1_bias, norm2_gain, norm2_bias, b_down, b_up)], axis=0
    )
    small = after(small, qkv_cols)
    small = lax.all_to_all(
        jnp.broadcast_to(small, (devices,) + small.shape), everyone, 0, 0, tiled=True
    ).astype(F32)
    first_gain, first_shift, second_gain, second_shift, down_bias = (
        small[:, n].reshape(1, width) for n in range(5)
    )
    up_bias = lax.dynamic_index_in_dim(small[:, 5:].reshape(head_count, f_here), head_at, 0)
    qkv_pieces = after(qkv_pieces, x_pieces, first_gain, first_shift)
    qkv_weight = laid_by_devices(qkv_pieces, (("head", head_in), ("blk", blk_in)), "lay_qkv").reshape(width, -1)
    joint = after(jnp.concatenate([w_down, w_output], axis=0), qkv_pieces)
    joint = lax.all_gather(joint, "blk", axis=0, tiled=False)
    down_weight, output_weight = stacked_part(joint, 0, f_part), stacked_part(joint, f_part, d_part)

    flat_table = block_table.reshape(-1)
    head_of_rel = jnp.arange(head_count, dtype=jnp.int32)
    head_outer = head_count // head_in
    rel_head = ((head_o - head_of_rel // head_in) % head_outer) * head_in + (
        head_i - head_of_rel % head_in
    ) % head_in
    head_ids = head_at * heads_here + jnp.arange(heads_here, dtype=jnp.int32)
    unit, part = blk_at // parts, blk_at % parts
    my_head = head_ids[0] + unit % heads_here
    slope = jnp.exp2(-8.0 * (my_head + 1).astype(F32) / HEADS) * (BIAS_SPAN / seq_len)

    plan = Plan(head_count, blk_count, sequences, tok_rows, heads_here)

    def units_turn(packed, kinds):
        packed = packed.reshape(blk_count, kinds, rel_part, tok_rows, HEAD_DIM)
        return lax.all_to_all(packed, "blk", 0, 0, tiled=True)

    hidden_one, qkv = project(plan, x_pieces, first_gain, first_shift, qkv_weight)
    g_all = gather_relative(after(g_own, hidden_one), "head", head_in)
    up_cols = columns(after(w_up, hidden_one)).reshape(head_count * d_part, f_here)
    received, g_all, up_cols = lax.optimization_barrier((units_turn(qkv, 3), g_all, up_cols))
    up_weight = lax.all_gather(up_cols, "blk", axis=0, tiled=False)
    up_weight = stacked_part(up_weight, 0, head_count * d_part)
    if parts == 1:
        tile = 2 * half_rows
        count = seq_len // tok_rows
        pieces = jnp.arange(count, dtype=jnp.int32)
        per_half = half_rows // tok_rows
        blocks = pieces // per_half
        slots = jnp.arange(flat_table.shape[0], dtype=jnp.int32)
        slot = jnp.sum(jnp.where(flat_table[None, :] == blocks[:, None], slots[None, :], 0), axis=1)
        head_src = (slot % 2) * per_half + pieces % per_half
        rel = ((head_o - head_src // head_in) % head_outer) * head_in + (head_i - head_src % head_in) % head_in
        sources = jnp.stack(
            [
                (slot // 2) * (3 * head_count) + rel,
                jnp.full((count,), head_count, jnp.int32),
                (slot // 2) * head_count + rel,
            ]
        )
        slope2 = (slope * LOG2E).reshape(1)
        attended_unit, *kept = unit_forward(received.reshape(-1, HEAD_DIM), sources, slope2, tile, tok_rows)
    else:
        rel_rows = rel_head.reshape(parts, 1, rel_part, 1) * tok_rows + jnp.arange(tok_rows, dtype=jnp.int32)
        rows_at = rel_rows + jnp.arange(blk_count, dtype=jnp.int32)[None, :, None, None] * cycle_rows
        block_ids = rows_at // half_rows
        slots = jnp.arange(flat_table.shape[0], dtype=jnp.int32)
        picked = jnp.sum(jnp.where(block_ids[..., None] == slots, flat_table, 0), axis=-1)
        places = (picked * half_rows + rows_at % half_rows).reshape(parts, -1)

        def whole_unit(own):
            whole = jnp.zeros((parts,) + own.shape, own.dtype)
            for n in range(parts):
                piece = shift(own, "blk", parts, 0, n)
                whole = lax.dynamic_update_index_in_dim(whole, piece, (part - n) % parts, 0)
            return whole.reshape(-1, HEAD_DIM)

        queries, own_keys, own_values = (received[:, n].reshape(-1, HEAD_DIM) for n in range(3))
        keys, values = whole_unit(own_keys), whole_unit(own_values)
        query_pos = lax.dynamic_index_in_dim(places, part, 0, keepdims=False)
        key_pos = places.reshape(-1)
        attended_unit, log_norm = general_forward(queries, keys, values, query_pos, key_pos, slope)
    attended = units_turn(attended_unit, 1).reshape(plan.packed(1))

    attended, keep, send = project_out(plan, attended, output_weight)
    came = shift(send, "head", 2, 0, -1)
    far = halves_far(halves_near(keep, came), "head")
    middle, hidden_two = second_norm(x_own, [keep, came, *far], second_gain, second_shift, [up_weight[0]])
    hidden_two = gather_pieces(hidden_two, "head", head_in)

    hidden_two, activated, grad_up_values, grad_up_bias, keep, send = feed_forward(
        plan, hidden_two, g_all, up_weight, up_bias, down_weight
    )
    grad_down = rows_dot(activated, g_all).astype(BF16).reshape(blk_count, f_part, width)
    came, grad_down = lax.optimization_barrier((shift(send, "head", 2, 0, -1), grad_down))
    near = halves_near(keep, came)
    near, grad_up_values = lax.optimization_barrier((near, grad_up_values))
    grad_up = rows_dot(hidden_two, grad_up_values).astype(BF16)
    grad_up = grad_up.reshape(head_count, blk_count, d_part, f_here)
    grad_down_far = scatter_far_first(grad_down, "blk", blk_in)
    grad_up_near = scatter_near(grad_up, "blk", blk_in, 1)

    grad_middle, grad_branch, grad_second_gain, grad_second_shift, grad_down_bias = second_norm_back(
        middle, g_own, [keep, came, *halves_far(near, "head")], second_gain, [grad_up]
    )
    grad_branch = gather_pieces(grad_branch, "head", head_in)
    grad_branch, grad_attended = project_out_back(plan, grad_branch, output_weight, [grad_up_near, grad_down_far])
    grad_output = rows_dot(attended, grad_branch).astype(BF16).reshape(blk_count, d_part, width)
    grad_output_near = scatter_near(grad_output, "blk", blk_in, 0)
    result = dot_stacked(after(activated, grad_branch), down_weight[0], f_part).astype(BF16)
    result = result.reshape(head_count // 2, 2, own_rows, width)
    result_keep, result_came = result[:, 0], shift(result[:, 1], "head", 2, 0, -1)
    result_near = halves_near(result_keep, result_came)
    grad_unit = units_turn(grad_attended, 1)
    grad_up_parts = far_parts(grad_up_near, "blk", blk_in, 1)
    if parts == 1:
        grad_qkv_unit = unit_backward(grad_unit.reshape(-1, HEAD_DIM), kept, sources, slope2, tile, tok_rows, [grad_output_near, *result_near])
    else:
        dq, dk, dv = general_backward(
            queries, keys, values, attended_unit, log_norm, grad_unit.reshape(-1, HEAD_DIM), query_pos, key_pos, slope
        )

        def own_part(grad):
            grad = grad.reshape(parts, -1, HEAD_DIM)
            total = 0.0
            for n in range(parts):
                piece = lax.dynamic_index_in_dim(grad, (part - n) % parts, 0, keepdims=False)
                total = total + shift(piece, "blk", parts, 0, -n).astype(F32)
            return total.astype(BF16)

        cut = (blk_count, rel_part, tok_rows, HEAD_DIM)
        grad_qkv_unit = jnp.stack([dq.reshape(cut), own_part(dk).reshape(cut), own_part(dv).reshape(cut)], axis=1)
    grad_qkv_unit, grad_up_parts = lax.optimization_barrier((grad_qkv_unit, grad_up_parts))
    grad_qkv = units_turn(grad_qkv_unit, 3).reshape(plan.packed(3))
    grad_up_cols = sum_slabs(grad_up_parts, "head", head_in, "sum_up")
    (grad_up_own,) = join_columns(exchange(grad_up_cols, "head", head_in), "head", head_in, 1, "join_up")
    grad_down_own = scatter_near_last(grad_down_far, "blk", blk_in)
    grad_output_own = scatter_far(grad_output_near, "blk", blk_in, 0)
    activations = middle + result_keep[0].astype(F32) + result_came[0].astype(F32) + down_bias
    activations = sum((f.astype(F32) for f in halves_far(result_near, "head")), activations)
    activations = activations.astype(BF16).reshape(tokens.shape)

    grad_qkv, keep, send = project_back(
        plan, grad_qkv, qkv_weight, [grad_up_own, grad_down_own, grad_output_own, activations]
    )
    grad_qkv_weight = rows_dot(hidden_one, grad_qkv).astype(BF16).reshape(head_count, blk_count, d_part, -1)
    came, grad_qkv_weight = lax.optimization_barrier((shift(send, "head", 2, 0, -1), grad_qkv_weight))
    grad_qkv_near = scatter_near(grad_qkv_weight, "blk", blk_in, 1)
    near = halves_near(keep, came)
    input_grad, grad_first_gain, grad_first_shift = first_norm_back(
        x_own, grad_middle, [keep, came, *halves_far(near, "head")], first_gain, []
    )
    input_grad, grad_qkv_near = lax.optimization_barrier((input_grad, grad_qkv_near))
    grad_qkv_parts = far_parts(grad_qkv_near, "blk", blk_in, 1)
    input_grad = input_grad.reshape(tokens.shape)

    mine = (jnp.arange(head_count) == head_at)[:, None]
    bias_terms = jnp.where(mine, grad_up_bias, 0.0).reshape(devices, f_part)
    terms = jnp.concatenate(
        [
            t.reshape(devices, d_part)
            for t in (grad_first_gain, grad_first_shift, grad_second_gain, grad_second_shift, grad_down_bias)
        ]
        + [bias_terms],
        axis=1,
    )
    terms = jnp.sum(lax.all_to_all(terms[:, None, :], everyone, 0, 0, tiled=True), axis=(0, 1))
    grad_qkv_cols = sum_slabs(after(grad_qkv_parts, terms), "head", head_in, "sum_qkv")
    grad_qkv_cols = exchange(grad_qkv_cols, "head", head_in)
    grad_query, grad_key, grad_value = join_columns(grad_qkv_cols, "head", head_in, 3, "join_qkv")
    g1, s1, g2, s2, bd = (terms[n * d_part : (n + 1) * d_part] for n in range(5))
    return (
        activations,
        input_grad,
        g1,
        s1,
        grad_query,
        grad_key,
        grad_value,
        grad_output_own,
        g2,
        s2,
        grad_up_own,
        terms[5 * d_part :],
        grad_down_own,
        bd,
    )


def solution(mesh):
    rows = P(None, "blk", "head", None)
    vector = P(("head", "blk"))
    matrix = P(("head", "blk"), None)
    params = (vector, vector, matrix, matrix, matrix, matrix, vector, vector, matrix, vector, matrix, vector)
    return jax.shard_map(
        body,
        mesh=mesh,
        in_specs=(rows, rows, P()) + params,
        out_specs=(rows, rows) + params,
        check_vma=False,
    )
```

```python
import functools
import itertools
import math

import jax
import jax.numpy as jnp
from jax import lax
from jax.experimental import pallas as pl
from jax.experimental.pallas import tpu as pltpu
from jax.sharding import PartitionSpec as P

HEADS = 8
HEAD_DIM = 128
BIAS_SPAN = 1024
EPSILON = 1e-05
NEG_LARGE = -1e30
LOG2E = 1.4426950408889634
VMEM_BYTES = 48 << 20
F32 = jnp.float32
BF16 = jnp.bfloat16
SMEM = pl.BlockSpec(memory_space=pltpu.SMEM)
VMEM = pl.BlockSpec(memory_space=pltpu.VMEM)
ANY = pl.BlockSpec(memory_space=pl.ANY)


def fixed(*shape):
    return pl.BlockSpec(shape, lambda n: (0,) * len(shape))


def swap(x, axis, bits):
    if not bits:
        return x
    return lax.ppermute(x, axis, [(n, n ^ bits) for n in range(lax.axis_size(axis))])


def bits_of(axis):
    top = lax.axis_size(axis).bit_length() - 1
    return [1 << n for n in reversed(range(top))]


def gather_pieces(x, axis, middle=()):
    pieces = {0: x}
    for bit in bits_of(axis):
        for n in list(pieces):
            pieces[n | bit] = swap(pieces[n], axis, bit)
        if middle:
            pieces, middle = after(pieces, middle), ()
    return [pieces[n] for n in range(lax.axis_size(axis))]


def gather_relative(x, axis):
    return jnp.concatenate(gather_pieces(x, axis), axis=0)


def relative(axis):
    return lax.axis_index(axis) ^ jnp.arange(lax.axis_size(axis), dtype=jnp.int32)


class Halving:
    def __init__(self, x, axis, dim, order):
        self.axis, self.dim, self.order = axis, dim, list(order)
        self.bits = bits_of(axis)
        self.x = x.reshape(x.shape[:dim] + (2,) * len(self.bits) + x.shape[dim + 1 :])
        self.whole = True
        self.first = self.order.pop(0)
        self.at = dim + self.bits.index(self.first)
        self.bits.remove(self.first)
        self.send = lax.dynamic_index_in_dim(self.x, 1 - self.mine(self.first), self.at, keepdims=False)
        self.came = swap(self.send, axis, self.first)

    def mine(self, bit):
        return (lax.axis_index(self.axis) // bit) % 2

    def fold(self, name, behind=()):
        bit = self.order.pop(0)
        there = self.dim + self.bits.index(bit)
        self.bits.remove(bit)
        whole, at = self.whole, self.at
        shape = self.came.shape
        left = shape[:there] + shape[there + 1 :]

        def kernel(numbers_ref, x_ref, came_ref, *refs):
            keep_ref, send_ref = refs[-2:]

            def value(where):
                own = where[:at] + (numbers_ref[0],) + where[at:] if whole else where
                return x_ref[own].astype(F32) + came_ref[where].astype(F32)

            for spot in itertools.product(*map(range, left[:-2])):
                keep_ref[spot] = value(spot[:there] + (numbers_ref[1],) + spot[there:])
                send_ref[spot] = value(spot[:there] + (1 - numbers_ref[1],) + spot[there:]).astype(BF16)

        arrays = [self.x, self.came]
        self.x, self.send = pl.pallas_call(
            kernel,
            grid=(1,),
            out_shape=(jax.ShapeDtypeStruct(left, F32), jax.ShapeDtypeStruct(left, BF16)),
            in_specs=[SMEM] + [fixed(*a.shape) for a in arrays] + [ANY] * len(behind),
            out_specs=(fixed(*left),) * 2,
            compiler_params=pltpu.CompilerParams(vmem_limit_bytes=VMEM_BYTES),
            cost_estimate=pl.CostEstimate(flops=0, bytes_accessed=4 << 20, transcendentals=0),
            name=name,
        )(jnp.stack([self.mine(self.first), self.mine(bit)]), *arrays, *behind)
        self.whole, self.first = False, bit
        self.came = swap(self.send, self.axis, bit)
        return self

    def fold_all(self, name, behind=()):
        while self.order:
            self.fold(name, behind)
        return self

    @property
    def terms(self):
        return [self.x, self.came]


def total(terms):
    return sum(t.astype(F32) for t in terms)


def copies_kernel(moves, count, numbers_ref, *refs):
    sems = refs[-1]
    started = []
    for n, (source, source_at, target, target_at) in enumerate(moves(numbers_ref)):
        from_ref, to_ref = refs[source], refs[count + target]
        move = pltpu.make_async_copy(from_ref.at[source_at], to_ref.at[target_at], sems.at[n])
        move.start()
        started.append(move)
    for move in started:
        move.wait()


def copy_blocks(arrays, numbers, shapes, moves, how_many, name):
    size = sum(math.prod(a.shape) for a in arrays) * 4
    return pl.pallas_call(
        functools.partial(copies_kernel, moves, len(arrays)),
        out_shape=tuple(jax.ShapeDtypeStruct(shape, arrays[0].dtype) for shape in shapes),
        in_specs=[SMEM] + [ANY] * len(arrays),
        out_specs=(VMEM,) * len(shapes),
        scratch_shapes=[pltpu.SemaphoreType.DMA((how_many,))],
        compiler_params=pltpu.CompilerParams(vmem_limit_bytes=VMEM_BYTES),
        cost_estimate=pl.CostEstimate(flops=0, bytes_accessed=size, transcendentals=0),
        name=name,
    )(numbers, *arrays)


def laid_by_devices(pieces, axes, name):
    count, stacked = len(pieces), pieces[0].shape[0]
    numbers = jnp.concatenate([relative(axis) for axis in axes])

    def moves(slots):
        return [
            (n, (r,), 0, (slots[r], slots[stacked + n])) for n in range(count) for r in range(stacked)
        ]

    shape = (stacked, count) + pieces[0].shape[1:]
    return copy_blocks(pieces, numbers, [shape], moves, count * stacked, name)[0]


def small_call(kernel, numbers, arrays, shapes, name):
    return pl.pallas_call(
        kernel,
        grid=(1,),
        out_shape=tuple(shapes),
        in_specs=[SMEM] + [fixed(*a.shape) for a in arrays],
        out_specs=tuple(fixed(*o.shape) for o in shapes),
        compiler_params=pltpu.CompilerParams(vmem_limit_bytes=VMEM_BYTES),
        cost_estimate=pl.CostEstimate(flops=0, bytes_accessed=1 << 20, transcendentals=0),
        name=name,
    )(numbers, *arrays)


def exchange(pieces, axis):
    return [swap(p, axis, n) for n, p in enumerate(pieces)]


def cut_columns(weights, axis, name):
    count, rows = lax.axis_size(axis), weights[0].shape[0]
    widths = [w.shape[1] // count for w in weights]

    def kernel(numbers_ref, *refs):
        for n in range(count):
            at = 0
            for ref, wide in zip(refs[: len(weights)], widths, strict=True):
                start = pl.multiple_of(numbers_ref[n] * wide, wide)
                refs[len(weights) + n][:, at : at + wide] = ref[:, pl.ds(start, wide)]
                at += wide

    shapes = [jax.ShapeDtypeStruct((rows, sum(widths)), BF16)] * count
    return small_call(kernel, relative(axis), weights, shapes, name)


def sum_slabs(groups, axis, name):
    count, rows, _ = groups[0][0].shape
    widths = [group[0].shape[2] for group in groups]
    arrays = [part for group in groups for part in group]

    def kernel(numbers_ref, *refs):
        for n in range(count):
            taken = at = 0
            for group, wide in zip(groups, widths, strict=True):
                slab = total([ref[numbers_ref[n]] for ref in refs[taken : taken + len(group)]])
                refs[len(arrays) + n][:, at : at + wide] = slab.astype(BF16)
                taken, at = taken + len(group), at + wide

    shapes = [jax.ShapeDtypeStruct((rows, sum(widths)), BF16)] * count
    return small_call(kernel, relative(axis), arrays, shapes, name)


def join_columns(pieces, axis, kinds, name):
    count = len(pieces)
    rows, wide = pieces[0].shape
    wide //= kinds

    def kernel(numbers_ref, *refs):
        for n in range(count):
            start = pl.multiple_of(numbers_ref[n] * wide, wide)
            for k in range(kinds):
                refs[count + k][:, pl.ds(start, wide)] = refs[n][:, k * wide : (k + 1) * wide].astype(F32)

    shapes = [jax.ShapeDtypeStruct((rows, wide * count), F32)] * kinds
    return small_call(kernel, relative(axis), pieces, shapes, name)


def after(value, *others):
    return lax.optimization_barrier((value, others))[0]


def halves_near(keep, came):
    return [total((keep[a], came[a])).astype(BF16) for a in range(1, keep.shape[0])]


def halves_far(near, axis):
    return [swap(n, axis, 2 + 2 * a) for a, n in enumerate(near)]


def norm_parts(values):
    center = values - jnp.mean(values, axis=-1, keepdims=True)
    spread = lax.rsqrt(jnp.mean(center * center, axis=-1, keepdims=True) + EPSILON)
    return (center * spread, spread)


def norm_back(grad_normed, normed, spread, gain):
    scaled = grad_normed * gain
    inner = (
        scaled
        - jnp.mean(scaled, axis=-1, keepdims=True)
        - normed * jnp.mean(scaled * normed, axis=-1, keepdims=True)
    )
    return (spread * inner, jnp.sum(grad_normed * normed, axis=0), jnp.sum(grad_normed, axis=0))


def plain_dot(left, right):
    return jnp.dot(left, right, preferred_element_type=F32)


def rows_dot(left, right):
    return lax.dot_general(left, right, (((0,), (0,)), ((), ())), preferred_element_type=F32)


def dot_stacked(left, right, rows):
    return plain_dot(left, right[:, :rows].reshape(-1, right.shape[2]))


def dot_trans(left, right):
    return lax.dot_general(left, right, (((1,), (1,)), ((), ())), preferred_element_type=F32)


def gelu_and_slope(u):
    k = math.sqrt(2.0 / math.pi)
    t = jnp.tanh(k * (u + 0.044715 * (u * u * u)))
    half = 0.5 * (1.0 + t)
    slope = half + 0.5 * u * (1.0 - t * t) * (k * (1.0 + 3 * 0.044715 * (u * u)))
    return u * half, slope


class Plan:
    def __init__(self, head_count, blk_count, sequences, tok_rows, heads_here):
        self.blocks, self.sequences, self.tok, self.heads = head_count, sequences, tok_rows, heads_here
        self.own = sequences * tok_rows
        self.units = sequences * heads_here
        self.parts = blk_count // self.units
        self.rel = head_count // self.parts

    def packed(self, kinds):
        return (self.units, self.parts, kinds, self.rel, self.tok, HEAD_DIM)

    def packed_spec(self, kinds):
        return pl.BlockSpec(
            (self.units, 1, kinds, 1, self.tok, HEAD_DIM), lambda n: (0, n // self.rel, 0, n % self.rel, 0, 0)
        )

    def rows_spec(self, width):
        return pl.BlockSpec((self.own, width), lambda n: (n, 0))

    def pick(self, refs):
        value = refs[0][...]
        for n in range(1, self.blocks):
            value = jnp.where(pl.program_id(0) == n, refs[n][...], value)
        return value

    def half_spec(self, width):
        return pl.BlockSpec((1, self.own, width), lambda n: (n // 2, 0, 0))

    def half(self, width):
        return jax.ShapeDtypeStruct((self.blocks // 2, self.own, width), BF16)

    def pack(self, out_ref, rows, kinds):
        for c in range(kinds):
            for e in range(self.heads):
                col = (c * self.heads + e) * HEAD_DIM
                for s in range(self.sequences):
                    cut = rows[s * self.tok : (s + 1) * self.tok, col : col + HEAD_DIM]
                    out_ref[s * self.heads + e, 0, c, 0] = cut

    def unpack(self, in_ref, rows_ref, kinds):
        for c in range(kinds):
            for e in range(self.heads):
                col = (c * self.heads + e) * HEAD_DIM
                for s in range(self.sequences):
                    cut = in_ref[s * self.heads + e, 0, c, 0]
                    rows_ref[s * self.tok : (s + 1) * self.tok, col : col + HEAD_DIM] = cut


def split_store(keep_ref, send_ref, value):
    odd = pl.program_id(0) % 2 == 1
    value = value.astype(BF16)

    @pl.when(jnp.logical_not(odd))
    def _():
        keep_ref[0] = value

    @pl.when(odd)
    def _():
        send_ref[0] = value


def stacked_part(joint, start, rows):
    count, _, width = joint.shape
    if start % rows or rows % 16:
        joint, start = joint[:, start : start + rows], 0
    at = start // rows
    return joint, pl.BlockSpec((count, rows, width), lambda n: (0, at, 0))


def big_call(kernel, plan, name, flops, out_shape, in_specs, out_specs, scratch=()):
    return pl.pallas_call(
        kernel,
        grid=(plan.blocks,),
        out_shape=out_shape,
        in_specs=in_specs,
        out_specs=out_specs,
        scratch_shapes=scratch,
        compiler_params=pltpu.CompilerParams(vmem_limit_bytes=VMEM_BYTES),
        cost_estimate=pl.CostEstimate(flops=flops, bytes_accessed=8 << 20, transcendentals=0),
        name=name,
    )


def project(plan, x, gain, shift_row, weight):
    width, kinds_width = weight.shape
    rows = plan.blocks * plan.own

    def kernel(*refs):
        x_refs, (gain_ref, shift_ref, w_ref, h_ref, out_ref) = refs[: plan.blocks], refs[plan.blocks :]
        normed, _ = norm_parts(plan.pick(x_refs).astype(F32))
        h = (normed * gain_ref[...] + shift_ref[...]).astype(BF16)
        h_ref[...] = h
        plan.pack(out_ref, plain_dot(h, w_ref[...]).astype(BF16), 3)

    return big_call(
        kernel,
        plan,
        "project",
        2 * rows * width * kinds_width,
        (jax.ShapeDtypeStruct((rows, width), BF16), jax.ShapeDtypeStruct(plan.packed(3), BF16)),
        [fixed(plan.own, width)] * plan.blocks + [fixed(1, width), fixed(1, width), fixed(width, kinds_width)],
        (plan.rows_spec(width), plan.packed_spec(3)),
    )(*x, gain, shift_row, weight)


def project_out(plan, received, weight):
    weight, w_spec = weight
    here, width = plan.heads * HEAD_DIM, weight.shape[2]

    def kernel(in_ref, w_ref, rows_ref, keep_ref, send_ref):
        plan.unpack(in_ref, rows_ref, 1)
        split_store(keep_ref, send_ref, plain_dot(rows_ref[...], w_ref[...].reshape(here, width)))

    rows = plan.blocks * plan.own
    return big_call(
        kernel,
        plan,
        "project_out",
        2 * rows * width * here,
        (jax.ShapeDtypeStruct((rows, here), BF16), plan.half(width), plan.half(width)),
        [plan.packed_spec(1), w_spec],
        (plan.rows_spec(here), plan.half_spec(width), plan.half_spec(width)),
    )(received, weight)


def project_out_back(plan, grad, weight, behind):
    weight, w_spec = weight
    here, width = plan.heads * HEAD_DIM, weight.shape[2]
    rows = plan.blocks * plan.own

    def kernel(*refs):
        in_refs, w_ref, (rows_ref, out_ref) = refs[: plan.blocks], refs[plan.blocks], refs[-2:]
        value = plan.pick(in_refs)
        rows_ref[...] = value
        plan.pack(out_ref, dot_trans(value, w_ref[...].reshape(here, width)).astype(BF16), 1)

    return big_call(
        kernel,
        plan,
        "project_out_back",
        2 * rows * width * here,
        (jax.ShapeDtypeStruct((rows, width), BF16), jax.ShapeDtypeStruct(plan.packed(1), BF16)),
        [fixed(plan.own, width)] * plan.blocks + [w_spec] + [ANY] * len(behind),
        (plan.rows_spec(width), plan.packed_spec(1)),
    )(*grad, weight, *behind)


def project_back(plan, received, weight, behind):
    width, here = weight.shape

    half = here // 2

    def kernel(in_ref, w_ref, *refs):
        left_ref, right_ref, keep_ref, send_ref, rows_ref = refs[-5:]
        plan.unpack(in_ref, rows_ref, 3)
        left_ref[...], right_ref[...] = rows_ref[:, :half], rows_ref[:, half:]
        split_store(keep_ref, send_ref, dot_trans(rows_ref[...], w_ref[...]))

    rows = plan.blocks * plan.own
    return big_call(
        kernel,
        plan,
        "project_back",
        2 * rows * width * here,
        (jax.ShapeDtypeStruct((rows, half), BF16),) * 2 + (plan.half(width),) * 2,
        [plan.packed_spec(3), fixed(width, here)] + [ANY] * len(behind),
        (plan.rows_spec(half),) * 2 + (plan.half_spec(width),) * 2,
        [pltpu.VMEM((plan.own, here), BF16)],
    )(received, weight, *behind)


def feed_forward(plan, hidden, grad, up_weight, up_bias, down_weight, head_slots):
    up_weight, up_spec = up_weight
    down_weight, down_spec = down_weight
    width, here = down_weight.shape[2], up_weight.shape[2]
    count, stacked = up_weight.shape[0], plan.blocks
    cut = width // (count * stacked)
    rows = plan.blocks * plan.own

    def kernel(slots_ref, *refs):
        h_refs, refs = refs[: plan.blocks], refs[plan.blocks :]
        g_ref, up_ref, bias_ref, down_ref, h_ref, act_ref, grad_ref, bias_grad_ref, keep_ref, send_ref, in_order = refs

        @pl.when(pl.program_id(0) == 0)
        def _():
            for b in range(count):
                for h in range(stacked):
                    in_order[slots_ref[h], b] = up_ref[b, h * cut : (h + 1) * cut, :]

        up_rows = in_order[...].reshape(width, here)
        value = plan.pick(h_refs)
        h_ref[...] = value
        act, slope = gelu_and_slope(plain_dot(value, up_rows) + bias_ref[...])
        act_ref[...] = act.astype(BF16)
        grad_up = (dot_trans(g_ref[...], down_ref[...].reshape(here, width)) * slope).astype(BF16)
        grad_ref[...] = grad_up
        sums = jnp.sum(grad_up.astype(F32), axis=0, keepdims=True)

        @pl.when(pl.program_id(0) == 0)
        def _():
            bias_grad_ref[...] = sums

        @pl.when(pl.program_id(0) > 0)
        def _():
            bias_grad_ref[...] += sums

        split_store(keep_ref, send_ref, dot_trans(grad_up, up_rows))

    return big_call(
        kernel,
        plan,
        "feed_forward",
        6 * rows * width * here,
        (
            jax.ShapeDtypeStruct((rows, width), BF16),
            jax.ShapeDtypeStruct((rows, here), BF16),
            jax.ShapeDtypeStruct((rows, here), BF16),
            jax.ShapeDtypeStruct((1, here), F32),
            plan.half(width),
            plan.half(width),
        ),
        [SMEM]
        + [fixed(plan.own, width)] * plan.blocks
        + [plan.rows_spec(width), up_spec, fixed(1, here), down_spec],
        (
            plan.rows_spec(width),
            plan.rows_spec(here),
            plan.rows_spec(here),
            fixed(1, here),
            plan.half_spec(width),
            plan.half_spec(width),
        ),
        [pltpu.VMEM((stacked, count, cut, here), BF16)],
    )(head_slots, *hidden, grad, up_weight, up_bias, down_weight)


def norm_call(kernel, arrays, behind, shapes, name):
    def body(*refs):
        kernel(refs[: len(arrays)], refs[len(arrays) + len(behind) :])

    return pl.pallas_call(
        body,
        grid=(1,),
        out_shape=tuple(shapes),
        in_specs=[fixed(*a.shape) for a in arrays] + [ANY] * len(behind),
        out_specs=tuple(fixed(*o.shape) for o in shapes),
        compiler_params=pltpu.CompilerParams(vmem_limit_bytes=VMEM_BYTES),
        cost_estimate=pl.CostEstimate(flops=10 << 20, bytes_accessed=4 << 20, transcendentals=0),
        name=name,
    )(*arrays, *behind)


def summed(refs):
    keep_ref, came_ref = refs[:2]
    total = keep_ref[0].astype(F32) + came_ref[0].astype(F32)
    for ref in refs[2:]:
        total = total + ref[...].astype(F32)
    return total


def second_norm(x, terms, gain, shift_row, behind):
    def kernel(ins, outs):
        middle = ins[0][...].astype(F32) + summed(ins[3:])
        normed, _ = norm_parts(middle)
        outs[0][...] = middle
        outs[1][...] = (normed * ins[1][...] + ins[2][...]).astype(BF16)

    shapes = [jax.ShapeDtypeStruct(x.shape, F32), jax.ShapeDtypeStruct(x.shape, BF16)]
    return norm_call(kernel, [x, gain, shift_row, *terms], behind, shapes, "second_norm")


def second_norm_back(middle, grad, terms, gain, behind):
    def kernel(ins, outs):
        normed, spread = norm_parts(ins[0][...])
        grad_out = ins[1][...].astype(F32)
        back, gain_sum, shift_sum = norm_back(summed(ins[3:]), normed, spread, ins[2][...])
        total = grad_out + back
        outs[0][...] = total
        outs[1][...] = total.astype(BF16)
        outs[2][...] = gain_sum[None]
        outs[3][...] = shift_sum[None]
        outs[4][...] = jnp.sum(grad_out, axis=0, keepdims=True)

    row = jax.ShapeDtypeStruct((1, grad.shape[1]), F32)
    shapes = [jax.ShapeDtypeStruct(grad.shape, F32), jax.ShapeDtypeStruct(grad.shape, BF16), row, row, row]
    return norm_call(kernel, [middle, grad, gain, *terms], behind, shapes, "second_norm_back")


def first_norm_back(x, grad, terms, gain, behind):
    def kernel(ins, outs):
        normed, spread = norm_parts(ins[0][...].astype(F32))
        back, gain_sum, shift_sum = norm_back(summed(ins[3:]), normed, spread, ins[2][...])
        outs[0][...] = (ins[1][...] + back).astype(BF16)
        outs[1][...] = gain_sum[None]
        outs[2][...] = shift_sum[None]

    row = jax.ShapeDtypeStruct((1, x.shape[1]), F32)
    return norm_call(kernel, [x, grad, gain, *terms], behind, [jax.ShapeDtypeStruct(x.shape, BF16), row, row], "first_norm_back")


def attend_forward_kernel(tile, piece, src_ref, slope_ref, recv_ref, out_ref, q_ref, k_ref, v_ref, o_ref, l_ref, vt_ref):
    pieces = q_ref.shape[0] // piece
    rel = recv_ref.shape[0] // piece // 3 // src_ref.shape[1]
    for t in range(pieces):
        for c, ref in enumerate((q_ref, k_ref, v_ref)):
            at = pl.multiple_of((src_ref[0, t] + c * src_ref[1, 0]) * piece, piece)
            ref[t * piece : (t + 1) * piece, :] = recv_ref[pl.ds(at, piece), :]
    tiles = q_ref.shape[0] // tile
    for j in range(tiles):
        rows = slice(j * tile, (j + 1) * tile)
        vt_ref[:, rows] = v_ref[rows, :].T
    slope = slope_ref[0]
    scale = LOG2E / math.sqrt(HEAD_DIM)
    for i in range(tiles):
        span = (i + 1) * tile
        scores = dot_trans(k_ref[0:span, :], q_ref[i * tile : span, :]) * scale
        key_at = lax.broadcasted_iota(jnp.int32, (span, tile), 0)
        scores = scores + slope * key_at.astype(F32)
        low = key_at[i * tile : span] - i * tile <= lax.broadcasted_iota(jnp.int32, (tile, tile), 1)
        last = jnp.where(low, scores[i * tile : span], NEG_LARGE)
        if i:
            scores = jnp.concatenate([scores[: i * tile], last], axis=0)
        else:
            scores = last
        top = jnp.max(scores, axis=0, keepdims=True)
        shifted = jnp.exp2(scores - top)
        total = jnp.sum(shifted, axis=0, keepdims=True)
        l_ref[i : i + 1, :] = top + jnp.log2(total)
        prob = (shifted * (1.0 / total)).astype(BF16)
        o_ref[i * tile : span, :] = plain_dot(vt_ref[:, 0:span], prob).T.astype(BF16)
    for t in range(pieces):
        at = pl.multiple_of(src_ref[2, t] * piece, piece)
        out_ref[pl.ds(at, piece), :] = o_ref[t * piece : (t + 1) * piece, :]


def attend_backward_kernel(tile, piece, src_ref, slope_ref, recv_ref, q_ref, k_ref, v_ref, o_ref, l_ref, *refs):
    out_ref, d_ref, kt_ref, dq_ref, dk_ref, dv_ref = refs[-6:]
    pieces = q_ref.shape[0] // piece
    for t in range(pieces):
        at = pl.multiple_of(src_ref[2, t] * piece, piece)
        d_ref[t * piece : (t + 1) * piece, :] = recv_ref[pl.ds(at, piece), :]
    tiles = q_ref.shape[0] // tile
    for j in range(tiles):
        rows = slice(j * tile, (j + 1) * tile)
        kt_ref[:, rows] = k_ref[rows, :].T
    slope = slope_ref[0]
    scale = LOG2E / math.sqrt(HEAD_DIM)
    for i in reversed(range(tiles)):
        span = (i + 1) * tile
        mine = slice(i * tile, span)
        queries, grads = q_ref[mine, :], d_ref[mine, :]
        row_dot = lax.dot_general(
            jnp.ones((8, HEAD_DIM), F32),
            grads.astype(F32) * o_ref[mine, :].astype(F32),
            (((1,), (1,)), ((), ())),
            precision=lax.Precision.HIGHEST,
            preferred_element_type=F32,
        )[0:1]
        scores = dot_trans(k_ref[0:span, :], queries) * scale
        key_at = lax.broadcasted_iota(jnp.int32, (span, tile), 0)
        scores = scores + slope * key_at.astype(F32)
        low = key_at[mine] - i * tile <= lax.broadcasted_iota(jnp.int32, (tile, tile), 1)
        last = jnp.where(low, scores[mine], NEG_LARGE)
        if i:
            scores = jnp.concatenate([scores[: i * tile], last], axis=0)
        else:
            scores = last
        prob = jnp.exp2(scores - l_ref[i : i + 1, :])
        grad_prob = dot_trans(v_ref[0:span, :], grads)
        grad_scores = (prob * (grad_prob - row_dot)).astype(BF16)
        dv = plain_dot(prob.astype(BF16), grads)
        dk = plain_dot(grad_scores, queries)
        if i == tiles - 1:
            dv_ref[...] = dv
            dk_ref[...] = dk
        else:
            dv_ref[0:span, :] += dv
            dk_ref[0:span, :] += dk
        dq_ref[mine, :] = plain_dot(kt_ref[:, 0:span], grad_scores).T
    for t in range(pieces):
        rows = slice(t * piece, (t + 1) * piece)
        for c, (ref, factor) in enumerate(
            ((dq_ref, 1.0 / math.sqrt(HEAD_DIM)), (dk_ref, 1.0 / math.sqrt(HEAD_DIM)), (dv_ref, 1.0))
        ):
            at = pl.multiple_of((src_ref[0, t] + c * src_ref[1, 0]) * piece, piece)
            out_ref[pl.ds(at, piece), :] = (ref[rows, :] * factor).astype(BF16)


def unit_forward(recv, sources, slope2, tile, piece):
    rows = recv.shape[0] // 3
    half = jax.ShapeDtypeStruct((rows, HEAD_DIM), BF16)
    area = rows * rows // 2 * HEAD_DIM
    return pl.pallas_call(
        functools.partial(attend_forward_kernel, tile, piece),
        grid=(1,),
        out_shape=(half,) * 5 + (jax.ShapeDtypeStruct((rows // tile, tile), F32),),
        in_specs=[SMEM, SMEM, fixed(*recv.shape)],
        out_specs=(fixed(rows, HEAD_DIM),) * 5 + (fixed(rows // tile, tile),),
        scratch_shapes=[pltpu.VMEM((HEAD_DIM, rows), BF16)],
        compiler_params=pltpu.CompilerParams(vmem_limit_bytes=VMEM_BYTES),
        cost_estimate=pl.CostEstimate(flops=4 * area, bytes_accessed=rows * 2048, transcendentals=rows * rows // 2),
        name="attend_forward",
    )(sources, slope2, recv)


def unit_backward(recv, kept, sources, slope2, tile, piece, behind):
    rows = recv.shape[0]
    area = rows * rows // 2 * HEAD_DIM
    return pl.pallas_call(
        functools.partial(attend_backward_kernel, tile, piece),
        grid=(1,),
        out_shape=jax.ShapeDtypeStruct((rows * 3, HEAD_DIM), BF16),
        in_specs=[SMEM, SMEM] + [fixed(*a.shape) for a in (recv, *kept)] + [ANY] * len(behind),
        out_specs=fixed(rows * 3, HEAD_DIM),
        scratch_shapes=[
            pltpu.VMEM((rows, HEAD_DIM), BF16),
            pltpu.VMEM((HEAD_DIM, rows), BF16),
            pltpu.VMEM((rows, HEAD_DIM), F32),
            pltpu.VMEM((rows, HEAD_DIM), F32),
            pltpu.VMEM((rows, HEAD_DIM), F32),
        ],
        compiler_params=pltpu.CompilerParams(vmem_limit_bytes=VMEM_BYTES),
        cost_estimate=pl.CostEstimate(flops=10 * area, bytes_accessed=rows * 2560, transcendentals=rows * rows // 2),
        name="attend_backward",
    )(sources, slope2, recv, *kept, *behind)


def general_scores(queries, keys, query_pos, key_pos, slope):
    scores = dot_trans(queries, keys) / math.sqrt(HEAD_DIM)
    distance = (query_pos[:, None] - key_pos[None, :]).astype(F32)
    allowed = key_pos[None, :] <= query_pos[:, None]
    return jnp.where(allowed, scores - slope * distance, NEG_LARGE), allowed


def general_forward(queries, keys, values, query_pos, key_pos, slope):
    count = queries.shape[0]
    span = math.gcd(keys.shape[0], 1024)

    def visit(n, state):
        top, total, weighted = state
        key_rows = lax.dynamic_slice_in_dim(keys, n * span, span, 0)
        value_rows = lax.dynamic_slice_in_dim(values, n * span, span, 0)
        place = lax.dynamic_slice_in_dim(key_pos, n * span, span, 0)
        scores, allowed = general_scores(queries, key_rows, query_pos, place, slope)
        new_top = jnp.maximum(top, jnp.max(scores, axis=-1, keepdims=True))
        fade = jnp.exp(top - new_top)
        shifted = jnp.where(allowed, jnp.exp(scores - new_top), 0.0)
        total = total * fade + jnp.sum(shifted, axis=-1, keepdims=True)
        return new_top, total, weighted * fade + plain_dot(shifted.astype(BF16), value_rows)

    start = (jnp.full((count, 1), NEG_LARGE, F32), jnp.zeros((count, 1), F32), jnp.zeros((count, HEAD_DIM), F32))
    top, total, weighted = lax.fori_loop(0, keys.shape[0] // span, visit, start)
    return (weighted / total).astype(BF16), top + jnp.log(total)


def general_backward(queries, keys, values, attended, log_norm, grads, query_pos, key_pos, slope):
    span = math.gcd(keys.shape[0], 1024)
    row_dot = jnp.sum(grads.astype(F32) * attended.astype(F32), axis=-1, keepdims=True)

    def visit(n, state):
        key_rows = lax.dynamic_slice_in_dim(keys, n * span, span, 0)
        value_rows = lax.dynamic_slice_in_dim(values, n * span, span, 0)
        place = lax.dynamic_slice_in_dim(key_pos, n * span, span, 0)
        scores, allowed = general_scores(queries, key_rows, query_pos, place, slope)
        prob = jnp.where(allowed, jnp.exp(scores - log_norm), 0.0)
        grad_scores = (prob * (dot_trans(grads, value_rows) - row_dot)).astype(BF16)
        dq = state[0] + plain_dot(grad_scores, key_rows)
        dk = lax.dynamic_update_slice_in_dim(state[1], rows_dot(grad_scores, queries), n * span, 0)
        dv = lax.dynamic_update_slice_in_dim(state[2], rows_dot(prob.astype(BF16), grads), n * span, 0)
        return dq, dk, dv

    start = (jnp.zeros(queries.shape, F32), jnp.zeros(keys.shape, F32), jnp.zeros(keys.shape, F32))
    dq, dk, dv = lax.fori_loop(0, keys.shape[0] // span, visit, start)
    scale = 1.0 / math.sqrt(HEAD_DIM)
    return (dq * scale).astype(BF16), (dk * scale).astype(BF16), dv.astype(BF16)


def body(
    tokens,
    cotangent,
    block_table,
    norm1_gain,
    norm1_bias,
    w_query,
    w_key,
    w_value,
    w_output,
    norm2_gain,
    norm2_bias,
    w_up,
    b_up,
    w_down,
    b_down,
):
    head_count, blk_count = lax.axis_size("head"), lax.axis_size("blk")
    devices = head_count * blk_count
    sequences, _, tok_rows, width = tokens.shape
    heads_here = HEADS // head_count
    cycle_rows = tok_rows * head_count
    half_rows = cycle_rows // 2
    seq_len = cycle_rows * blk_count
    own_rows = sequences * tok_rows
    d_part, f_part = width // devices, b_up.shape[0]
    hidden = f_part * devices
    f_here = hidden // head_count
    units = sequences * heads_here
    parts = blk_count // units
    rel_part = head_count // parts
    head_at, blk_at = lax.axis_index("head"), lax.axis_index("blk")
    head_slots = relative("head")
    everyone = ("head", "blk")

    x_own = tokens[:, 0].reshape(own_rows, width)
    g_own = cotangent[:, 0].reshape(own_rows, width)

    def turned_columns(weights, name):
        return jnp.stack(exchange(cut_columns(weights, "head", name), "head"))

    qkv_cols = turned_columns([w_query, w_key, w_value], "cut_qkv")
    qkv_pieces = gather_pieces(qkv_cols, "blk")
    direct = [qkv_pieces[bit] for bit in bits_of("blk")]
    second = [piece for n, piece in enumerate(qkv_pieces) if n.bit_count() == 2]
    x_pieces = gather_pieces(after(x_own, direct), "head", second)
    small = jnp.concatenate(
        [v.reshape(-1, d_part) for v in (norm1_gain, norm1_bias, norm2_gain, norm2_bias, b_down, b_up)], axis=0
    )
    small = after(small, direct)
    small = lax.all_to_all(
        jnp.broadcast_to(small, (devices,) + small.shape), everyone, 0, 0, tiled=True
    ).astype(F32)
    first_gain, first_shift, second_gain, second_shift, down_bias = (
        small[:, n].reshape(1, width) for n in range(5)
    )
    up_bias = lax.dynamic_index_in_dim(small[:, 5:].reshape(head_count, f_here), head_at, 0)
    qkv_pieces = after(qkv_pieces, x_pieces, first_gain, first_shift)
    qkv_weight = laid_by_devices(qkv_pieces, ("head", "blk"), "lay_qkv").reshape(width, -1)
    joint = after(jnp.concatenate([w_down, w_output], axis=0), qkv_pieces)
    joint = lax.all_gather(joint, "blk", axis=0, tiled=False)
    down_weight, output_weight = stacked_part(joint, 0, f_part), stacked_part(joint, f_part, d_part)

    flat_table = block_table.reshape(-1)
    head_ids = head_at * heads_here + jnp.arange(heads_here, dtype=jnp.int32)
    unit, part = blk_at // parts, blk_at % parts
    my_head = head_ids[0] + unit % heads_here
    slope = jnp.exp2(-8.0 * (my_head + 1).astype(F32) / HEADS) * (BIAS_SPAN / seq_len)

    plan = Plan(head_count, blk_count, sequences, tok_rows, heads_here)

    def units_turn(packed, kinds):
        packed = packed.reshape(blk_count, kinds, rel_part, tok_rows, HEAD_DIM)
        return lax.all_to_all(packed, "blk", 0, 0, tiled=True)

    hidden_one, qkv = project(plan, x_pieces, first_gain, first_shift, qkv_weight)
    g_all = gather_relative(after(g_own, hidden_one), "head")
    up_cols = turned_columns([after(w_up, hidden_one)], "cut_up").reshape(head_count * d_part, f_here)
    received, g_all, up_cols = lax.optimization_barrier((units_turn(qkv, 3), g_all, up_cols))
    up_weight = lax.all_gather(up_cols, "blk", axis=0, tiled=False)
    up_weight = stacked_part(up_weight, 0, head_count * d_part)
    if parts == 1:
        tile = 2 * half_rows
        count = seq_len // tok_rows
        pieces = jnp.arange(count, dtype=jnp.int32)
        per_half = half_rows // tok_rows
        blocks = pieces // per_half
        slots = jnp.arange(flat_table.shape[0], dtype=jnp.int32)
        slot = jnp.sum(jnp.where(flat_table[None, :] == blocks[:, None], slots[None, :], 0), axis=1)
        head_src = (slot % 2) * per_half + pieces % per_half
        rel = head_at ^ head_src
        sources = jnp.stack(
            [
                (slot // 2) * (3 * head_count) + rel,
                jnp.full((count,), head_count, jnp.int32),
                (slot // 2) * head_count + rel,
            ]
        )
        slope2 = (slope * LOG2E).reshape(1)
        attended_unit, *kept = unit_forward(received.reshape(-1, HEAD_DIM), sources, slope2, tile, tok_rows)
    else:
        rel_rows = head_slots.reshape(parts, 1, rel_part, 1) * tok_rows + jnp.arange(tok_rows, dtype=jnp.int32)
        rows_at = rel_rows + jnp.arange(blk_count, dtype=jnp.int32)[None, :, None, None] * cycle_rows
        block_ids = rows_at // half_rows
        slots = jnp.arange(flat_table.shape[0], dtype=jnp.int32)
        picked = jnp.sum(jnp.where(block_ids[..., None] == slots, flat_table, 0), axis=-1)
        places = (picked * half_rows + rows_at % half_rows).reshape(parts, -1)

        def whole_unit(own):
            whole = jnp.zeros((parts,) + own.shape, own.dtype)
            for n in range(parts):
                whole = lax.dynamic_update_index_in_dim(whole, swap(own, "blk", n), part ^ n, 0)
            return whole.reshape(-1, HEAD_DIM)

        queries, own_keys, own_values = (received[:, n].reshape(-1, HEAD_DIM) for n in range(3))
        keys, values = whole_unit(own_keys), whole_unit(own_values)
        query_pos = lax.dynamic_index_in_dim(places, part, 0, keepdims=False)
        key_pos = places.reshape(-1)
        attended_unit, log_norm = general_forward(queries, keys, values, query_pos, key_pos, slope)
    attended = units_turn(attended_unit, 1).reshape(plan.packed(1))

    attended, keep, send = project_out(plan, attended, output_weight)
    came = swap(send, "head", 1)
    far = halves_far(halves_near(keep, came), "head")
    middle, hidden_two = second_norm(x_own, [keep, came, *far], second_gain, second_shift, [up_weight[0]])
    hidden_two = gather_pieces(hidden_two, "head")

    hidden_two, activated, grad_up_values, grad_up_bias, keep, send = feed_forward(
        plan, hidden_two, g_all, up_weight, up_bias, down_weight, head_slots
    )
    grad_up = rows_dot(hidden_two, grad_up_values).astype(BF16).reshape(head_count, blk_count, d_part, f_here)
    came, grad_up = lax.optimization_barrier((swap(send, "head", 1), grad_up))
    near = halves_near(keep, came)
    near, activated = lax.optimization_barrier((near, activated))
    grad_down = rows_dot(activated, g_all).astype(BF16).reshape(blk_count, f_part, width)
    order = bits_of("blk")[::-1]
    grad_down_sum = Halving(grad_down, "blk", 0, order)
    cross = [order[1], order[0], *order[2:]]
    grad_up_sum = Halving(grad_up, "blk", 1, cross)

    grad_middle, grad_branch, grad_second_gain, grad_second_shift, grad_down_bias = second_norm_back(
        middle, g_own, [keep, came, *halves_far(near, "head")], second_gain, [grad_down_sum.send, grad_up_sum.send]
    )
    mine = (jnp.arange(head_count) == head_at)[:, None]
    early = [grad_second_gain, grad_second_shift, grad_down_bias, jnp.where(mine, grad_up_bias, 0.0)]
    early = jnp.concatenate([v.reshape(devices, 1, -1) for v in early], axis=2)
    result = dot_stacked(after(activated, grad_branch), down_weight[0], f_part).astype(BF16)
    result = result.reshape(head_count // 2, 2, own_rows, width)
    result_keep, result_send = result[:, 0], result[:, 1]
    grad_branch = gather_pieces(grad_branch, "head")
    grad_down_sum.fold("fold_down")
    grad_up_sum.fold("fold_up")
    grad_branch, grad_attended = project_out_back(plan, grad_branch, output_weight, [grad_down_sum.send, grad_up_sum.send, early, result_send])
    grad_output = rows_dot(attended, grad_branch).astype(BF16).reshape(blk_count, d_part, width)
    grad_output_sum = Halving(grad_output, "blk", 0, order)
    grad_output_sum.fold("fold_output", [grad_attended])
    grad_down_sum.fold("fold_down", [grad_attended])
    grad_up_sum.fold("fold_up", [grad_attended])
    result_came = swap(result_send, "head", 1)
    result_near = halves_near(result_keep, result_came)
    grad_unit = units_turn(grad_attended, 1)
    if parts == 1:
        behind = [grad_down_sum.send, grad_up_sum.send, grad_output_sum.send, *result_near]
        grad_unit = grad_unit.reshape(-1, HEAD_DIM)
        grad_qkv_unit = unit_backward(grad_unit, kept, sources, slope2, tile, tok_rows, behind)
    else:
        dq, dk, dv = general_backward(
            queries, keys, values, attended_unit, log_norm, grad_unit.reshape(-1, HEAD_DIM), query_pos, key_pos, slope
        )

        def own_part(grad):
            grad = grad.reshape(parts, -1, HEAD_DIM)
            terms = []
            for n in range(parts):
                piece = lax.dynamic_index_in_dim(grad, part ^ n, 0, keepdims=False)
                terms.append(swap(piece, "blk", n))
            return total(terms).astype(BF16)

        cut = (blk_count, rel_part, tok_rows, HEAD_DIM)
        grad_qkv_unit = jnp.stack([dq.reshape(cut), own_part(dk).reshape(cut), own_part(dv).reshape(cut)], axis=1)
    behind = [grad_qkv_unit]
    grad_down_sum.fold_all("fold_down", behind)
    grad_output_sum.fold_all("fold_output", behind)
    grad_up_sum.fold_all("fold_up", behind)
    result_far = halves_far(result_near, "head")
    last = (grad_qkv_unit, grad_down_sum.terms, grad_output_sum.terms[0], grad_up_sum.terms, result_far)
    grad_qkv_unit, down_terms, output_kept, up_terms, result_far = lax.optimization_barrier(last)
    grad_qkv = units_turn(grad_qkv_unit, 3).reshape(plan.packed(3))
    grad_down_own = total(down_terms)
    activations = total([middle, result_keep[0], result_came[0], *result_far]) + down_bias
    activations = activations.astype(BF16).reshape(tokens.shape)

    left, right, keep, send = project_back(
        plan, grad_qkv, qkv_weight, [grad_down_own, activations]
    )
    grad_output_own = total([output_kept, grad_output_sum.came])
    up_cols = sum_slabs([after(up_terms, send)], "head", "sum_up")
    (grad_up_own,) = join_columns(exchange(up_cols, "head"), "head", 1, "join_up")
    left = rows_dot(hidden_one, left).astype(BF16).reshape(head_count, blk_count, d_part, -1)
    came, left = lax.optimization_barrier((swap(send, "head", 1), left))
    near = halves_near(keep, came)
    near, right = lax.optimization_barrier((near, right))
    right = rows_dot(hidden_one, right).astype(BF16).reshape(head_count, blk_count, d_part, -1)
    left_sum = Halving(left, "blk", 1, order)
    right_sum = Halving(right, "blk", 1, cross)
    input_grad, grad_first_gain, grad_first_shift = first_norm_back(
        x_own, grad_middle, [keep, came, *halves_far(near, "head")], first_gain, [left_sum.send, right_sum.send]
    )
    left_sum.fold("fold_left").fold_all("fold_left", [input_grad])
    right_sum.fold("fold_right").fold_all("fold_right", [input_grad])
    input_grad = input_grad.reshape(tokens.shape)
    terms = [early] + [v.reshape(devices, 1, d_part) for v in (grad_first_gain, grad_first_shift)]
    terms = lax.all_to_all(jnp.concatenate(terms, axis=2), everyone, 0, 0, tiled=True)
    terms = jnp.sum(terms, axis=(0, 1))
    g2, s2, bd = (terms[n * d_part : (n + 1) * d_part] for n in range(3))
    up_bias_grad = terms[3 * d_part : 3 * d_part + f_part]
    g1, s1 = terms[3 * d_part + f_part : 4 * d_part + f_part], terms[4 * d_part + f_part :]
    qkv_cols = sum_slabs([after(left_sum.terms, terms), right_sum.terms], "head", "sum_qkv")
    grad_query, grad_key, grad_value = join_columns(exchange(qkv_cols, "head"), "head", 3, "join_qkv")
    return (
        activations,
        input_grad,
        g1,
        s1,
        grad_query,
        grad_key,
        grad_value,
        grad_output_own,
        g2,
        s2,
        grad_up_own,
        up_bias_grad,
        grad_down_own,
        bd,
    )


def solution(mesh):
    rows = P(None, "blk", "head", None)
    vector = P(("head", "blk"))
    matrix = P(("head", "blk"), None)
    params = (vector, vector, matrix, matrix, matrix, matrix, vector, vector, matrix, vector, matrix, vector)
    return jax.shard_map(
        body,
        mesh=mesh,
        in_specs=(rows, rows, P()) + params,
        out_specs=(rows, rows) + params,
        check_vma=False,
    )
```

```python
import functools
import itertools
import math

import jax
import jax.numpy as jnp
from jax import lax
from jax.experimental import pallas as pl
from jax.experimental.pallas import tpu as pltpu
from jax.sharding import PartitionSpec as P

HEADS = 8
HEAD_DIM = 128
BIAS_SPAN = 1024
EPSILON = 1e-05
NEG_LARGE = -1e30
LOG2E = 1.4426950408889634
VMEM_BYTES = 48 << 20
F32 = jnp.float32
BF16 = jnp.bfloat16
SMEM = pl.BlockSpec(memory_space=pltpu.SMEM)
VMEM = pl.BlockSpec(memory_space=pltpu.VMEM)
ANY = pl.BlockSpec(memory_space=pl.ANY)


def fixed(*shape):
    return pl.BlockSpec(shape, lambda n: (0,) * len(shape))


def swap(x, axis, bits):
    if not bits:
        return x
    return lax.ppermute(x, axis, [(n, n ^ bits) for n in range(lax.axis_size(axis))])


def bits_of(axis):
    top = lax.axis_size(axis).bit_length() - 1
    return [1 << n for n in reversed(range(top))]


def gather_pieces(x, axis, middle=()):
    pieces = {0: x}
    for bit in bits_of(axis):
        for n in list(pieces):
            pieces[n | bit] = swap(pieces[n], axis, bit)
        if middle:
            pieces, middle = after(pieces, middle), ()
    return [pieces[n] for n in range(lax.axis_size(axis))]


def gather_relative(x, axis):
    return jnp.concatenate(gather_pieces(x, axis), axis=0)


def gather_rest(first, axis):
    pieces = {0: first[0], lax.axis_size(axis) // 2: first[1]}
    for bit in bits_of(axis)[1:]:
        for n in list(pieces):
            pieces[n | bit] = swap(pieces[n], axis, bit)
    return [pieces[n] for n in range(lax.axis_size(axis))]


def relative(axis):
    return lax.axis_index(axis) ^ jnp.arange(lax.axis_size(axis), dtype=jnp.int32)


class Halving:
    def __init__(self, x, axis, dim, order):
        self.axis, self.dim, self.order = axis, dim, list(order)
        self.bits = bits_of(axis)
        self.x = x.reshape(x.shape[:dim] + (2,) * len(self.bits) + x.shape[dim + 1 :])
        self.whole = True
        self.first = self.order.pop(0)
        self.at = dim + self.bits.index(self.first)
        self.bits.remove(self.first)
        self.send = lax.dynamic_index_in_dim(self.x, 1 - self.mine(self.first), self.at, keepdims=False)
        self.came = swap(self.send, axis, self.first)

    def mine(self, bit):
        return (lax.axis_index(self.axis) // bit) % 2

    def fold(self, name, behind=()):
        bit = self.order.pop(0)
        there = self.dim + self.bits.index(bit)
        self.bits.remove(bit)
        whole, at = self.whole, self.at
        shape = self.came.shape
        left = shape[:there] + shape[there + 1 :]

        def kernel(numbers_ref, x_ref, came_ref, *refs):
            keep_ref, send_ref = refs[-2:]

            def value(where):
                own = where[:at] + (numbers_ref[0],) + where[at:] if whole else where
                return x_ref[own].astype(F32) + came_ref[where].astype(F32)

            for spot in itertools.product(*map(range, left[:-2])):
                keep_ref[spot] = value(spot[:there] + (numbers_ref[1],) + spot[there:])
                send_ref[spot] = value(spot[:there] + (1 - numbers_ref[1],) + spot[there:]).astype(BF16)

        arrays = [self.x, self.came]
        self.x, self.send = pl.pallas_call(
            kernel,
            grid=(1,),
            out_shape=(jax.ShapeDtypeStruct(left, F32), jax.ShapeDtypeStruct(left, BF16)),
            in_specs=[SMEM] + [fixed(*a.shape) for a in arrays] + [ANY] * len(behind),
            out_specs=(fixed(*left),) * 2,
            compiler_params=pltpu.CompilerParams(vmem_limit_bytes=VMEM_BYTES),
            cost_estimate=pl.CostEstimate(flops=0, bytes_accessed=4 << 20, transcendentals=0),
            name=name,
        )(jnp.stack([self.mine(self.first), self.mine(bit)]), *arrays, *behind)
        self.whole, self.first = False, bit
        self.came = swap(self.send, self.axis, bit)
        return self

    def fold_all(self, name, behind=()):
        while self.order:
            self.fold(name, behind)
        return self

    @property
    def terms(self):
        return [self.x, self.came]


def total(terms):
    return sum(t.astype(F32) for t in terms)


def copies_kernel(moves, count, numbers_ref, *refs):
    sems = refs[-1]
    started = []
    for n, (source, source_at, target, target_at) in enumerate(moves(numbers_ref)):
        from_ref, to_ref = refs[source], refs[count + target]
        move = pltpu.make_async_copy(from_ref.at[source_at], to_ref.at[target_at], sems.at[n])
        move.start()
        started.append(move)
    for move in started:
        move.wait()


def copy_blocks(arrays, numbers, shapes, moves, how_many, name):
    size = sum(math.prod(a.shape) for a in arrays) * 4
    return pl.pallas_call(
        functools.partial(copies_kernel, moves, len(arrays)),
        out_shape=tuple(jax.ShapeDtypeStruct(shape, arrays[0].dtype) for shape in shapes),
        in_specs=[SMEM] + [ANY] * len(arrays),
        out_specs=(VMEM,) * len(shapes),
        scratch_shapes=[pltpu.SemaphoreType.DMA((how_many,))],
        compiler_params=pltpu.CompilerParams(vmem_limit_bytes=VMEM_BYTES),
        cost_estimate=pl.CostEstimate(flops=0, bytes_accessed=size, transcendentals=0),
        name=name,
    )(numbers, *arrays)


def laid_by_devices(pieces, axes, name):
    count, stacked = len(pieces), pieces[0].shape[0]
    numbers = jnp.concatenate([relative(axis) for axis in axes])

    def moves(slots):
        return [
            (n, (r,), 0, (slots[r], slots[stacked + n])) for n in range(count) for r in range(stacked)
        ]

    shape = (stacked, count) + pieces[0].shape[1:]
    return copy_blocks(pieces, numbers, [shape], moves, count * stacked, name)[0]


def small_call(kernel, numbers, arrays, shapes, name):
    return pl.pallas_call(
        kernel,
        grid=(1,),
        out_shape=tuple(shapes),
        in_specs=[SMEM] + [fixed(*a.shape) for a in arrays],
        out_specs=tuple(fixed(*o.shape) for o in shapes),
        compiler_params=pltpu.CompilerParams(vmem_limit_bytes=VMEM_BYTES),
        cost_estimate=pl.CostEstimate(flops=0, bytes_accessed=1 << 20, transcendentals=0),
        name=name,
    )(numbers, *arrays)


def exchange(pieces, axis):
    return [swap(p, axis, n) for n, p in enumerate(pieces)]


def cut_columns(weights, axis, name):
    count, rows = lax.axis_size(axis), weights[0].shape[0]
    widths = [w.shape[1] // count for w in weights]

    def kernel(numbers_ref, *refs):
        for n in range(count):
            at = 0
            for ref, wide in zip(refs[: len(weights)], widths, strict=True):
                start = pl.multiple_of(numbers_ref[n] * wide, wide)
                refs[len(weights) + n][:, at : at + wide] = ref[:, pl.ds(start, wide)]
                at += wide

    shapes = [jax.ShapeDtypeStruct((rows, sum(widths)), BF16)] * count
    return small_call(kernel, relative(axis), weights, shapes, name)


def sum_slabs(groups, axis, name):
    count, rows, _ = groups[0][0].shape
    widths = [group[0].shape[2] for group in groups]
    arrays = [part for group in groups for part in group]

    def kernel(numbers_ref, *refs):
        for n in range(count):
            taken = at = 0
            for group, wide in zip(groups, widths, strict=True):
                slab = total([ref[numbers_ref[n]] for ref in refs[taken : taken + len(group)]])
                refs[len(arrays) + n][:, at : at + wide] = slab.astype(BF16)
                taken, at = taken + len(group), at + wide

    shapes = [jax.ShapeDtypeStruct((rows, sum(widths)), BF16)] * count
    return small_call(kernel, relative(axis), arrays, shapes, name)


def join_columns(pieces, axis, kinds, name):
    count = len(pieces)
    rows, wide = pieces[0].shape
    wide //= kinds

    def kernel(numbers_ref, *refs):
        for n in range(count):
            start = pl.multiple_of(numbers_ref[n] * wide, wide)
            for k in range(kinds):
                refs[count + k][:, pl.ds(start, wide)] = refs[n][:, k * wide : (k + 1) * wide].astype(F32)

    shapes = [jax.ShapeDtypeStruct((rows, wide * count), F32)] * kinds
    return small_call(kernel, relative(axis), pieces, shapes, name)


def after(value, *others):
    return lax.optimization_barrier((value, others))[0]


def halves_near(keep, came):
    return [total(pair).astype(BF16) for pair in list(zip(keep, came, strict=True))[1:]]


def halves_far(near, axis):
    return [swap(n, axis, 2 + 2 * a) for a, n in enumerate(near)]


def norm_parts(values):
    center = values - jnp.mean(values, axis=-1, keepdims=True)
    spread = lax.rsqrt(jnp.mean(center * center, axis=-1, keepdims=True) + EPSILON)
    return (center * spread, spread)


def norm_back(grad_normed, normed, spread, gain):
    scaled = grad_normed * gain
    inner = (
        scaled
        - jnp.mean(scaled, axis=-1, keepdims=True)
        - normed * jnp.mean(scaled * normed, axis=-1, keepdims=True)
    )
    return (spread * inner, jnp.sum(grad_normed * normed, axis=0), jnp.sum(grad_normed, axis=0))


def plain_dot(left, right):
    return jnp.dot(left, right, preferred_element_type=F32)


def rows_dot(left, right):
    return lax.dot_general(left, right, (((0,), (0,)), ((), ())), preferred_element_type=F32)


def dot_stacked(left, right, rows):
    return plain_dot(left, right[:, :rows].reshape(-1, right.shape[2]))


def dot_trans(left, right):
    return lax.dot_general(left, right, (((1,), (1,)), ((), ())), preferred_element_type=F32)


def gelu_and_slope(u):
    k = math.sqrt(2.0 / math.pi)
    t = jnp.tanh(k * (u + 0.044715 * (u * u * u)))
    half = 0.5 * (1.0 + t)
    slope = half + 0.5 * u * (1.0 - t * t) * (k * (1.0 + 3 * 0.044715 * (u * u)))
    return u * half, slope


class Plan:
    def __init__(self, head_count, blk_count, sequences, tok_rows, heads_here, d_part):
        self.d_part = d_part
        self.blocks, self.sequences, self.tok, self.heads = head_count, sequences, tok_rows, heads_here
        self.own = sequences * tok_rows
        self.units = sequences * heads_here
        self.parts = blk_count // self.units
        self.rel = head_count // self.parts

    def packed(self, kinds):
        return (self.units, self.parts, kinds, self.rel, self.tok, HEAD_DIM)

    def packed_spec(self, kinds):
        return pl.BlockSpec(
            (self.units, 1, kinds, 1, self.tok, HEAD_DIM), lambda n: (0, n // self.rel, 0, n % self.rel, 0, 0)
        )

    def rows_spec(self, width):
        return pl.BlockSpec((self.own, width), lambda n: (n, 0))

    def pick(self, refs):
        value = refs[0][...]
        for n in range(1, self.blocks):
            value = jnp.where(pl.program_id(0) == n, refs[n][...], value)
        return value

    def half_spec(self, width):
        return pl.BlockSpec((1, self.own, width), lambda n: (n // 2, 0, 0))

    def half(self, width):
        return jax.ShapeDtypeStruct((self.blocks // 2, self.own, width), BF16)

    def pack(self, out_ref, rows, kinds):
        for c in range(kinds):
            for e in range(self.heads):
                col = (c * self.heads + e) * HEAD_DIM
                for s in range(self.sequences):
                    cut = rows[s * self.tok : (s + 1) * self.tok, col : col + HEAD_DIM]
                    out_ref[s * self.heads + e, 0, c, 0] = cut

    def unpack(self, in_ref, rows_ref, kinds):
        for c in range(kinds):
            for e in range(self.heads):
                col = (c * self.heads + e) * HEAD_DIM
                for s in range(self.sequences):
                    cut = in_ref[s * self.heads + e, 0, c, 0]
                    rows_ref[s * self.tok : (s + 1) * self.tok, col : col + HEAD_DIM] = cut


def split_store(keep_ref, send_ref, value):
    odd = pl.program_id(0) % 2 == 1
    value = value.astype(BF16)

    @pl.when(jnp.logical_not(odd))
    def _():
        keep_ref[0] = value

    @pl.when(odd)
    def _():
        send_ref[0] = value


def stacked_part(joint, start, rows):
    count, _, width = joint.shape
    if start % rows or rows % 16:
        joint, start = joint[:, start : start + rows], 0
    at = start // rows
    return joint, pl.BlockSpec((count, rows, width), lambda n: (0, at, 0))


def big_call(kernel, plan, name, flops, out_shape, in_specs, out_specs, scratch=()):
    return pl.pallas_call(
        kernel,
        grid=(plan.blocks,),
        out_shape=out_shape,
        in_specs=in_specs,
        out_specs=out_specs,
        scratch_shapes=scratch,
        compiler_params=pltpu.CompilerParams(vmem_limit_bytes=VMEM_BYTES),
        cost_estimate=pl.CostEstimate(flops=flops, bytes_accessed=8 << 20, transcendentals=0),
        name=name,
    )


def project(plan, x, gain, shift_row, weight):
    width, kinds_width = weight.shape
    rows = plan.blocks * plan.own

    def kernel(*refs):
        x_refs, (gain_ref, shift_ref, w_ref, h_ref, out_ref) = refs[: plan.blocks], refs[plan.blocks :]
        normed, _ = norm_parts(plan.pick(x_refs).astype(F32))
        h = (normed * gain_ref[...] + shift_ref[...]).astype(BF16)
        h_ref[...] = h
        plan.pack(out_ref, plain_dot(h, w_ref[...]).astype(BF16), 3)

    return big_call(
        kernel,
        plan,
        "project",
        2 * rows * width * kinds_width,
        (jax.ShapeDtypeStruct((rows, width), BF16), jax.ShapeDtypeStruct(plan.packed(3), BF16)),
        [fixed(plan.own, width)] * plan.blocks + [fixed(1, width), fixed(1, width), fixed(width, kinds_width)],
        (plan.rows_spec(width), plan.packed_spec(3)),
    )(*x, gain, shift_row, weight)


def project_out(plan, received, weight):
    weight, w_spec = weight
    here, width = plan.heads * HEAD_DIM, weight.shape[2]

    def kernel(in_ref, w_ref, rows_ref, keep_ref, send_ref):
        plan.unpack(in_ref, rows_ref, 1)
        split_store(keep_ref, send_ref, plain_dot(rows_ref[...], w_ref[...].reshape(here, width)))

    rows = plan.blocks * plan.own
    return big_call(
        kernel,
        plan,
        "project_out",
        2 * rows * width * here,
        (jax.ShapeDtypeStruct((rows, here), BF16), plan.half(width), plan.half(width)),
        [plan.packed_spec(1), w_spec],
        (plan.rows_spec(here), plan.half_spec(width), plan.half_spec(width)),
    )(received, weight)


def project_out_back(plan, grad, weight, behind):
    weight, w_spec = weight
    here, width = plan.heads * HEAD_DIM, weight.shape[2]
    rows = plan.blocks * plan.own

    def kernel(*refs):
        in_refs, w_ref, (rows_ref, out_ref) = refs[: plan.blocks], refs[plan.blocks], refs[-2:]
        value = plan.pick(in_refs)
        rows_ref[...] = value
        plan.pack(out_ref, dot_trans(value, w_ref[...].reshape(here, width)).astype(BF16), 1)

    return big_call(
        kernel,
        plan,
        "project_out_back",
        2 * rows * width * here,
        (jax.ShapeDtypeStruct((rows, width), BF16), jax.ShapeDtypeStruct(plan.packed(1), BF16)),
        [fixed(plan.own, width)] * plan.blocks + [w_spec] + [ANY] * len(behind),
        (plan.rows_spec(width), plan.packed_spec(1)),
    )(*grad, weight, *behind)


def project_back(plan, received, weight, behind):
    width, here = weight.shape

    half = here // 2

    def kernel(in_ref, w_ref, *refs):
        left_ref, right_ref, keep_ref, send_ref, rows_ref = refs[-5:]
        plan.unpack(in_ref, rows_ref, 3)
        left_ref[...], right_ref[...] = rows_ref[:, :half], rows_ref[:, half:]
        split_store(keep_ref, send_ref, dot_trans(rows_ref[...], w_ref[...]))

    rows = plan.blocks * plan.own
    return big_call(
        kernel,
        plan,
        "project_back",
        2 * rows * width * here,
        (jax.ShapeDtypeStruct((rows, half), BF16),) * 2 + (plan.half(width),) * 2,
        [plan.packed_spec(3), fixed(width, here)] + [ANY] * len(behind),
        (plan.rows_spec(half),) * 2 + (plan.half_spec(width),) * 2,
        [pltpu.VMEM((plan.own, here), BF16)],
    )(received, weight, *behind)


def feed_forward(plan, hidden, grad_act, up_weight, up_bias, head_slots, before=None):
    half = plan.blocks // 2
    first = before is None
    width, here = plan.blocks * plan.parts * plan.units * plan.d_part, up_bias.shape[1]
    rows = plan.blocks * plan.own
    base = 0 if first else 1
    count = 0 if not first else up_weight[0].shape[0]
    cut = plan.d_part

    def kernel(*refs):
        if first:
            slots_ref, refs = refs[0], refs[1:]
        h_refs, (grad_ref, up_ref, bias_ref, bias_before_ref) = refs[:half], refs[half : half + 4]
        outs = refs[-7:] if first else refs[-6:]
        h_ref, act_ref, out_ref, bias_grad_ref, keep_ref, send_ref = outs[:6]
        value = jnp.concatenate([ref[...] for ref in h_refs], axis=0)
        if first:
            in_order = outs[6]
            for b in range(count):
                for h in range(plan.blocks):
                    in_order[slots_ref[h], b] = up_ref[b, h * cut : (h + 1) * cut, :]
            up_rows = in_order[...].reshape(width, here)
        else:
            up_rows = up_ref[...].reshape(width, here)
        h_ref[...] = value
        act, slope = gelu_and_slope(plain_dot(value, up_rows) + bias_ref[...])
        act_ref[...] = act.astype(BF16)
        grad_up = (grad_ref[...].astype(F32) * slope).astype(BF16)
        out_ref[...] = grad_up
        bias_grad_ref[...] = bias_before_ref[...] + jnp.sum(grad_up.astype(F32), axis=0, keepdims=True)
        back = dot_trans(grad_up, up_rows).astype(BF16).reshape(half, plan.own, width)
        for n in range(half):
            (send_ref if n % 2 else keep_ref)[n // 2] = back[n]

    def rows_spec(wide):
        return pl.BlockSpec((half * plan.own, wide), lambda n: (base, 0))

    part = jax.ShapeDtypeStruct((half // 2, plan.own, width), BF16)
    shapes = [jax.ShapeDtypeStruct((rows, wide), BF16) for wide in (width, here, here)]
    shapes += [jax.ShapeDtypeStruct((1, here), F32), part, part]
    specs = [rows_spec(width), rows_spec(here), rows_spec(here), fixed(1, here)] + [fixed(*part.shape)] * 2
    if first:
        turned = (plan.blocks, count, cut, here)
        shapes.append(jax.ShapeDtypeStruct(turned, BF16))
        specs.append(fixed(*turned))
        arrays = [head_slots, *hidden, grad_act, up_weight[0], up_bias, jnp.zeros((1, here), F32)]
        in_specs = [SMEM] + [fixed(plan.own, width)] * half + [rows_spec(here), up_weight[1]] + [fixed(1, here)] * 2
        aliases = {}
    else:
        arrays = [*hidden, grad_act, before[6], up_bias, before[3], *before[:3]]
        in_specs = [fixed(plan.own, width)] * half + [rows_spec(here), fixed(*before[6].shape)]
        in_specs += [fixed(1, here)] * 2 + [ANY] * 3
        aliases = {half + 4 + n: n for n in range(3)}
    return pl.pallas_call(
        kernel,
        grid=(1,),
        out_shape=tuple(shapes),
        in_specs=in_specs,
        out_specs=tuple(specs),
        input_output_aliases=aliases,
        compiler_params=pltpu.CompilerParams(vmem_limit_bytes=VMEM_BYTES),
        cost_estimate=pl.CostEstimate(flops=2 * rows * width * here, bytes_accessed=6 << 20, transcendentals=0),
        name="feed_forward",
    )(*arrays)


def norm_call(kernel, arrays, behind, shapes, name):
    def body(*refs):
        kernel(refs[: len(arrays)], refs[len(arrays) + len(behind) :])

    return pl.pallas_call(
        body,
        grid=(1,),
        out_shape=tuple(shapes),
        in_specs=[fixed(*a.shape) for a in arrays] + [ANY] * len(behind),
        out_specs=tuple(fixed(*o.shape) for o in shapes),
        compiler_params=pltpu.CompilerParams(vmem_limit_bytes=VMEM_BYTES),
        cost_estimate=pl.CostEstimate(flops=10 << 20, bytes_accessed=4 << 20, transcendentals=0),
        name=name,
    )(*arrays, *behind)


def summed(refs):
    keep_ref, came_ref = refs[:2]
    total = keep_ref[0].astype(F32) + came_ref[0].astype(F32)
    for ref in refs[2:]:
        total = total + ref[...].astype(F32)
    return total


def second_norm(x, terms, gain, shift_row, behind):
    def kernel(ins, outs):
        middle = ins[0][...].astype(F32) + summed(ins[3:])
        normed, _ = norm_parts(middle)
        outs[0][...] = middle
        outs[1][...] = (normed * ins[1][...] + ins[2][...]).astype(BF16)

    shapes = [jax.ShapeDtypeStruct(x.shape, F32), jax.ShapeDtypeStruct(x.shape, BF16)]
    return norm_call(kernel, [x, gain, shift_row, *terms], behind, shapes, "second_norm")


def second_norm_back(middle, grad, terms, gain, behind):
    def kernel(ins, outs):
        normed, spread = norm_parts(ins[0][...])
        grad_out = ins[1][...].astype(F32)
        back, gain_sum, shift_sum = norm_back(summed(ins[3:]), normed, spread, ins[2][...])
        total = grad_out + back
        outs[0][...] = total
        outs[1][...] = total.astype(BF16)
        outs[2][...] = gain_sum[None]
        outs[3][...] = shift_sum[None]
        outs[4][...] = jnp.sum(grad_out, axis=0, keepdims=True)

    row = jax.ShapeDtypeStruct((1, grad.shape[1]), F32)
    shapes = [jax.ShapeDtypeStruct(grad.shape, F32), jax.ShapeDtypeStruct(grad.shape, BF16), row, row, row]
    return norm_call(kernel, [middle, grad, gain, *terms], behind, shapes, "second_norm_back")


def first_norm_back(x, grad, terms, gain, behind):
    def kernel(ins, outs):
        normed, spread = norm_parts(ins[0][...].astype(F32))
        back, gain_sum, shift_sum = norm_back(summed(ins[3:]), normed, spread, ins[2][...])
        outs[0][...] = (ins[1][...] + back).astype(BF16)
        outs[1][...] = gain_sum[None]
        outs[2][...] = shift_sum[None]

    row = jax.ShapeDtypeStruct((1, x.shape[1]), F32)
    return norm_call(kernel, [x, grad, gain, *terms], behind, [jax.ShapeDtypeStruct(x.shape, BF16), row, row], "first_norm_back")


def attend_forward_kernel(tile, piece, src_ref, slope_ref, recv_ref, out_ref, q_ref, k_ref, v_ref, o_ref, l_ref, vt_ref):
    pieces = q_ref.shape[0] // piece
    rel = recv_ref.shape[0] // piece // 3 // src_ref.shape[1]
    for t in range(pieces):
        for c, ref in enumerate((q_ref, k_ref, v_ref)):
            at = pl.multiple_of((src_ref[0, t] + c * src_ref[1, 0]) * piece, piece)
            ref[t * piece : (t + 1) * piece, :] = recv_ref[pl.ds(at, piece), :]
    tiles = q_ref.shape[0] // tile
    for j in range(tiles):
        rows = slice(j * tile, (j + 1) * tile)
        vt_ref[:, rows] = v_ref[rows, :].T
    slope = slope_ref[0]
    scale = LOG2E / math.sqrt(HEAD_DIM)
    for i in range(tiles):
        span = (i + 1) * tile
        scores = dot_trans(k_ref[0:span, :], q_ref[i * tile : span, :]) * scale
        key_at = lax.broadcasted_iota(jnp.int32, (span, tile), 0)
        scores = scores + slope * key_at.astype(F32)
        low = key_at[i * tile : span] - i * tile <= lax.broadcasted_iota(jnp.int32, (tile, tile), 1)
        last = jnp.where(low, scores[i * tile : span], NEG_LARGE)
        if i:
            scores = jnp.concatenate([scores[: i * tile], last], axis=0)
        else:
            scores = last
        top = jnp.max(scores, axis=0, keepdims=True)
        shifted = jnp.exp2(scores - top)
        total = jnp.sum(shifted, axis=0, keepdims=True)
        l_ref[i : i + 1, :] = top + jnp.log2(total)
        prob = (shifted * (1.0 / total)).astype(BF16)
        o_ref[i * tile : span, :] = plain_dot(vt_ref[:, 0:span], prob).T.astype(BF16)
    for t in range(pieces):
        at = pl.multiple_of(src_ref[2, t] * piece, piece)
        out_ref[pl.ds(at, piece), :] = o_ref[t * piece : (t + 1) * piece, :]


def attend_backward_kernel(tile, piece, src_ref, slope_ref, recv_ref, q_ref, k_ref, v_ref, o_ref, l_ref, *refs):
    out_ref, d_ref, kt_ref, dq_ref, dk_ref, dv_ref = refs[-6:]
    pieces = q_ref.shape[0] // piece
    for t in range(pieces):
        at = pl.multiple_of(src_ref[2, t] * piece, piece)
        d_ref[t * piece : (t + 1) * piece, :] = recv_ref[pl.ds(at, piece), :]
    tiles = q_ref.shape[0] // tile
    for j in range(tiles):
        rows = slice(j * tile, (j + 1) * tile)
        kt_ref[:, rows] = k_ref[rows, :].T
    slope = slope_ref[0]
    scale = LOG2E / math.sqrt(HEAD_DIM)
    for i in reversed(range(tiles)):
        span = (i + 1) * tile
        mine = slice(i * tile, span)
        queries, grads = q_ref[mine, :], d_ref[mine, :]
        row_dot = lax.dot_general(
            jnp.ones((8, HEAD_DIM), F32),
            grads.astype(F32) * o_ref[mine, :].astype(F32),
            (((1,), (1,)), ((), ())),
            precision=lax.Precision.HIGHEST,
            preferred_element_type=F32,
        )[0:1]
        scores = dot_trans(k_ref[0:span, :], queries) * scale
        key_at = lax.broadcasted_iota(jnp.int32, (span, tile), 0)
        scores = scores + slope * key_at.astype(F32)
        low = key_at[mine] - i * tile <= lax.broadcasted_iota(jnp.int32, (tile, tile), 1)
        last = jnp.where(low, scores[mine], NEG_LARGE)
        if i:
            scores = jnp.concatenate([scores[: i * tile], last], axis=0)
        else:
            scores = last
        prob = jnp.exp2(scores - l_ref[i : i + 1, :])
        grad_prob = dot_trans(v_ref[0:span, :], grads)
        grad_scores = (prob * (grad_prob - row_dot)).astype(BF16)
        dv = plain_dot(prob.astype(BF16), grads)
        dk = plain_dot(grad_scores, queries)
        if i == tiles - 1:
            dv_ref[...] = dv
            dk_ref[...] = dk
        else:
            dv_ref[0:span, :] += dv
            dk_ref[0:span, :] += dk
        dq_ref[mine, :] = plain_dot(kt_ref[:, 0:span], grad_scores).T
    for t in range(pieces):
        rows = slice(t * piece, (t + 1) * piece)
        for c, (ref, factor) in enumerate(
            ((dq_ref, 1.0 / math.sqrt(HEAD_DIM)), (dk_ref, 1.0 / math.sqrt(HEAD_DIM)), (dv_ref, 1.0))
        ):
            at = pl.multiple_of((src_ref[0, t] + c * src_ref[1, 0]) * piece, piece)
            out_ref[pl.ds(at, piece), :] = (ref[rows, :] * factor).astype(BF16)


def unit_forward(recv, sources, slope2, tile, piece):
    rows = recv.shape[0] // 3
    half = jax.ShapeDtypeStruct((rows, HEAD_DIM), BF16)
    area = rows * rows // 2 * HEAD_DIM
    return pl.pallas_call(
        functools.partial(attend_forward_kernel, tile, piece),
        grid=(1,),
        out_shape=(half,) * 5 + (jax.ShapeDtypeStruct((rows // tile, tile), F32),),
        in_specs=[SMEM, SMEM, fixed(*recv.shape)],
        out_specs=(fixed(rows, HEAD_DIM),) * 5 + (fixed(rows // tile, tile),),
        scratch_shapes=[pltpu.VMEM((HEAD_DIM, rows), BF16)],
        compiler_params=pltpu.CompilerParams(vmem_limit_bytes=VMEM_BYTES),
        cost_estimate=pl.CostEstimate(flops=4 * area, bytes_accessed=rows * 2048, transcendentals=rows * rows // 2),
        name="attend_forward",
    )(sources, slope2, recv)


def unit_backward(recv, kept, sources, slope2, tile, piece, behind):
    rows = recv.shape[0]
    area = rows * rows // 2 * HEAD_DIM
    return pl.pallas_call(
        functools.partial(attend_backward_kernel, tile, piece),
        grid=(1,),
        out_shape=jax.ShapeDtypeStruct((rows * 3, HEAD_DIM), BF16),
        in_specs=[SMEM, SMEM] + [fixed(*a.shape) for a in (recv, *kept)] + [ANY] * len(behind),
        out_specs=fixed(rows * 3, HEAD_DIM),
        scratch_shapes=[
            pltpu.VMEM((rows, HEAD_DIM), BF16),
            pltpu.VMEM((HEAD_DIM, rows), BF16),
            pltpu.VMEM((rows, HEAD_DIM), F32),
            pltpu.VMEM((rows, HEAD_DIM), F32),
            pltpu.VMEM((rows, HEAD_DIM), F32),
        ],
        compiler_params=pltpu.CompilerParams(vmem_limit_bytes=VMEM_BYTES),
        cost_estimate=pl.CostEstimate(flops=10 * area, bytes_accessed=rows * 2560, transcendentals=rows * rows // 2),
        name="attend_backward",
    )(sources, slope2, recv, *kept, *behind)


def general_scores(queries, keys, query_pos, key_pos, slope):
    scores = dot_trans(queries, keys) / math.sqrt(HEAD_DIM)
    distance = (query_pos[:, None] - key_pos[None, :]).astype(F32)
    allowed = key_pos[None, :] <= query_pos[:, None]
    return jnp.where(allowed, scores - slope * distance, NEG_LARGE), allowed


def general_forward(queries, keys, values, query_pos, key_pos, slope):
    count = queries.shape[0]
    span = math.gcd(keys.shape[0], 1024)

    def visit(n, state):
        top, total, weighted = state
        key_rows = lax.dynamic_slice_in_dim(keys, n * span, span, 0)
        value_rows = lax.dynamic_slice_in_dim(values, n * span, span, 0)
        place = lax.dynamic_slice_in_dim(key_pos, n * span, span, 0)
        scores, allowed = general_scores(queries, key_rows, query_pos, place, slope)
        new_top = jnp.maximum(top, jnp.max(scores, axis=-1, keepdims=True))
        fade = jnp.exp(top - new_top)
        shifted = jnp.where(allowed, jnp.exp(scores - new_top), 0.0)
        total = total * fade + jnp.sum(shifted, axis=-1, keepdims=True)
        return new_top, total, weighted * fade + plain_dot(shifted.astype(BF16), value_rows)

    start = (jnp.full((count, 1), NEG_LARGE, F32), jnp.zeros((count, 1), F32), jnp.zeros((count, HEAD_DIM), F32))
    top, total, weighted = lax.fori_loop(0, keys.shape[0] // span, visit, start)
    return (weighted / total).astype(BF16), top + jnp.log(total)


def general_backward(queries, keys, values, attended, log_norm, grads, query_pos, key_pos, slope):
    span = math.gcd(keys.shape[0], 1024)
    row_dot = jnp.sum(grads.astype(F32) * attended.astype(F32), axis=-1, keepdims=True)

    def visit(n, state):
        key_rows = lax.dynamic_slice_in_dim(keys, n * span, span, 0)
        value_rows = lax.dynamic_slice_in_dim(values, n * span, span, 0)
        place = lax.dynamic_slice_in_dim(key_pos, n * span, span, 0)
        scores, allowed = general_scores(queries, key_rows, query_pos, place, slope)
        prob = jnp.where(allowed, jnp.exp(scores - log_norm), 0.0)
        grad_scores = (prob * (dot_trans(grads, value_rows) - row_dot)).astype(BF16)
        dq = state[0] + plain_dot(grad_scores, key_rows)
        dk = lax.dynamic_update_slice_in_dim(state[1], rows_dot(grad_scores, queries), n * span, 0)
        dv = lax.dynamic_update_slice_in_dim(state[2], rows_dot(prob.astype(BF16), grads), n * span, 0)
        return dq, dk, dv

    start = (jnp.zeros(queries.shape, F32), jnp.zeros(keys.shape, F32), jnp.zeros(keys.shape, F32))
    dq, dk, dv = lax.fori_loop(0, keys.shape[0] // span, visit, start)
    scale = 1.0 / math.sqrt(HEAD_DIM)
    return (dq * scale).astype(BF16), (dk * scale).astype(BF16), dv.astype(BF16)


def body(
    tokens,
    cotangent,
    block_table,
    norm1_gain,
    norm1_bias,
    w_query,
    w_key,
    w_value,
    w_output,
    norm2_gain,
    norm2_bias,
    w_up,
    b_up,
    w_down,
    b_down,
):
    head_count, blk_count = lax.axis_size("head"), lax.axis_size("blk")
    devices = head_count * blk_count
    sequences, _, tok_rows, width = tokens.shape
    heads_here = HEADS // head_count
    cycle_rows = tok_rows * head_count
    half_rows = cycle_rows // 2
    seq_len = cycle_rows * blk_count
    own_rows = sequences * tok_rows
    d_part, f_part = width // devices, b_up.shape[0]
    hidden = f_part * devices
    f_here = hidden // head_count
    units = sequences * heads_here
    parts = blk_count // units
    rel_part = head_count // parts
    head_at, blk_at = lax.axis_index("head"), lax.axis_index("blk")
    head_slots = relative("head")
    everyone = ("head", "blk")

    x_own = tokens[:, 0].reshape(own_rows, width)
    g_own = cotangent[:, 0].reshape(own_rows, width)

    def turned_columns(weights, name):
        return jnp.stack(exchange(cut_columns(weights, "head", name), "head"))

    qkv_cols = turned_columns([w_query, w_key, w_value], "cut_qkv")
    qkv_pieces = gather_pieces(qkv_cols, "blk")
    direct = [qkv_pieces[bit] for bit in bits_of("blk")]
    small = jnp.concatenate(
        [v.reshape(-1, d_part) for v in (norm1_gain, norm1_bias, norm2_gain, norm2_bias, b_down, b_up)], axis=0
    )
    small = after(small, direct)
    small = lax.all_to_all(
        jnp.broadcast_to(small, (devices,) + small.shape), everyone, 0, 0, tiled=True
    ).astype(F32)
    second = [piece for n, piece in enumerate(qkv_pieces) if n.bit_count() == 2]
    x_pieces = gather_pieces(after(x_own, direct), "head", [second, small])
    first_gain, first_shift, second_gain, second_shift, down_bias = (
        small[:, n].reshape(1, width) for n in range(5)
    )
    up_bias = lax.dynamic_index_in_dim(small[:, 5:].reshape(head_count, f_here), head_at, 0)
    qkv_pieces = after(qkv_pieces, x_pieces, first_gain, first_shift)
    qkv_weight = laid_by_devices(qkv_pieces, ("head", "blk"), "lay_qkv").reshape(width, -1)
    joint = after(jnp.concatenate([w_down, w_output], axis=0), qkv_pieces)
    joint = lax.all_gather(joint, "blk", axis=0, tiled=False)
    down_weight, output_weight = stacked_part(joint, 0, f_part), stacked_part(joint, f_part, d_part)

    flat_table = block_table.reshape(-1)
    head_ids = head_at * heads_here + jnp.arange(heads_here, dtype=jnp.int32)
    unit, part = blk_at // parts, blk_at % parts
    my_head = head_ids[0] + unit % heads_here
    slope = jnp.exp2(-8.0 * (my_head + 1).astype(F32) / HEADS) * (BIAS_SPAN / seq_len)

    plan = Plan(head_count, blk_count, sequences, tok_rows, heads_here, d_part)

    def units_turn(packed, kinds):
        packed = packed.reshape(blk_count, kinds, rel_part, tok_rows, HEAD_DIM)
        return lax.all_to_all(packed, "blk", 0, 0, tiled=True)

    hidden_one, qkv = project(plan, x_pieces, first_gain, first_shift, qkv_weight)
    g_all = gather_relative(after(g_own, hidden_one), "head")
    up_cols = turned_columns([after(w_up, hidden_one)], "cut_up").reshape(head_count * d_part, f_here)
    received, g_all, up_cols = lax.optimization_barrier((units_turn(qkv, 3), g_all, up_cols))
    up_weight = lax.all_gather(up_cols, "blk", axis=0, tiled=False)
    up_weight = stacked_part(up_weight, 0, head_count * d_part)
    if parts == 1:
        tile = 2 * half_rows
        count = seq_len // tok_rows
        pieces = jnp.arange(count, dtype=jnp.int32)
        per_half = half_rows // tok_rows
        blocks = pieces // per_half
        slots = jnp.arange(flat_table.shape[0], dtype=jnp.int32)
        slot = jnp.sum(jnp.where(flat_table[None, :] == blocks[:, None], slots[None, :], 0), axis=1)
        head_src = (slot % 2) * per_half + pieces % per_half
        rel = head_at ^ head_src
        sources = jnp.stack(
            [
                (slot // 2) * (3 * head_count) + rel,
                jnp.full((count,), head_count, jnp.int32),
                (slot // 2) * head_count + rel,
            ]
        )
        slope2 = (slope * LOG2E).reshape(1)
        attended_unit, *kept = unit_forward(received.reshape(-1, HEAD_DIM), sources, slope2, tile, tok_rows)
    else:
        rel_rows = head_slots.reshape(parts, 1, rel_part, 1) * tok_rows + jnp.arange(tok_rows, dtype=jnp.int32)
        rows_at = rel_rows + jnp.arange(blk_count, dtype=jnp.int32)[None, :, None, None] * cycle_rows
        block_ids = rows_at // half_rows
        slots = jnp.arange(flat_table.shape[0], dtype=jnp.int32)
        picked = jnp.sum(jnp.where(block_ids[..., None] == slots, flat_table, 0), axis=-1)
        places = (picked * half_rows + rows_at % half_rows).reshape(parts, -1)

        def whole_unit(own):
            whole = jnp.zeros((parts,) + own.shape, own.dtype)
            for n in range(parts):
                whole = lax.dynamic_update_index_in_dim(whole, swap(own, "blk", n), part ^ n, 0)
            return whole.reshape(-1, HEAD_DIM)

        queries, own_keys, own_values = (received[:, n].reshape(-1, HEAD_DIM) for n in range(3))
        keys, values = whole_unit(own_keys), whole_unit(own_values)
        query_pos = lax.dynamic_index_in_dim(places, part, 0, keepdims=False)
        key_pos = places.reshape(-1)
        attended_unit, log_norm = general_forward(queries, keys, values, query_pos, key_pos, slope)
    grad_act = dot_trans(g_all, down_weight[0][:, :f_part].reshape(f_here, width)).astype(BF16)
    attended, grad_act = lax.optimization_barrier((units_turn(attended_unit, 1).reshape(plan.packed(1)), grad_act))

    attended, keep, send = project_out(plan, attended, output_weight)
    came = swap(send, "head", 1)
    far = halves_far(halves_near(keep, came), "head")
    middle, hidden_two = second_norm(x_own, [keep, came, *far], second_gain, second_shift, [up_weight[0]])
    near_two = {0: hidden_two}
    for bit in bits_of("head")[1:]:
        for n in list(near_two):
            near_two[n | bit] = swap(near_two[n], "head", bit)
    half = head_count // 2
    near_two = [near_two[n] for n in range(half)]

    done = feed_forward(plan, near_two, grad_act, up_weight, up_bias, head_slots)
    keep, came = done[4], swap(done[5], "head", 1)
    hidden_far = after(swap(hidden_two, "head", half), done[4])
    hidden_two = gather_rest([hidden_two, hidden_far], "head")
    done = feed_forward(plan, hidden_two[half:], grad_act, None, up_bias, None, done)
    hidden_two, activated, grad_up_values, grad_up_bias, keep_far, send = done
    grad_up = rows_dot(hidden_two, grad_up_values).astype(BF16).reshape(head_count, blk_count, d_part, f_here)
    came_far, grad_up = lax.optimization_barrier((swap(send, "head", 1), grad_up))
    near = halves_near([*keep, *keep_far], [*came, *came_far])
    near, activated = lax.optimization_barrier((near, activated))
    grad_down = rows_dot(activated, g_all).astype(BF16).reshape(blk_count, f_part, width)
    order = bits_of("blk")[::-1]
    grad_down_sum = Halving(grad_down, "blk", 0, order)
    cross = [order[1], order[0], *order[2:]]
    grad_up_sum = Halving(grad_up, "blk", 1, cross)

    grad_middle, grad_branch, grad_second_gain, grad_second_shift, grad_down_bias = second_norm_back(
        middle, g_own, [keep, came, *halves_far(near, "head")], second_gain, [grad_down_sum.send, grad_up_sum.send]
    )
    mine = (jnp.arange(head_count) == head_at)[:, None]
    early = [grad_second_gain, grad_second_shift, grad_down_bias, jnp.where(mine, grad_up_bias, 0.0)]
    early = jnp.concatenate([v.reshape(devices, 1, -1) for v in early], axis=2)
    result = dot_stacked(after(activated, grad_branch), down_weight[0], f_part).astype(BF16)
    result = result.reshape(head_count // 2, 2, own_rows, width)
    result_keep, result_send = result[:, 0], result[:, 1]
    grad_branch = gather_pieces(grad_branch, "head")
    grad_down_sum.fold("fold_down")
    grad_up_sum.fold("fold_up")
    grad_branch, grad_attended = project_out_back(plan, grad_branch, output_weight, [grad_down_sum.send, grad_up_sum.send, early, result_send])
    grad_output = rows_dot(attended, grad_branch).astype(BF16).reshape(blk_count, d_part, width)
    grad_output_sum = Halving(grad_output, "blk", 0, order)
    grad_output_sum.fold("fold_output", [grad_attended])
    grad_down_sum.fold("fold_down", [grad_attended])
    grad_up_sum.fold("fold_up", [grad_attended])
    result_came = swap(result_send, "head", 1)
    result_near = halves_near(result_keep, result_came)
    grad_unit = units_turn(grad_attended, 1)
    if parts == 1:
        behind = [grad_down_sum.send, grad_up_sum.send, grad_output_sum.send, *result_near]
        grad_unit = grad_unit.reshape(-1, HEAD_DIM)
        grad_qkv_unit = unit_backward(grad_unit, kept, sources, slope2, tile, tok_rows, behind)
    else:
        dq, dk, dv = general_backward(
            queries, keys, values, attended_unit, log_norm, grad_unit.reshape(-1, HEAD_DIM), query_pos, key_pos, slope
        )

        def own_part(grad):
            grad = grad.reshape(parts, -1, HEAD_DIM)
            terms = []
            for n in range(parts):
                piece = lax.dynamic_index_in_dim(grad, part ^ n, 0, keepdims=False)
                terms.append(swap(piece, "blk", n))
            return total(terms).astype(BF16)

        cut = (blk_count, rel_part, tok_rows, HEAD_DIM)
        grad_qkv_unit = jnp.stack([dq.reshape(cut), own_part(dk).reshape(cut), own_part(dv).reshape(cut)], axis=1)
    behind = [grad_qkv_unit]
    grad_down_sum.fold_all("fold_down", behind)
    grad_output_sum.fold_all("fold_output", behind)
    grad_up_sum.fold_all("fold_up", behind)
    result_far = halves_far(result_near, "head")
    last = (grad_qkv_unit, grad_down_sum.terms, grad_output_sum.terms[0], grad_up_sum.terms, result_far)
    grad_qkv_unit, down_terms, output_kept, up_terms, result_far = lax.optimization_barrier(last)
    grad_qkv = units_turn(grad_qkv_unit, 3).reshape(plan.packed(3))
    grad_down_own = total(down_terms)
    activations = total([middle, result_keep[0], result_came[0], *result_far]) + down_bias
    activations = activations.astype(BF16).reshape(tokens.shape)

    left, right, keep, send = project_back(
        plan, grad_qkv, qkv_weight, [grad_down_own, activations]
    )
    grad_output_own = total([output_kept, grad_output_sum.came])
    left = rows_dot(hidden_one, left).astype(BF16).reshape(head_count, blk_count, d_part, -1)
    came, left = lax.optimization_barrier((swap(send, "head", 1), left))
    near = halves_near(keep, came)
    near, right = lax.optimization_barrier((near, right))
    right = rows_dot(hidden_one, right).astype(BF16).reshape(head_count, blk_count, d_part, -1)
    left_sum = Halving(left, "blk", 1, order)
    right_sum = Halving(right, "blk", 1, cross)
    input_grad, grad_first_gain, grad_first_shift = first_norm_back(
        x_own, grad_middle, [keep, came, *halves_far(near, "head")], first_gain, [left_sum.send, right_sum.send]
    )
    left_sum.fold("fold_left").fold_all("fold_left", [input_grad])
    right_sum.fold("fold_right").fold_all("fold_right", [input_grad])
    input_grad = input_grad.reshape(tokens.shape)
    terms = [early] + [v.reshape(devices, 1, d_part) for v in (grad_first_gain, grad_first_shift)]
    last = (jnp.concatenate(terms, axis=2), up_terms, left_sum.send, right_sum.send)
    terms, up_terms, *_ = lax.optimization_barrier(last)
    terms = lax.all_to_all(terms, everyone, 0, 0, tiled=True)
    up_cols = sum_slabs([up_terms], "head", "sum_up")
    (grad_up_own,) = join_columns(exchange(up_cols, "head"), "head", 1, "join_up")
    terms = jnp.sum(terms, axis=(0, 1))
    g2, s2, bd = (terms[n * d_part : (n + 1) * d_part] for n in range(3))
    up_bias_grad = terms[3 * d_part : 3 * d_part + f_part]
    g1, s1 = terms[3 * d_part + f_part : 4 * d_part + f_part], terms[4 * d_part + f_part :]
    qkv_cols = sum_slabs([left_sum.terms, right_sum.terms], "head", "sum_qkv")
    grad_query, grad_key, grad_value = join_columns(exchange(qkv_cols, "head"), "head", 3, "join_qkv")
    return (
        activations,
        input_grad,
        g1,
        s1,
        grad_query,
        grad_key,
        grad_value,
        grad_output_own,
        g2,
        s2,
        grad_up_own,
        up_bias_grad,
        grad_down_own,
        bd,
    )


def solution(mesh):
    rows = P(None, "blk", "head", None)
    vector = P(("head", "blk"))
    matrix = P(("head", "blk"), None)
    params = (vector, vector, matrix, matrix, matrix, matrix, vector, vector, matrix, vector, matrix, vector)
    return jax.shard_map(
        body,
        mesh=mesh,
        in_specs=(rows, rows, P()) + params,
        out_specs=(rows, rows) + params,
        check_vma=False,
    )
```

```python
import functools
import itertools
import math

import jax
import jax.numpy as jnp
from jax import lax
from jax.experimental import pallas as pl
from jax.experimental.pallas import tpu as pltpu
from jax.sharding import PartitionSpec as P

HEADS = 8
HEAD_DIM = 128
BIAS_SPAN = 1024
EPSILON = 1e-05
NEG_LARGE = -1e30
LOG2E = 1.4426950408889634
VMEM_BYTES = 48 << 20
F32 = jnp.float32
BF16 = jnp.bfloat16
SMEM = pl.BlockSpec(memory_space=pltpu.SMEM)
VMEM = pl.BlockSpec(memory_space=pltpu.VMEM)
ANY = pl.BlockSpec(memory_space=pl.ANY)


def fixed(*shape):
    return pl.BlockSpec(shape, lambda n: (0,) * len(shape))


def swap(x, axis, bits):
    if not bits:
        return x
    return lax.ppermute(x, axis, [(n, n ^ bits) for n in range(lax.axis_size(axis))])


def bits_of(axis):
    top = lax.axis_size(axis).bit_length() - 1
    return [1 << n for n in reversed(range(top))]


def gather_pieces(x, axis, middle=()):
    pieces = {0: x}
    for bit in bits_of(axis):
        for n in list(pieces):
            pieces[n | bit] = swap(pieces[n], axis, bit)
        if middle:
            pieces, middle = after(pieces, middle), ()
    return [pieces[n] for n in range(lax.axis_size(axis))]


def gather_relative(x, axis):
    return jnp.concatenate(gather_pieces(x, axis), axis=0)


def gather_rest(first, axis):
    pieces = {0: first[0], lax.axis_size(axis) // 2: first[1]}
    for bit in bits_of(axis)[1:]:
        for n in list(pieces):
            pieces[n | bit] = swap(pieces[n], axis, bit)
    return [pieces[n] for n in range(lax.axis_size(axis))]


def relative(axis):
    return lax.axis_index(axis) ^ jnp.arange(lax.axis_size(axis), dtype=jnp.int32)


class Halving:
    def __init__(self, x, axis, dim, order):
        self.axis, self.dim, self.order = axis, dim, list(order)
        self.bits = bits_of(axis)
        self.x = x.reshape(x.shape[:dim] + (2,) * len(self.bits) + x.shape[dim + 1 :])
        self.whole = True
        self.first = self.order.pop(0)
        self.at = dim + self.bits.index(self.first)
        self.bits.remove(self.first)
        self.send = lax.dynamic_index_in_dim(self.x, 1 - self.mine(self.first), self.at, keepdims=False)
        self.came = swap(self.send, axis, self.first)

    def mine(self, bit):
        return (lax.axis_index(self.axis) // bit) % 2

    def fold(self, name, behind=()):
        bit = self.order.pop(0)
        there = self.dim + self.bits.index(bit)
        self.bits.remove(bit)
        whole, at = self.whole, self.at
        shape = self.came.shape
        left = shape[:there] + shape[there + 1 :]

        def kernel(numbers_ref, x_ref, came_ref, *refs):
            keep_ref, send_ref = refs[-2:]

            def value(where):
                own = where[:at] + (numbers_ref[0],) + where[at:] if whole else where
                return x_ref[own].astype(F32) + came_ref[where].astype(F32)

            for spot in itertools.product(*map(range, left[:-2])):
                keep_ref[spot] = value(spot[:there] + (numbers_ref[1],) + spot[there:])
                send_ref[spot] = value(spot[:there] + (1 - numbers_ref[1],) + spot[there:]).astype(BF16)

        arrays = [self.x, self.came]
        self.x, self.send = pl.pallas_call(
            kernel,
            grid=(1,),
            out_shape=(jax.ShapeDtypeStruct(left, F32), jax.ShapeDtypeStruct(left, BF16)),
            in_specs=[SMEM] + [fixed(*a.shape) for a in arrays] + [ANY] * len(behind),
            out_specs=(fixed(*left),) * 2,
            compiler_params=pltpu.CompilerParams(vmem_limit_bytes=VMEM_BYTES),
            cost_estimate=pl.CostEstimate(flops=0, bytes_accessed=4 << 20, transcendentals=0),
            name=name,
        )(jnp.stack([self.mine(self.first), self.mine(bit)]), *arrays, *behind)
        self.whole, self.first = False, bit
        self.came = swap(self.send, self.axis, bit)
        return self

    def fold_all(self, name, behind=()):
        while self.order:
            self.fold(name, behind)
        return self

    @property
    def terms(self):
        return [self.x, self.came]


def total(terms):
    return sum(t.astype(F32) for t in terms)


def small_call(kernel, numbers, arrays, shapes, name):
    return pl.pallas_call(
        kernel,
        grid=(1,),
        out_shape=tuple(shapes),
        in_specs=[SMEM] + [fixed(*a.shape) for a in arrays],
        out_specs=tuple(fixed(*o.shape) for o in shapes),
        compiler_params=pltpu.CompilerParams(vmem_limit_bytes=VMEM_BYTES),
        cost_estimate=pl.CostEstimate(flops=0, bytes_accessed=1 << 20, transcendentals=0),
        name=name,
    )(numbers, *arrays)


def laid_by_devices(pieces, axes, name):
    count, stacked = len(pieces), pieces[0].shape[0]
    numbers = jnp.concatenate([relative(axis) for axis in axes])

    def kernel(numbers_ref, *refs):
        for n in range(count):
            for r in range(stacked):
                refs[-1][numbers_ref[r], numbers_ref[stacked + n]] = refs[n][r]

    shape = jax.ShapeDtypeStruct((stacked, count) + pieces[0].shape[1:], BF16)
    return small_call(kernel, numbers, pieces, [shape], name)[0]


def exchange(pieces, axis):
    return [swap(p, axis, n) for n, p in enumerate(pieces)]


def cut_columns(weights, axis, name):
    count, rows = lax.axis_size(axis), weights[0].shape[0]
    widths = [w.shape[1] // count for w in weights]

    def kernel(numbers_ref, *refs):
        for n in range(count):
            at = 0
            for ref, wide in zip(refs[: len(weights)], widths, strict=True):
                start = pl.multiple_of(numbers_ref[n] * wide, wide)
                refs[len(weights) + n][:, at : at + wide] = ref[:, pl.ds(start, wide)]
                at += wide

    shapes = [jax.ShapeDtypeStruct((rows, sum(widths)), BF16)] * count
    return small_call(kernel, relative(axis), weights, shapes, name)


def sum_slabs(groups, axis, name):
    count, rows, _ = groups[0][0].shape
    widths = [group[0].shape[2] for group in groups]
    arrays = [part for group in groups for part in group]

    def kernel(numbers_ref, *refs):
        for n in range(count):
            taken = at = 0
            for group, wide in zip(groups, widths, strict=True):
                slab = total([ref[numbers_ref[n]] for ref in refs[taken : taken + len(group)]])
                refs[len(arrays) + n][:, at : at + wide] = slab.astype(BF16)
                taken, at = taken + len(group), at + wide

    shapes = [jax.ShapeDtypeStruct((rows, sum(widths)), BF16)] * count
    return small_call(kernel, relative(axis), arrays, shapes, name)


def join_columns(pieces, axis, kinds, name):
    count = len(pieces)
    rows, wide = pieces[0].shape
    wide //= kinds

    def kernel(numbers_ref, *refs):
        for n in range(count):
            start = pl.multiple_of(numbers_ref[n] * wide, wide)
            for k in range(kinds):
                refs[count + k][:, pl.ds(start, wide)] = refs[n][:, k * wide : (k + 1) * wide].astype(F32)

    shapes = [jax.ShapeDtypeStruct((rows, wide * count), F32)] * kinds
    return small_call(kernel, relative(axis), pieces, shapes, name)


def after(value, *others):
    return lax.optimization_barrier((value, others))[0]


def halves_near(keep, came):
    return [total(pair).astype(BF16) for pair in list(zip(keep, came, strict=True))[1:]]


def halves_far(near, axis):
    return [swap(n, axis, 2 + 2 * a) for a, n in enumerate(near)]


def norm_parts(values):
    center = values - jnp.mean(values, axis=-1, keepdims=True)
    spread = lax.rsqrt(jnp.mean(center * center, axis=-1, keepdims=True) + EPSILON)
    return (center * spread, spread)


def norm_back(grad_normed, normed, spread, gain):
    scaled = grad_normed * gain
    inner = (
        scaled
        - jnp.mean(scaled, axis=-1, keepdims=True)
        - normed * jnp.mean(scaled * normed, axis=-1, keepdims=True)
    )
    return (spread * inner, jnp.sum(grad_normed * normed, axis=0), jnp.sum(grad_normed, axis=0))


def plain_dot(left, right):
    return jnp.dot(left, right, preferred_element_type=F32)


def rows_dot(left, right):
    return lax.dot_general(left, right, (((0,), (0,)), ((), ())), preferred_element_type=F32)


def dot_stacked(left, right, rows):
    return plain_dot(left, right[:, :rows].reshape(-1, right.shape[2]))


def dot_trans(left, right):
    return lax.dot_general(left, right, (((1,), (1,)), ((), ())), preferred_element_type=F32)


def gelu_and_slope(u):
    k = math.sqrt(2.0 / math.pi)
    t = jnp.tanh(k * (u + 0.044715 * (u * u * u)))
    half = 0.5 * (1.0 + t)
    slope = half + 0.5 * u * (1.0 - t * t) * (k * (1.0 + 3 * 0.044715 * (u * u)))
    return u * half, slope


class Plan:
    def __init__(self, head_count, blk_count, sequences, tok_rows, heads_here, d_part):
        self.d_part = d_part
        self.blocks, self.sequences, self.tok, self.heads = head_count, sequences, tok_rows, heads_here
        self.own = sequences * tok_rows
        self.units = sequences * heads_here
        self.parts = blk_count // self.units
        self.rel = head_count // self.parts

    def packed(self, kinds):
        return (self.units, self.parts, kinds, self.rel, self.tok, HEAD_DIM)

    def packed_spec(self, kinds):
        return pl.BlockSpec(
            (self.units, 1, kinds, 1, self.tok, HEAD_DIM), lambda n: (0, n // self.rel, 0, n % self.rel, 0, 0)
        )

    def rows_spec(self, width):
        return pl.BlockSpec((self.own, width), lambda n: (n, 0))

    def pick(self, refs):
        value = refs[0][...]
        for n in range(1, self.blocks):
            value = jnp.where(pl.program_id(0) == n, refs[n][...], value)
        return value

    def half_spec(self, width):
        return pl.BlockSpec((1, self.own, width), lambda n: (n // 2, 0, 0))

    def half(self, width):
        return jax.ShapeDtypeStruct((self.blocks // 2, self.own, width), BF16)

    def pack(self, out_ref, rows, kinds):
        for c in range(kinds):
            for e in range(self.heads):
                col = (c * self.heads + e) * HEAD_DIM
                for s in range(self.sequences):
                    cut = rows[s * self.tok : (s + 1) * self.tok, col : col + HEAD_DIM]
                    out_ref[s * self.heads + e, 0, c, 0] = cut

    def unpack(self, in_ref, rows_ref, kinds):
        for c in range(kinds):
            for e in range(self.heads):
                col = (c * self.heads + e) * HEAD_DIM
                for s in range(self.sequences):
                    cut = in_ref[s * self.heads + e, 0, c, 0]
                    rows_ref[s * self.tok : (s + 1) * self.tok, col : col + HEAD_DIM] = cut


def split_store(keep_ref, send_ref, value):
    odd = pl.program_id(0) % 2 == 1
    value = value.astype(BF16)

    @pl.when(jnp.logical_not(odd))
    def _():
        keep_ref[0] = value

    @pl.when(odd)
    def _():
        send_ref[0] = value


def stacked_part(joint, start, rows):
    count, _, width = joint.shape
    if start % rows or rows % 16:
        joint, start = joint[:, start : start + rows], 0
    at = start // rows
    return joint, pl.BlockSpec((count, rows, width), lambda n: (0, at, 0))


def big_call(kernel, plan, name, flops, out_shape, in_specs, out_specs, scratch=()):
    return pl.pallas_call(
        kernel,
        grid=(plan.blocks,),
        out_shape=out_shape,
        in_specs=in_specs,
        out_specs=out_specs,
        scratch_shapes=scratch,
        compiler_params=pltpu.CompilerParams(vmem_limit_bytes=VMEM_BYTES),
        cost_estimate=pl.CostEstimate(flops=flops, bytes_accessed=8 << 20, transcendentals=0),
        name=name,
    )


def project(plan, x, gain, shift_row, weight):
    width, kinds_width = weight.shape
    rows = plan.blocks * plan.own

    def kernel(*refs):
        x_refs, (gain_ref, shift_ref, w_ref, h_ref, out_ref) = refs[: plan.blocks], refs[plan.blocks :]
        normed, _ = norm_parts(plan.pick(x_refs).astype(F32))
        h = (normed * gain_ref[...] + shift_ref[...]).astype(BF16)
        h_ref[...] = h
        plan.pack(out_ref, plain_dot(h, w_ref[...]).astype(BF16), 3)

    return big_call(
        kernel,
        plan,
        "project",
        2 * rows * width * kinds_width,
        (jax.ShapeDtypeStruct((rows, width), BF16), jax.ShapeDtypeStruct(plan.packed(3), BF16)),
        [fixed(plan.own, width)] * plan.blocks + [fixed(1, width), fixed(1, width), fixed(width, kinds_width)],
        (plan.rows_spec(width), plan.packed_spec(3)),
    )(*x, gain, shift_row, weight)


def project_out(plan, received, weight):
    weight, w_spec = weight
    here, width = plan.heads * HEAD_DIM, weight.shape[2]

    def kernel(in_ref, w_ref, rows_ref, keep_ref, send_ref):
        plan.unpack(in_ref, rows_ref, 1)
        split_store(keep_ref, send_ref, plain_dot(rows_ref[...], w_ref[...].reshape(here, width)))

    rows = plan.blocks * plan.own
    return big_call(
        kernel,
        plan,
        "project_out",
        2 * rows * width * here,
        (jax.ShapeDtypeStruct((rows, here), BF16), plan.half(width), plan.half(width)),
        [plan.packed_spec(1), w_spec],
        (plan.rows_spec(here), plan.half_spec(width), plan.half_spec(width)),
    )(received, weight)


def project_out_back(plan, grad, weight, behind):
    weight, w_spec = weight
    here, width = plan.heads * HEAD_DIM, weight.shape[2]
    rows = plan.blocks * plan.own

    def kernel(*refs):
        in_refs, w_ref, (rows_ref, out_ref) = refs[: plan.blocks], refs[plan.blocks], refs[-2:]
        value = plan.pick(in_refs)
        rows_ref[...] = value
        plan.pack(out_ref, dot_trans(value, w_ref[...].reshape(here, width)).astype(BF16), 1)

    return big_call(
        kernel,
        plan,
        "project_out_back",
        2 * rows * width * here,
        (jax.ShapeDtypeStruct((rows, width), BF16), jax.ShapeDtypeStruct(plan.packed(1), BF16)),
        [fixed(plan.own, width)] * plan.blocks + [w_spec] + [ANY] * len(behind),
        (plan.rows_spec(width), plan.packed_spec(1)),
    )(*grad, weight, *behind)


def project_back(plan, received, weight, behind):
    width, here = weight.shape

    half = here // 2

    def kernel(in_ref, w_ref, *refs):
        left_ref, right_ref, keep_ref, send_ref, rows_ref = refs[-5:]
        plan.unpack(in_ref, rows_ref, 3)
        left_ref[...], right_ref[...] = rows_ref[:, :half], rows_ref[:, half:]
        split_store(keep_ref, send_ref, dot_trans(rows_ref[...], w_ref[...]))

    rows = plan.blocks * plan.own
    return big_call(
        kernel,
        plan,
        "project_back",
        2 * rows * width * here,
        (jax.ShapeDtypeStruct((rows, half), BF16),) * 2 + (plan.half(width),) * 2,
        [plan.packed_spec(3), fixed(width, here)] + [ANY] * len(behind),
        (plan.rows_spec(half),) * 2 + (plan.half_spec(width),) * 2,
        [pltpu.VMEM((plan.own, here), BF16)],
    )(received, weight, *behind)


def feed_forward(plan, hidden, grad_act, up_weight, up_bias, head_slots, before=None):
    half = plan.blocks // 2
    first = before is None
    width, here = plan.blocks * plan.parts * plan.units * plan.d_part, up_bias.shape[1]
    rows = plan.blocks * plan.own
    base = 0 if first else 1
    count = 0 if not first else up_weight[0].shape[0]
    cut = plan.d_part

    def kernel(*refs):
        if first:
            slots_ref, refs = refs[0], refs[1:]
        h_refs, (grad_ref, up_ref, bias_ref, bias_before_ref) = refs[:half], refs[half : half + 4]
        outs = refs[-7:] if first else refs[-6:]
        h_ref, act_ref, out_ref, bias_grad_ref, keep_ref, send_ref = outs[:6]
        value = jnp.concatenate([ref[...] for ref in h_refs], axis=0)
        if first:
            in_order = outs[6]
            for b in range(count):
                for h in range(plan.blocks):
                    in_order[slots_ref[h], b] = up_ref[b, h * cut : (h + 1) * cut, :]
            up_rows = in_order[...].reshape(width, here)
        else:
            up_rows = up_ref[...].reshape(width, here)
        h_ref[...] = value
        act, slope = gelu_and_slope(plain_dot(value, up_rows) + bias_ref[...])
        act_ref[...] = act.astype(BF16)
        grad_up = (grad_ref[...].astype(F32) * slope).astype(BF16)
        out_ref[...] = grad_up
        bias_grad_ref[...] = bias_before_ref[...] + jnp.sum(grad_up.astype(F32), axis=0, keepdims=True)
        back = dot_trans(grad_up, up_rows).astype(BF16).reshape(half, plan.own, width)
        for n in range(half):
            (send_ref if n % 2 else keep_ref)[n // 2] = back[n]

    def rows_spec(wide):
        return pl.BlockSpec((half * plan.own, wide), lambda n: (base, 0))

    part = jax.ShapeDtypeStruct((half // 2, plan.own, width), BF16)
    shapes = [jax.ShapeDtypeStruct((rows, wide), BF16) for wide in (width, here, here)]
    shapes += [jax.ShapeDtypeStruct((1, here), F32), part, part]
    specs = [rows_spec(width), rows_spec(here), rows_spec(here), fixed(1, here)] + [fixed(*part.shape)] * 2
    if first:
        turned = (plan.blocks, count, cut, here)
        shapes.append(jax.ShapeDtypeStruct(turned, BF16))
        specs.append(fixed(*turned))
        arrays = [head_slots, *hidden, grad_act, up_weight[0], up_bias, jnp.zeros((1, here), F32)]
        in_specs = [SMEM] + [fixed(plan.own, width)] * half + [rows_spec(here), up_weight[1]] + [fixed(1, here)] * 2
        aliases = {}
    else:
        arrays = [*hidden, grad_act, before[6], up_bias, before[3], *before[:3]]
        in_specs = [fixed(plan.own, width)] * half + [rows_spec(here), fixed(*before[6].shape)]
        in_specs += [fixed(1, here)] * 2 + [ANY] * 3
        aliases = {half + 4 + n: n for n in range(3)}
    return pl.pallas_call(
        kernel,
        grid=(1,),
        out_shape=tuple(shapes),
        in_specs=in_specs,
        out_specs=tuple(specs),
        input_output_aliases=aliases,
        compiler_params=pltpu.CompilerParams(vmem_limit_bytes=VMEM_BYTES),
        cost_estimate=pl.CostEstimate(flops=2 * rows * width * here, bytes_accessed=6 << 20, transcendentals=0),
        name="feed_forward",
    )(*arrays)


def norm_call(kernel, arrays, behind, shapes, name):
    def body(*refs):
        kernel(refs[: len(arrays)], refs[len(arrays) + len(behind) :])

    return pl.pallas_call(
        body,
        grid=(1,),
        out_shape=tuple(shapes),
        in_specs=[fixed(*a.shape) for a in arrays] + [ANY] * len(behind),
        out_specs=tuple(fixed(*o.shape) for o in shapes),
        compiler_params=pltpu.CompilerParams(vmem_limit_bytes=VMEM_BYTES),
        cost_estimate=pl.CostEstimate(flops=10 << 20, bytes_accessed=4 << 20, transcendentals=0),
        name=name,
    )(*arrays, *behind)


def summed(refs):
    keep_ref, came_ref = refs[:2]
    total = keep_ref[0].astype(F32) + came_ref[0].astype(F32)
    for ref in refs[2:]:
        total = total + ref[...].astype(F32)
    return total


def second_norm(x, terms, gain, shift_row, behind):
    def kernel(ins, outs):
        middle = ins[0][...].astype(F32) + summed(ins[3:])
        normed, _ = norm_parts(middle)
        outs[0][...] = middle
        outs[1][...] = (normed * ins[1][...] + ins[2][...]).astype(BF16)

    shapes = [jax.ShapeDtypeStruct(x.shape, F32), jax.ShapeDtypeStruct(x.shape, BF16)]
    return norm_call(kernel, [x, gain, shift_row, *terms], behind, shapes, "second_norm")


def second_norm_back(middle, grad, terms, gain, behind):
    def kernel(ins, outs):
        normed, spread = norm_parts(ins[0][...])
        grad_out = ins[1][...].astype(F32)
        back, gain_sum, shift_sum = norm_back(summed(ins[3:]), normed, spread, ins[2][...])
        total = grad_out + back
        outs[0][...] = total
        outs[1][...] = total.astype(BF16)
        outs[2][...] = gain_sum[None]
        outs[3][...] = shift_sum[None]
        outs[4][...] = jnp.sum(grad_out, axis=0, keepdims=True)

    row = jax.ShapeDtypeStruct((1, grad.shape[1]), F32)
    shapes = [jax.ShapeDtypeStruct(grad.shape, F32), jax.ShapeDtypeStruct(grad.shape, BF16), row, row, row]
    return norm_call(kernel, [middle, grad, gain, *terms], behind, shapes, "second_norm_back")


def first_norm_back(x, grad, terms, gain, behind):
    def kernel(ins, outs):
        normed, spread = norm_parts(ins[0][...].astype(F32))
        back, gain_sum, shift_sum = norm_back(summed(ins[3:]), normed, spread, ins[2][...])
        outs[0][...] = (ins[1][...] + back).astype(BF16)
        outs[1][...] = gain_sum[None]
        outs[2][...] = shift_sum[None]

    row = jax.ShapeDtypeStruct((1, x.shape[1]), F32)
    return norm_call(kernel, [x, grad, gain, *terms], behind, [jax.ShapeDtypeStruct(x.shape, BF16), row, row], "first_norm_back")


def with_bias(rows, slope2, scale):
    place = lax.broadcasted_iota(jnp.int32, (rows, HEAD_DIM), 0).astype(F32) * (slope2 / scale)
    high = place.astype(BF16).astype(F32)
    middle = (place - high).astype(BF16).astype(F32)
    low = place - high - middle
    lane = lax.broadcasted_iota(jnp.int32, (rows, HEAD_DIM), 1)
    parts = jnp.where(lane == 0, high, jnp.where(lane == 1, middle, jnp.where(lane == 2, low, 0.0)))
    return parts.astype(BF16)


def raw_scores(ka_ref, queries, span):
    tile = queries.shape[0]
    lane = lax.broadcasted_iota(jnp.int32, queries.shape, 1)
    ones = jnp.where(lane < 3, 1.0, 0.0).astype(BF16)
    scores = dot_trans(ka_ref[0:span, :], jnp.concatenate([queries, ones], axis=1))
    spot = (tile, tile)
    allowed = lax.broadcasted_iota(jnp.int32, spot, 0) <= lax.broadcasted_iota(jnp.int32, spot, 1)
    last = jnp.where(allowed, scores[span - tile :], NEG_LARGE)
    return jnp.concatenate([scores[: span - tile], last], axis=0) if span > tile else last


def attend_forward_kernel(tile, piece, src_ref, slope_ref, recv_ref, out_ref, q_ref, k_ref, v_ref, o_ref, l_ref, vt_ref, ka_ref):
    pieces = q_ref.shape[0] // piece
    rel = recv_ref.shape[0] // piece // 3 // src_ref.shape[1]
    for t in range(pieces):
        for c, ref in enumerate((q_ref, k_ref, v_ref)):
            at = pl.multiple_of((src_ref[0, t] + c * src_ref[1, 0]) * piece, piece)
            ref[t * piece : (t + 1) * piece, :] = recv_ref[pl.ds(at, piece), :]
    tiles = q_ref.shape[0] // tile
    for j in range(tiles):
        rows = slice(j * tile, (j + 1) * tile)
        vt_ref[:, rows] = v_ref[rows, :].T
    scale = LOG2E / math.sqrt(HEAD_DIM)
    ka_ref[:, :HEAD_DIM] = k_ref[...]
    ka_ref[:, HEAD_DIM:] = with_bias(k_ref.shape[0], slope_ref[0], scale)
    for i in range(tiles):
        span = (i + 1) * tile
        scores = raw_scores(ka_ref, q_ref[i * tile : span, :], span)
        top = jnp.max(scores, axis=0, keepdims=True) * scale
        shifted = jnp.exp2(scores * scale - top)
        total = jnp.sum(shifted, axis=0, keepdims=True)
        l_ref[i : i + 1, :] = top + jnp.log2(total)
        weighted = plain_dot(vt_ref[:, 0:span], shifted.astype(BF16)) * (1.0 / total)
        o_ref[i * tile : span, :] = weighted.T.astype(BF16)
    for t in range(pieces):
        at = pl.multiple_of(src_ref[2, t] * piece, piece)
        out_ref[pl.ds(at, piece), :] = o_ref[t * piece : (t + 1) * piece, :]


def attend_backward_kernel(tile, piece, src_ref, slope_ref, recv_ref, q_ref, k_ref, v_ref, o_ref, l_ref, *refs):
    out_ref, d_ref, kt_ref, dq_ref, dk_ref, dv_ref, ka_ref = refs[-7:]
    pieces = q_ref.shape[0] // piece
    for t in range(pieces):
        at = pl.multiple_of(src_ref[2, t] * piece, piece)
        d_ref[t * piece : (t + 1) * piece, :] = recv_ref[pl.ds(at, piece), :]
    tiles = q_ref.shape[0] // tile
    for j in range(tiles):
        rows = slice(j * tile, (j + 1) * tile)
        kt_ref[:, rows] = k_ref[rows, :].T
    scale = LOG2E / math.sqrt(HEAD_DIM)
    ka_ref[:, :HEAD_DIM] = k_ref[...]
    ka_ref[:, HEAD_DIM:] = with_bias(k_ref.shape[0], slope_ref[0], scale)
    for i in reversed(range(tiles)):
        span = (i + 1) * tile
        mine = slice(i * tile, span)
        queries, grads = q_ref[mine, :], d_ref[mine, :]
        row_dot = lax.dot_general(
            jnp.ones((8, HEAD_DIM), F32),
            grads.astype(F32) * o_ref[mine, :].astype(F32),
            (((1,), (1,)), ((), ())),
            precision=lax.Precision.HIGHEST,
            preferred_element_type=F32,
        )[0:1]
        prob = jnp.exp2(raw_scores(ka_ref, queries, span) * scale - l_ref[i : i + 1, :])
        grad_prob = dot_trans(v_ref[0:span, :], grads)
        grad_scores = (prob * (grad_prob - row_dot)).astype(BF16)
        dv = plain_dot(prob.astype(BF16), grads)
        dk = plain_dot(grad_scores, queries)
        if i == tiles - 1:
            dv_ref[...] = dv
            dk_ref[...] = dk
        else:
            dv_ref[0:span, :] += dv
            dk_ref[0:span, :] += dk
        dq_ref[mine, :] = plain_dot(kt_ref[:, 0:span], grad_scores).T
    for t in range(pieces):
        rows = slice(t * piece, (t + 1) * piece)
        for c, (ref, factor) in enumerate(
            ((dq_ref, 1.0 / math.sqrt(HEAD_DIM)), (dk_ref, 1.0 / math.sqrt(HEAD_DIM)), (dv_ref, 1.0))
        ):
            at = pl.multiple_of((src_ref[0, t] + c * src_ref[1, 0]) * piece, piece)
            out_ref[pl.ds(at, piece), :] = (ref[rows, :] * factor).astype(BF16)


def unit_forward(recv, sources, slope2, tile, piece):
    rows = recv.shape[0] // 3
    half = jax.ShapeDtypeStruct((rows, HEAD_DIM), BF16)
    area = rows * rows // 2 * HEAD_DIM
    return pl.pallas_call(
        functools.partial(attend_forward_kernel, tile, piece),
        grid=(1,),
        out_shape=(half,) * 5 + (jax.ShapeDtypeStruct((rows // tile, tile), F32),),
        in_specs=[SMEM, SMEM, fixed(*recv.shape)],
        out_specs=(fixed(rows, HEAD_DIM),) * 5 + (fixed(rows // tile, tile),),
        scratch_shapes=[pltpu.VMEM((HEAD_DIM, rows), BF16), pltpu.VMEM((rows, 2 * HEAD_DIM), BF16)],
        compiler_params=pltpu.CompilerParams(vmem_limit_bytes=VMEM_BYTES),
        cost_estimate=pl.CostEstimate(flops=4 * area, bytes_accessed=rows * 2048, transcendentals=rows * rows // 2),
        name="attend_forward",
    )(sources, slope2, recv)


def unit_backward(recv, kept, sources, slope2, tile, piece, behind):
    rows = recv.shape[0]
    area = rows * rows // 2 * HEAD_DIM
    return pl.pallas_call(
        functools.partial(attend_backward_kernel, tile, piece),
        grid=(1,),
        out_shape=jax.ShapeDtypeStruct((rows * 3, HEAD_DIM), BF16),
        in_specs=[SMEM, SMEM] + [fixed(*a.shape) for a in (recv, *kept)] + [ANY] * len(behind),
        out_specs=fixed(rows * 3, HEAD_DIM),
        scratch_shapes=[
            pltpu.VMEM((rows, HEAD_DIM), BF16),
            pltpu.VMEM((HEAD_DIM, rows), BF16),
            pltpu.VMEM((rows, HEAD_DIM), F32),
            pltpu.VMEM((rows, HEAD_DIM), F32),
            pltpu.VMEM((rows, HEAD_DIM), F32),
            pltpu.VMEM((rows, 2 * HEAD_DIM), BF16),
        ],
        compiler_params=pltpu.CompilerParams(vmem_limit_bytes=VMEM_BYTES),
        cost_estimate=pl.CostEstimate(flops=10 * area, bytes_accessed=rows * 2560, transcendentals=rows * rows // 2),
        name="attend_backward",
    )(sources, slope2, recv, *kept, *behind)


def general_scores(queries, keys, query_pos, key_pos, slope):
    scores = dot_trans(queries, keys) / math.sqrt(HEAD_DIM)
    distance = (query_pos[:, None] - key_pos[None, :]).astype(F32)
    allowed = key_pos[None, :] <= query_pos[:, None]
    return jnp.where(allowed, scores - slope * distance, NEG_LARGE), allowed


def general_forward(queries, keys, values, query_pos, key_pos, slope):
    count = queries.shape[0]
    span = math.gcd(keys.shape[0], 1024)

    def visit(n, state):
        top, total, weighted = state
        key_rows = lax.dynamic_slice_in_dim(keys, n * span, span, 0)
        value_rows = lax.dynamic_slice_in_dim(values, n * span, span, 0)
        place = lax.dynamic_slice_in_dim(key_pos, n * span, span, 0)
        scores, allowed = general_scores(queries, key_rows, query_pos, place, slope)
        new_top = jnp.maximum(top, jnp.max(scores, axis=-1, keepdims=True))
        fade = jnp.exp(top - new_top)
        shifted = jnp.where(allowed, jnp.exp(scores - new_top), 0.0)
        total = total * fade + jnp.sum(shifted, axis=-1, keepdims=True)
        return new_top, total, weighted * fade + plain_dot(shifted.astype(BF16), value_rows)

    start = (jnp.full((count, 1), NEG_LARGE, F32), jnp.zeros((count, 1), F32), jnp.zeros((count, HEAD_DIM), F32))
    top, total, weighted = lax.fori_loop(0, keys.shape[0] // span, visit, start)
    return (weighted / total).astype(BF16), top + jnp.log(total)


def general_backward(queries, keys, values, attended, log_norm, grads, query_pos, key_pos, slope):
    span = math.gcd(keys.shape[0], 1024)
    row_dot = jnp.sum(grads.astype(F32) * attended.astype(F32), axis=-1, keepdims=True)

    def visit(n, state):
        key_rows = lax.dynamic_slice_in_dim(keys, n * span, span, 0)
        value_rows = lax.dynamic_slice_in_dim(values, n * span, span, 0)
        place = lax.dynamic_slice_in_dim(key_pos, n * span, span, 0)
        scores, allowed = general_scores(queries, key_rows, query_pos, place, slope)
        prob = jnp.where(allowed, jnp.exp(scores - log_norm), 0.0)
        grad_scores = (prob * (dot_trans(grads, value_rows) - row_dot)).astype(BF16)
        dq = state[0] + plain_dot(grad_scores, key_rows)
        dk = lax.dynamic_update_slice_in_dim(state[1], rows_dot(grad_scores, queries), n * span, 0)
        dv = lax.dynamic_update_slice_in_dim(state[2], rows_dot(prob.astype(BF16), grads), n * span, 0)
        return dq, dk, dv

    start = (jnp.zeros(queries.shape, F32), jnp.zeros(keys.shape, F32), jnp.zeros(keys.shape, F32))
    dq, dk, dv = lax.fori_loop(0, keys.shape[0] // span, visit, start)
    scale = 1.0 / math.sqrt(HEAD_DIM)
    return (dq * scale).astype(BF16), (dk * scale).astype(BF16), dv.astype(BF16)


def body(
    tokens,
    cotangent,
    block_table,
    norm1_gain,
    norm1_bias,
    w_query,
    w_key,
    w_value,
    w_output,
    norm2_gain,
    norm2_bias,
    w_up,
    b_up,
    w_down,
    b_down,
):
    head_count, blk_count = lax.axis_size("head"), lax.axis_size("blk")
    devices = head_count * blk_count
    sequences, _, tok_rows, width = tokens.shape
    heads_here = HEADS // head_count
    cycle_rows = tok_rows * head_count
    half_rows = cycle_rows // 2
    seq_len = cycle_rows * blk_count
    own_rows = sequences * tok_rows
    d_part, f_part = width // devices, b_up.shape[0]
    hidden = f_part * devices
    f_here = hidden // head_count
    units = sequences * heads_here
    parts = blk_count // units
    rel_part = head_count // parts
    head_at, blk_at = lax.axis_index("head"), lax.axis_index("blk")
    head_slots = relative("head")
    everyone = ("head", "blk")

    x_own = tokens[:, 0].reshape(own_rows, width)
    g_own = cotangent[:, 0].reshape(own_rows, width)

    def turned_columns(weights, name):
        return jnp.stack(exchange(cut_columns(weights, "head", name), "head"))

    qkv_cols = turned_columns([w_query, w_key, w_value], "cut_qkv")
    qkv_pieces = gather_pieces(qkv_cols, "blk")
    direct = [qkv_pieces[bit] for bit in bits_of("blk")]
    small = jnp.concatenate(
        [v.reshape(-1, d_part) for v in (norm1_gain, norm1_bias, norm2_gain, norm2_bias, b_down, b_up)], axis=0
    )
    small = after(small, direct)
    small = lax.all_to_all(
        jnp.broadcast_to(small, (devices,) + small.shape), everyone, 0, 0, tiled=True
    ).astype(F32)
    second = [piece for n, piece in enumerate(qkv_pieces) if n.bit_count() == 2]
    x_pieces = gather_pieces(after(x_own, direct), "head", [second, small])
    first_gain, first_shift, second_gain, second_shift, down_bias = (
        small[:, n].reshape(1, width) for n in range(5)
    )
    up_bias = lax.dynamic_index_in_dim(small[:, 5:].reshape(head_count, f_here), head_at, 0)
    qkv_pieces = after(qkv_pieces, x_pieces, first_gain, first_shift)
    qkv_weight = laid_by_devices(qkv_pieces, ("head", "blk"), "lay_qkv").reshape(width, -1)
    joint = after(jnp.concatenate([w_down, w_output], axis=0), qkv_pieces)
    joint = lax.all_gather(joint, "blk", axis=0, tiled=False)
    down_weight, output_weight = stacked_part(joint, 0, f_part), stacked_part(joint, f_part, d_part)

    flat_table = block_table.reshape(-1)
    head_ids = head_at * heads_here + jnp.arange(heads_here, dtype=jnp.int32)
    unit, part = blk_at // parts, blk_at % parts
    my_head = head_ids[0] + unit % heads_here
    slope = jnp.exp2(-8.0 * (my_head + 1).astype(F32) / HEADS) * (BIAS_SPAN / seq_len)

    plan = Plan(head_count, blk_count, sequences, tok_rows, heads_here, d_part)

    def units_turn(packed, kinds):
        packed = packed.reshape(blk_count, kinds, rel_part, tok_rows, HEAD_DIM)
        return lax.all_to_all(packed, "blk", 0, 0, tiled=True)

    hidden_one, qkv = project(plan, x_pieces, first_gain, first_shift, qkv_weight)
    g_all = gather_relative(after(g_own, hidden_one), "head")
    up_cols = turned_columns([after(w_up, hidden_one)], "cut_up").reshape(head_count * d_part, f_here)
    received, g_all, up_cols = lax.optimization_barrier((units_turn(qkv, 3), g_all, up_cols))
    up_weight = lax.all_gather(up_cols, "blk", axis=0, tiled=False)
    up_weight = stacked_part(up_weight, 0, head_count * d_part)
    if parts == 1:
        tile = 2 * half_rows
        count = seq_len // tok_rows
        pieces = jnp.arange(count, dtype=jnp.int32)
        per_half = half_rows // tok_rows
        blocks = pieces // per_half
        slots = jnp.arange(flat_table.shape[0], dtype=jnp.int32)
        slot = jnp.sum(jnp.where(flat_table[None, :] == blocks[:, None], slots[None, :], 0), axis=1)
        head_src = (slot % 2) * per_half + pieces % per_half
        rel = head_at ^ head_src
        sources = jnp.stack(
            [
                (slot // 2) * (3 * head_count) + rel,
                jnp.full((count,), head_count, jnp.int32),
                (slot // 2) * head_count + rel,
            ]
        )
        slope2 = (slope * LOG2E).reshape(1)
        attended_unit, *kept = unit_forward(received.reshape(-1, HEAD_DIM), sources, slope2, tile, tok_rows)
    else:
        rel_rows = head_slots.reshape(parts, 1, rel_part, 1) * tok_rows + jnp.arange(tok_rows, dtype=jnp.int32)
        rows_at = rel_rows + jnp.arange(blk_count, dtype=jnp.int32)[None, :, None, None] * cycle_rows
        block_ids = rows_at // half_rows
        slots = jnp.arange(flat_table.shape[0], dtype=jnp.int32)
        picked = jnp.sum(jnp.where(block_ids[..., None] == slots, flat_table, 0), axis=-1)
        places = (picked * half_rows + rows_at % half_rows).reshape(parts, -1)

        def whole_unit(own):
            whole = jnp.zeros((parts,) + own.shape, own.dtype)
            for n in range(parts):
                whole = lax.dynamic_update_index_in_dim(whole, swap(own, "blk", n), part ^ n, 0)
            return whole.reshape(-1, HEAD_DIM)

        queries, own_keys, own_values = (received[:, n].reshape(-1, HEAD_DIM) for n in range(3))
        keys, values = whole_unit(own_keys), whole_unit(own_values)
        query_pos = lax.dynamic_index_in_dim(places, part, 0, keepdims=False)
        key_pos = places.reshape(-1)
        attended_unit, log_norm = general_forward(queries, keys, values, query_pos, key_pos, slope)
    grad_act = dot_trans(g_all, down_weight[0][:, :f_part].reshape(f_here, width)).astype(BF16)
    attended, grad_act = lax.optimization_barrier((units_turn(attended_unit, 1).reshape(plan.packed(1)), grad_act))

    attended, keep, send = project_out(plan, attended, output_weight)
    came = swap(send, "head", 1)
    far = halves_far(halves_near(keep, came), "head")
    middle, hidden_two = second_norm(x_own, [keep, came, *far], second_gain, second_shift, [])
    near_two = {0: hidden_two}
    for bit in bits_of("head")[1:]:
        for n in list(near_two):
            near_two[n | bit] = swap(near_two[n], "head", bit)
    half = head_count // 2
    near_two = [near_two[n] for n in range(half)]

    done = feed_forward(plan, near_two, grad_act, up_weight, up_bias, head_slots)
    keep, came = done[4], swap(done[5], "head", 1)
    hidden_far = after(swap(hidden_two, "head", half), done[4])
    hidden_two = gather_rest([hidden_two, hidden_far], "head")
    done = feed_forward(plan, hidden_two[half:], grad_act, None, up_bias, None, done)
    hidden_two, activated, grad_up_values, grad_up_bias, keep_far, send = done
    grad_up = rows_dot(hidden_two, grad_up_values).astype(BF16).reshape(head_count, blk_count, d_part, f_here)
    came_far, grad_up = lax.optimization_barrier((swap(send, "head", 1), grad_up))
    near = halves_near([*keep, *keep_far], [*came, *came_far])
    near, activated = lax.optimization_barrier((near, activated))
    grad_down = rows_dot(activated, g_all).astype(BF16).reshape(blk_count, f_part, width)
    order = bits_of("blk")[::-1]
    grad_down_sum = Halving(grad_down, "blk", 0, order)
    cross = [order[1], order[0], *order[2:]]
    grad_up_sum = Halving(grad_up, "blk", 1, cross)

    grad_middle, grad_branch, grad_second_gain, grad_second_shift, grad_down_bias = second_norm_back(
        middle, g_own, [keep, came, *halves_far(near, "head")], second_gain, [grad_down_sum.send, grad_up_sum.send]
    )
    mine = (jnp.arange(head_count) == head_at)[:, None]
    early = [grad_second_gain, grad_second_shift, grad_down_bias, jnp.where(mine, grad_up_bias, 0.0)]
    early = jnp.concatenate([v.reshape(devices, 1, -1) for v in early], axis=2)
    result = dot_stacked(after(activated, grad_branch), down_weight[0], f_part).astype(BF16)
    result = result.reshape(head_count // 2, 2, own_rows, width)
    result_keep, result_send = result[:, 0], result[:, 1]
    grad_branch = gather_pieces(grad_branch, "head")
    grad_down_sum.fold("fold_down")
    grad_up_sum.fold("fold_up")
    grad_branch, grad_attended = project_out_back(plan, grad_branch, output_weight, [grad_down_sum.send, grad_up_sum.send, early, result_send])
    grad_output = rows_dot(attended, grad_branch).astype(BF16).reshape(blk_count, d_part, width)
    grad_output_sum = Halving(grad_output, "blk", 0, order)
    grad_output_sum.fold("fold_output", [grad_attended])
    grad_down_sum.fold("fold_down", [grad_attended])
    grad_up_sum.fold("fold_up", [grad_attended])
    result_came = swap(result_send, "head", 1)
    result_near = halves_near(result_keep, result_came)
    grad_unit = units_turn(grad_attended, 1)
    if parts == 1:
        behind = [grad_down_sum.send, grad_up_sum.send, grad_output_sum.send, *result_near]
        grad_unit = grad_unit.reshape(-1, HEAD_DIM)
        grad_qkv_unit = unit_backward(grad_unit, kept, sources, slope2, tile, tok_rows, behind)
    else:
        dq, dk, dv = general_backward(
            queries, keys, values, attended_unit, log_norm, grad_unit.reshape(-1, HEAD_DIM), query_pos, key_pos, slope
        )

        def own_part(grad):
            grad = grad.reshape(parts, -1, HEAD_DIM)
            terms = []
            for n in range(parts):
                piece = lax.dynamic_index_in_dim(grad, part ^ n, 0, keepdims=False)
                terms.append(swap(piece, "blk", n))
            return total(terms).astype(BF16)

        cut = (blk_count, rel_part, tok_rows, HEAD_DIM)
        grad_qkv_unit = jnp.stack([dq.reshape(cut), own_part(dk).reshape(cut), own_part(dv).reshape(cut)], axis=1)
    behind = [grad_qkv_unit]
    grad_down_sum.fold_all("fold_down", behind)
    grad_output_sum.fold_all("fold_output", behind)
    grad_up_sum.fold_all("fold_up", behind)
    result_far = halves_far(result_near, "head")
    last = (grad_qkv_unit, grad_down_sum.terms, grad_output_sum.terms[0], grad_up_sum.terms, result_far)
    grad_qkv_unit, down_terms, output_kept, up_terms, result_far = lax.optimization_barrier(last)
    grad_qkv = units_turn(grad_qkv_unit, 3).reshape(plan.packed(3))
    grad_down_own = total(down_terms)
    activations = total([middle, result_keep[0], result_came[0], *result_far]) + down_bias
    activations = activations.astype(BF16).reshape(tokens.shape)

    left, right, keep, send = project_back(
        plan, grad_qkv, qkv_weight, [grad_down_own, activations]
    )
    grad_output_own = total([output_kept, grad_output_sum.came])
    left = rows_dot(hidden_one, left).astype(BF16).reshape(head_count, blk_count, d_part, -1)
    came, left = lax.optimization_barrier((swap(send, "head", 1), left))
    near = halves_near(keep, came)
    near, right = lax.optimization_barrier((near, right))
    right = rows_dot(hidden_one, right).astype(BF16).reshape(head_count, blk_count, d_part, -1)
    left_sum = Halving(left, "blk", 1, order)
    right_sum = Halving(right, "blk", 1, cross)
    input_grad, grad_first_gain, grad_first_shift = first_norm_back(
        x_own, grad_middle, [keep, came, *halves_far(near, "head")], first_gain, [left_sum.send, right_sum.send]
    )
    left_sum.fold("fold_left").fold_all("fold_left", [input_grad])
    right_sum.fold("fold_right").fold_all("fold_right", [input_grad])
    input_grad = input_grad.reshape(tokens.shape)
    terms = [early] + [v.reshape(devices, 1, d_part) for v in (grad_first_gain, grad_first_shift)]
    last = (jnp.concatenate(terms, axis=2), up_terms, left_sum.send, right_sum.send)
    terms, up_terms, *_ = lax.optimization_barrier(last)
    terms = lax.all_to_all(terms, everyone, 0, 0, tiled=True)
    up_cols = sum_slabs([up_terms], "head", "sum_up")
    (grad_up_own,) = join_columns(exchange(up_cols, "head"), "head", 1, "join_up")
    terms = jnp.sum(terms, axis=(0, 1))
    g2, s2, bd = (terms[n * d_part : (n + 1) * d_part] for n in range(3))
    up_bias_grad = terms[3 * d_part : 3 * d_part + f_part]
    g1, s1 = terms[3 * d_part + f_part : 4 * d_part + f_part], terms[4 * d_part + f_part :]
    qkv_cols = sum_slabs([left_sum.terms, right_sum.terms], "head", "sum_qkv")
    grad_query, grad_key, grad_value = join_columns(exchange(qkv_cols, "head"), "head", 3, "join_qkv")
    return (
        activations,
        input_grad,
        g1,
        s1,
        grad_query,
        grad_key,
        grad_value,
        grad_output_own,
        g2,
        s2,
        grad_up_own,
        up_bias_grad,
        grad_down_own,
        bd,
    )


def solution(mesh):
    rows = P(None, "blk", "head", None)
    vector = P(("head", "blk"))
    matrix = P(("head", "blk"), None)
    params = (vector, vector, matrix, matrix, matrix, matrix, vector, vector, matrix, vector, matrix, vector)
    return jax.shard_map(
        body,
        mesh=mesh,
        in_specs=(rows, rows, P()) + params,
        out_specs=(rows, rows) + params,
        check_vma=False,
    )
```
